256 devices in a mesh: row: 16 (over y, x_hi, core), res: 16 (over z, x_lo).
Axes of the slice: x: 4 (x_hi: 2, x_lo: 2; x = x_hi * 2 + x_lo), y: 4, z: 8, core: 2. Of those that a mesh axis runs over, the one named last changes fastest.
Arguments:
- sequence_stack: bfloat16 [128, 1024, 768], P('row', 'res'), may hold values from -6 to 6
- asking_projector: bfloat16 [768, 768], replicated, may hold values from -0.5 to 0.5
- lookup_projector: bfloat16 [768, 768], replicated, may hold values from -0.5 to 0.5
- content_projector: bfloat16 [768, 768], replicated, may hold values from -0.21875 to 0.21875
- final_projector: bfloat16 [768, 768], replicated, may hold values from -0.21875 to 0.21875
Outputs:
- attended: bfloat16 [128, 1024, 768], P('row', 'res')
The draws below stay inside these ranges and needn't reach their ends.
All inputs are finite; a program needn't handle non-finite values.
Results may differ from the reference program's by a relative error of at most 0.012.
The reference program's roundings to bfloat16 on the way count: a program that leaves them out, or rounds other values in their place, can miss the bound.
Values may be sent and summed in bfloat16 or wider, within the bound.
No kernel may reach another device: no remote copies, remote signals or barrier semaphores. Data moves between devices by JAX's collectives and lax.ppermute only.
A program may use at most 128 MiB of HBM per device.

```python
import math
import jax
import jax.numpy as jnp
from jax import lax

EMBED_DIMENSION = 768
H = 12
DH = 64
SEQUENCE_TOTAL = 128
POSITION_TOTAL = 1024


def draw_sequence_stack(key, part):
    key = jax.random.fold_in(key, 5)
    first = jax.random.fold_in(key, 0)
    field = jax.random.normal(first, (SEQUENCE_TOTAL, POSITION_TOTAL, EMBED_DIMENSION), jnp.float32)
    return jnp.clip(field, -6.0, 6.0).astype(jnp.bfloat16)


def draw_asking_projector(key, part):
    own_key = jax.random.fold_in(key, 11)
    matrix = jax.random.normal(own_key, (EMBED_DIMENSION, EMBED_DIMENSION), jnp.float32) / math.sqrt(EMBED_DIMENSION)
    return jnp.clip(matrix, -0.5, 0.5).astype(jnp.bfloat16)


def draw_lookup_projector(key, part):
    own_key = jax.random.fold_in(key, 13)
    own_part = jax.random.normal(own_key, (EMBED_DIMENSION, EMBED_DIMENSION), jnp.float32)
    matrix = own_part / math.sqrt(EMBED_DIMENSION)
    return jnp.clip(matrix, -0.5, 0.5).astype(jnp.bfloat16)


def bell_draw(key, shape, width, limit, dtype=jnp.bfloat16):
    return jnp.clip(width * jax.random.normal(key, shape, jnp.float32), -limit, limit).astype(dtype)


def setup_inputs(seed: int = 0) -> dict:
    key_list = jax.random.split(jax.random.key(seed), 6)
    return {
        "sequence_stack": draw_sequence_stack(jax.random.fold_in(key_list[5], 71), 0),
        "asking_projector": draw_asking_projector(jax.random.fold_in(key_list[5], 71), 0),
        "lookup_projector": draw_lookup_projector(jax.random.fold_in(key_list[5], 71), 0),
        "content_projector": bell_draw(key_list[3], (EMBED_DIMENSION, EMBED_DIMENSION), EMBED_DIMENSION ** -0.5, 0.21875),
        "final_projector": bell_draw(key_list[4], (EMBED_DIMENSION, EMBED_DIMENSION), EMBED_DIMENSION ** -0.5, 0.21875),
    }


def standardize_block(values_in):
    widened = values_in.astype(jnp.float32)
    average = lax.optimization_barrier(jnp.mean(widened, axis=-1, keepdims=True))
    centred = widened - average
    variance = lax.optimization_barrier(jnp.mean(centred * centred, axis=-1, keepdims=True))
    return (centred * lax.rsqrt(variance + 1e-05)).astype(jnp.bfloat16)

def project(standardized_activity, weight_matrix):
    return jnp.dot(standardized_activity, weight_matrix, preferred_element_type=jnp.float32).astype(jnp.bfloat16)

def softmax_rows(logits):
    shifted = logits - lax.optimization_barrier(jnp.max(logits, axis=-1, keepdims=True))
    powered = jnp.exp(shifted)
    return powered / lax.optimization_barrier(jnp.sum(powered, axis=-1, keepdims=True))

def reference(sequence_stack, asking_projector, lookup_projector, content_projector, final_projector):
    standardized_activity = standardize_block(sequence_stack).reshape(SEQUENCE_TOTAL * POSITION_TOTAL, EMBED_DIMENSION)
    queries = project(standardized_activity, asking_projector).reshape(SEQUENCE_TOTAL, POSITION_TOTAL, H, DH).transpose(2, 0, 1, 3)
    keys = project(standardized_activity, lookup_projector).reshape(SEQUENCE_TOTAL, POSITION_TOTAL, H, DH).transpose(2, 0, 1, 3)
    values = project(standardized_activity, content_projector).reshape(SEQUENCE_TOTAL, POSITION_TOTAL, H, DH).transpose(2, 0, 1, 3)
    factor = 1.0 / math.sqrt(DH * SEQUENCE_TOTAL)

    def one_head(operands):
        query_head, key_head, value_head = operands
        logits = jnp.einsum('rid,rjd->ij', query_head.astype(jnp.float32), key_head.astype(jnp.float32)) * factor
        probs = softmax_rows(logits).astype(jnp.bfloat16)
        return jnp.einsum('ij,rjd->rid', probs.astype(jnp.float32), value_head.astype(jnp.float32))
    mixed = lax.map(one_head, (queries, keys, values))
    mixed = mixed.transpose(1, 2, 0, 3).reshape(SEQUENCE_TOTAL * POSITION_TOTAL, EMBED_DIMENSION).astype(jnp.bfloat16)
    return project(mixed, final_projector).reshape(SEQUENCE_TOTAL, POSITION_TOTAL, EMBED_DIMENSION)
```

```python
import functools
import math

import jax
import jax.numpy as jnp
from jax import lax
from jax.experimental import pallas as pl
from jax.experimental.pallas import tpu as pltpu
from jax.sharding import Mesh, PartitionSpec as P

H = 12
DH = 64
EMBED = 768
ROWS = 8
RES = 64
Z = 8
CHUNK = EMBED // Z
FULL = DH
HALF = CHUNK - DH
PEERS = 8
SUB = RES // 2
QUERIES = Z * SUB
KEYS = 2 * Z * RES

f32 = jnp.float32
bf16 = jnp.bfloat16
PARAMS = pltpu.CompilerParams(vmem_limit_bytes=48 * 1024 * 1024)
VMEM = pl.BlockSpec(memory_space=pltpu.VMEM)
SMEM = pl.BlockSpec(memory_space=pltpu.SMEM)


def chunk_pieces(z):
    base = z * CHUNK
    if z % 2 == 0:
        return (base, FULL), (base + FULL, HALF)
    return (base + HALF, FULL), (base, HALF)


def dot(a, b, ca, cb):
    return lax.dot_general(a, b, (((ca,), (cb,)), ((), ())), preferred_element_type=f32)


def embed_kernel(x_ref, wq_ref, wk_ref, wv_ref, q_ref, k_ref, v_ref, n_ref):
    x = x_ref[...].astype(f32)
    centred = x - jnp.mean(x, axis=-1, keepdims=True)
    var = jnp.mean(centred * centred, axis=-1, keepdims=True)
    n_ref[...] = (centred * lax.rsqrt(var + 1e-05)).astype(bf16)
    n = n_ref[...].reshape(ROWS * RES, EMBED)
    for w_ref, o_ref in ((wk_ref, k_ref), (wv_ref, v_ref)):
        t = dot(w_ref[...], n, 0, 1).astype(bf16)
        for z in range(Z):
            (a, na), (b, nb) = chunk_pieces(z)
            o_ref[z, 0:FULL, :] = t[a : a + na]
            o_ref[z, FULL:CHUNK, :] = t[b : b + nb]
    for c in range(2):
        n = n_ref[:, c * SUB : (c + 1) * SUB, :].reshape(ROWS * SUB, EMBED)
        t = dot(wq_ref[...], n, 0, 1).astype(bf16)
        for z in range(Z):
            (a, na), (b, nb) = chunk_pieces(z)
            q_ref[2 * z + c, 0:FULL, :] = t[a : a + na]
            q_ref[2 * z + c, FULL:CHUNK, :] = t[b : b + nb]


def embed(x, wq, wk, wv):
    return pl.pallas_call(
        embed_kernel,
        out_shape=(
            jax.ShapeDtypeStruct((2 * Z, CHUNK, ROWS * SUB), bf16),
            jax.ShapeDtypeStruct((Z, CHUNK, ROWS * RES), bf16),
            jax.ShapeDtypeStruct((Z, CHUNK, ROWS * RES), bf16),
        ),
        in_specs=[VMEM] * 4,
        out_specs=(VMEM,) * 3,
        scratch_shapes=[pltpu.VMEM((ROWS, RES, EMBED), bf16)],
        compiler_params=PARAMS,
    )(x, wq, wk, wv)


def widen(refs, r):
    return jnp.concatenate(
        [ref[z][:, r * RES : (r + 1) * RES] for ref in refs for z in range(Z)], axis=1
    )


def score_kernel(me_ref, q_ref, k00, k01, k10, k11, *rest):
    outs, (qf, qh, kf, kh) = rest[:PEERS], rest[PEERS:]
    me, core = me_ref[0], me_ref[1]
    for cr, ks in ((0, (k00, k01)), (1, (k10, k11))):
        c = jnp.bitwise_xor(core, cr)
        blocks = [q_ref[2 * jnp.bitwise_xor(me, s) + c] for s in range(PEERS)]
        for r in range(ROWS):
            n = cr * ROWS + r
            t = jnp.concatenate([b[:, r * SUB : (r + 1) * SUB] for b in blocks], axis=1)
            qf[n * FULL : (n + 1) * FULL, :] = t[:FULL]
            qh[n * HALF : (n + 1) * HALF, :] = t[FULL:]
            t = widen(ks, r)
            kf[n * FULL : (n + 1) * FULL, :] = t[:FULL]
            kh[n * HALF : (n + 1) * HALF, :] = t[FULL:]
    for i, (a, b) in enumerate(((qf, kf), (qh, kh))):
        s = dot(a[...], b[...], 0, 0)
        for p in range(PEERS):
            outs[p][i] = s[p * SUB : (p + 1) * SUB]


def score(me, q, ks):
    rows = 2 * ROWS
    return pl.pallas_call(
        score_kernel,
        out_shape=(jax.ShapeDtypeStruct((2, SUB, KEYS), f32),) * PEERS,
        in_specs=[SMEM] + [VMEM] * 5,
        out_specs=(VMEM,) * PEERS,
        scratch_shapes=[
            pltpu.VMEM((rows * FULL, QUERIES), bf16),
            pltpu.VMEM((rows * HALF, QUERIES), bf16),
            pltpu.VMEM((rows * FULL, KEYS), bf16),
            pltpu.VMEM((rows * HALF, KEYS), bf16),
        ],
        compiler_params=PARAMS,
    )(me, q, *ks)


def total_kernel(*refs):
    ins, (full, half) = refs[:PEERS], refs[PEERS:]
    for i, out in enumerate((full, half)):
        t = ins[0][i]
        for ref in ins[1:]:
            t = t + ref[i]
        out[...] = t


def total(parts):
    return pl.pallas_call(
        total_kernel,
        out_shape=(jax.ShapeDtypeStruct((SUB, KEYS), f32),) * 2,
        in_specs=[VMEM] * PEERS,
        out_specs=(VMEM,) * 2,
        compiler_params=PARAMS,
    )(*parts)


def softmax_kernel(factor, full, half, other, out):
    for i, logits in enumerate((full[...], half[...] + other[...])):
        logits = logits * factor
        powered = jnp.exp(logits - jnp.max(logits, axis=-1, keepdims=True))
        out[i] = (powered / jnp.sum(powered, axis=-1, keepdims=True)).astype(bf16)


def softmax(factor, full, half, other):
    return pl.pallas_call(
        functools.partial(softmax_kernel, factor),
        out_shape=jax.ShapeDtypeStruct((2, SUB, KEYS), bf16),
        in_specs=[VMEM] * 3,
        out_specs=VMEM,
        compiler_params=PARAMS,
    )(full, half, other)


def mix_kernel(me_ref, v00, v01, v10, v11, *rest):
    ps, o_ref, (vf, vh) = rest[:PEERS], rest[PEERS], rest[PEERS + 1 :]
    me, core = me_ref[0], me_ref[1]
    pf = jnp.concatenate([p[0] for p in ps], axis=0)
    ph = jnp.concatenate([p[1] for p in ps], axis=0)
    for cr, vs in ((0, (v00, v01)), (1, (v10, v11))):
        c = jnp.bitwise_xor(core, cr)
        for r in range(ROWS):
            t = widen(vs, r)
            vf[r * FULL : (r + 1) * FULL, :] = t[:FULL]
            vh[r * HALF : (r + 1) * HALF, :] = t[FULL:]
        for v, p, first, n in ((vf, pf, 0, FULL), (vh, ph, FULL, HALF)):
            mixed = dot(v[...], p, 1, 1).astype(bf16)
            for s in range(PEERS):
                o_ref[2 * jnp.bitwise_xor(me, s) + c, first : first + n, :] = jnp.concatenate(
                    [mixed[r * n : (r + 1) * n, s * SUB : (s + 1) * SUB] for r in range(ROWS)], axis=1
                )


def mix(me, vs, ps):
    return pl.pallas_call(
        mix_kernel,
        out_shape=jax.ShapeDtypeStruct((2 * Z, CHUNK, ROWS * SUB), bf16),
        in_specs=[SMEM] + [VMEM] * (4 + PEERS),
        out_specs=VMEM,
        scratch_shapes=[
            pltpu.VMEM((ROWS * FULL, KEYS), bf16),
            pltpu.VMEM((ROWS * HALF, KEYS), bf16),
        ],
        compiler_params=PARAMS,
    )(me, *vs, *ps)


def final_kernel(m_ref, w_ref, o_ref, t_ref):
    for c in range(2):
        for z in range(Z):
            (a, na), (b, nb) = chunk_pieces(z)
            t_ref[a : a + na, :] = m_ref[2 * z + c, 0:FULL, :]
            t_ref[b : b + nb, :] = m_ref[2 * z + c, FULL:CHUNK, :]
        attended = dot(t_ref[...], w_ref[...], 0, 0).astype(bf16)
        o_ref[:, c * SUB : (c + 1) * SUB, :] = attended.reshape(ROWS, SUB, EMBED)


def final(m, w):
    return pl.pallas_call(
        final_kernel,
        out_shape=jax.ShapeDtypeStruct((ROWS, RES, EMBED), bf16),
        in_specs=[VMEM] * 2,
        out_specs=VMEM,
        scratch_shapes=[pltpu.VMEM((EMBED, ROWS * SUB), bf16)],
        compiler_params=PARAMS,
    )(m, w)


def flip(x, axes, n, s):
    return lax.ppermute(x, axes, [(i, i ^ s) for i in range(n)])


def gather4(own):
    far = flip(own, "xl", 2, 1)
    return own, far, flip(own, "c", 2, 1), flip(far, "c", 2, 1)


def local(x, wq, wk, wv, wf):
    me = jnp.stack([lax.axis_index(("y", "xh")), lax.axis_index("c")]).astype(jnp.int32)
    q, k, v = embed(x, wq, wk, wv)
    ks = gather4(lax.all_to_all(k, "z", 0, 0, tiled=True))
    q = lax.all_to_all(q, ("z", "c"), 0, 0, tiled=True)
    parts = score(me, q, ks)
    parts = [parts[0]] + [flip(parts[s], ("y", "xh"), PEERS, s) for s in range(1, PEERS)]
    vs = gather4(lax.all_to_all(v, "z", 0, 0, tiled=True))
    full, half = total(parts)
    rows = ROWS * 2 * PEERS
    probs = softmax(1.0 / math.sqrt(DH * rows), full, half, flip(half, "z", Z, 1))
    ps = [probs] + [flip(probs, ("y", "xh"), PEERS, s) for s in range(1, PEERS)]
    mixed = lax.all_to_all(mix(me, vs, ps), ("z", "c"), 0, 0, tiled=True)
    return final(mixed, wf)


def solution(mesh):
    fine = Mesh(mesh.devices.reshape(4, 2, 2, 8, 2), ("y", "xh", "c", "z", "xl"))
    spec = P(("y", "xh", "c"), ("z", "xl"), None)
    return jax.shard_map(
        local,
        mesh=fine,
        in_specs=(spec, P(), P(), P(), P()),
        out_specs=spec,
        check_vma=False,
    )
```

```python
import functools
import math

import jax
import jax.numpy as jnp
from jax import lax
from jax.experimental import pallas as pl
from jax.experimental.pallas import tpu as pltpu
from jax.sharding import Mesh, PartitionSpec as P

H = 12
DH = 64
EMBED = 768
ROWS = 8
RES = 64
Z = 8
CHUNK = EMBED // Z
FULL = DH
HALF = CHUNK - DH
PEERS = 8
SUB = RES // 2
QUERIES = Z * SUB
KEYS = 2 * Z * RES

f32 = jnp.float32
bf16 = jnp.bfloat16
PARAMS = pltpu.CompilerParams(vmem_limit_bytes=48 * 1024 * 1024)
PROJECTION = pl.CostEstimate(
    flops=2 * ROWS * RES * EMBED * EMBED, bytes_accessed=2 * EMBED * (EMBED + 2 * ROWS * RES), transcendentals=0
)
VMEM = pl.BlockSpec(memory_space=pltpu.VMEM)
SMEM = pl.BlockSpec(memory_space=pltpu.SMEM)


def chunk_pieces(z):
    base = z * CHUNK
    if z % 2 == 0:
        return (base, FULL), (base + FULL, HALF)
    return (base + HALF, FULL), (base, HALF)


def dot(a, b, ca, cb):
    return lax.dot_general(a, b, (((ca,), (cb,)), ((), ())), preferred_element_type=f32)


def chunk_rows(z):
    odd = lax.rem(z, 2)
    base = z * CHUNK
    return pl.multiple_of(base + odd * HALF, HALF), pl.multiple_of(base + (1 - odd) * FULL, HALF)


def send_pieces(z, t_ref, outs):
    for s, out in enumerate(outs):
        full, half = chunk_rows(lax.rem(z + s, Z))
        out[0:FULL, :] = t_ref[pl.ds(full, FULL), :]
        out[FULL:CHUNK, :] = t_ref[pl.ds(half, HALF), :]


def key_kernel(me_ref, x_ref, w_ref, n_ref, *rest):
    outs, t_ref = rest[:Z], rest[Z]
    x = x_ref[...].astype(f32)
    centred = x - jnp.mean(x, axis=-1, keepdims=True)
    var = jnp.mean(centred * centred, axis=-1, keepdims=True)
    n_ref[...] = (centred * lax.rsqrt(var + 1e-05)).astype(bf16)
    t_ref[...] = dot(w_ref[...], n_ref[...].reshape(ROWS * RES, EMBED), 0, 1).astype(bf16)
    send_pieces(me_ref[2], t_ref, outs)


def key_chunks(me, x, w):
    n, *k = pl.pallas_call(
        key_kernel,
        out_shape=(jax.ShapeDtypeStruct((ROWS, RES, EMBED), bf16),)
        + (jax.ShapeDtypeStruct((CHUNK, ROWS * RES), bf16),) * Z,
        in_specs=[SMEM, VMEM, VMEM],
        out_specs=(VMEM,) * (Z + 1),
        scratch_shapes=[pltpu.VMEM((EMBED, ROWS * RES), bf16)],
        compiler_params=PARAMS,
    )(me, x, w)
    return n, k


def query_kernel(n_ref, w_ref, q_ref):
    for c in range(2):
        n = n_ref[:, c * SUB : (c + 1) * SUB, :].reshape(ROWS * SUB, EMBED)
        t = dot(w_ref[...], n, 0, 1).astype(bf16)
        for z in range(Z):
            (a, na), (b, nb) = chunk_pieces(z)
            q_ref[2 * z + c, 0:FULL, :] = t[a : a + na]
            q_ref[2 * z + c, FULL:CHUNK, :] = t[b : b + nb]


def query_chunks(n, w):
    return pl.pallas_call(
        query_kernel,
        out_shape=jax.ShapeDtypeStruct((2 * Z, CHUNK, ROWS * SUB), bf16),
        in_specs=[VMEM] * 2,
        out_specs=VMEM,
        compiler_params=PARAMS,
        cost_estimate=PROJECTION,
    )(n, w)


def value_kernel(me_ref, n_ref, w_ref, *rest):
    outs, t_ref = rest[:Z], rest[Z]
    t_ref[...] = dot(w_ref[...], n_ref[...].reshape(ROWS * RES, EMBED), 0, 1).astype(bf16)
    send_pieces(me_ref[2], t_ref, outs)


def value_chunks(me, n, w):
    return pl.pallas_call(
        value_kernel,
        out_shape=(jax.ShapeDtypeStruct((CHUNK, ROWS * RES), bf16),) * Z,
        in_specs=[SMEM, VMEM, VMEM],
        out_specs=(VMEM,) * Z,
        scratch_shapes=[pltpu.VMEM((EMBED, ROWS * RES), bf16)],
        compiler_params=PARAMS,
        cost_estimate=PROJECTION,
    )(me, n, w)


def arrived(z, refs):
    return [ref[lax.rem(z - source + Z, Z)] for ref in refs for source in range(Z)]


def widen(blocks, r):
    return jnp.concatenate([b[:, r * RES : (r + 1) * RES] for b in blocks], axis=1)


def score_kernel(me_ref, q_ref, k00, k01, k10, k11, out, qf, qh, kf, kh):
    core, z = me_ref[1], me_ref[2]
    for cr, ks in ((0, (k00, k01)), (1, (k10, k11))):
        c = jnp.bitwise_xor(core, cr)
        queries = [q_ref[2 * p + c] for p in range(PEERS)]
        keys = arrived(z, ks)
        for r in range(ROWS):
            n = cr * ROWS + r
            t = jnp.concatenate([b[:, r * SUB : (r + 1) * SUB] for b in queries], axis=1)
            qf[n * FULL : (n + 1) * FULL, :] = t[:FULL]
            qh[n * HALF : (n + 1) * HALF, :] = t[FULL:]
            t = widen(keys, r)
            kf[n * FULL : (n + 1) * FULL, :] = t[:FULL]
            kh[n * HALF : (n + 1) * HALF, :] = t[FULL:]
    for i, (a, b) in enumerate(((qf, kf), (qh, kh))):
        s = dot(a[...], b[...], 0, 0)
        for p in range(PEERS):
            out[p, i] = s[p * SUB : (p + 1) * SUB]


def score(me, q, ks):
    rows = 2 * ROWS
    return pl.pallas_call(
        score_kernel,
        out_shape=jax.ShapeDtypeStruct((PEERS, 2, SUB, KEYS), f32),
        in_specs=[SMEM] + [VMEM] * 5,
        out_specs=VMEM,
        scratch_shapes=[
            pltpu.VMEM((rows * FULL, QUERIES), bf16),
            pltpu.VMEM((rows * HALF, QUERIES), bf16),
            pltpu.VMEM((rows * FULL, KEYS), bf16),
            pltpu.VMEM((rows * HALF, KEYS), bf16),
        ],
        compiler_params=PARAMS,
    )(me, q, *ks)


def total_kernel(parts, full, half):
    for i, out in enumerate((full, half)):
        t = parts[0, i]
        for p in range(1, PEERS):
            t = t + parts[p, i]
        out[...] = t


def total(parts):
    return pl.pallas_call(
        total_kernel,
        out_shape=(jax.ShapeDtypeStruct((SUB, KEYS), f32),) * 2,
        in_specs=[VMEM],
        out_specs=(VMEM,) * 2,
        compiler_params=PARAMS,
    )(parts)


def softmax_kernel(factor, full, half, other, out):
    for i, logits in enumerate((full[...], half[...] + other[...])):
        logits = logits * factor
        powered = jnp.exp(logits - jnp.max(logits, axis=-1, keepdims=True))
        probs = (powered / jnp.sum(powered, axis=-1, keepdims=True)).astype(bf16)
        for p in range(PEERS):
            out[p, i] = probs


def softmax(factor, full, half, other):
    return pl.pallas_call(
        functools.partial(softmax_kernel, factor),
        out_shape=jax.ShapeDtypeStruct((PEERS, 2, SUB, KEYS), bf16),
        in_specs=[VMEM] * 3,
        out_specs=VMEM,
        compiler_params=PARAMS,
    )(full, half, other)


def mix_kernel(me_ref, v00, v01, v10, v11, p_ref, o_ref, vf, vh):
    core, z = me_ref[1], me_ref[2]
    pf, ph = (p_ref[:, i].reshape(QUERIES, KEYS) for i in range(2))
    for cr, vs in ((0, (v00, v01)), (1, (v10, v11))):
        c = jnp.bitwise_xor(core, cr)
        values = arrived(z, vs)
        for r in range(ROWS):
            t = widen(values, r)
            vf[r * FULL : (r + 1) * FULL, :] = t[:FULL]
            vh[r * HALF : (r + 1) * HALF, :] = t[FULL:]
        for v, p, first, n in ((vf, pf, 0, FULL), (vh, ph, FULL, HALF)):
            mixed = dot(v[...], p, 1, 1).astype(bf16)
            for s in range(PEERS):
                o_ref[2 * s + c, first : first + n, :] = jnp.concatenate(
                    [mixed[r * n : (r + 1) * n, s * SUB : (s + 1) * SUB] for r in range(ROWS)], axis=1
                )


def mix(me, vs, probs):
    return pl.pallas_call(
        mix_kernel,
        out_shape=jax.ShapeDtypeStruct((2 * Z, CHUNK, ROWS * SUB), bf16),
        in_specs=[SMEM] + [VMEM] * 5,
        out_specs=VMEM,
        scratch_shapes=[
            pltpu.VMEM((ROWS * FULL, KEYS), bf16),
            pltpu.VMEM((ROWS * HALF, KEYS), bf16),
        ],
        compiler_params=PARAMS,
    )(me, *vs, probs)


def final_kernel(m_ref, w_ref, o_ref, t_ref):
    for c in range(2):
        for z in range(Z):
            (a, na), (b, nb) = chunk_pieces(z)
            t_ref[a : a + na, :] = m_ref[2 * z + c, 0:FULL, :]
            t_ref[b : b + nb, :] = m_ref[2 * z + c, FULL:CHUNK, :]
        attended = dot(t_ref[...], w_ref[...], 0, 0).astype(bf16)
        o_ref[:, c * SUB : (c + 1) * SUB, :] = attended.reshape(ROWS, SUB, EMBED)


def final(m, w):
    return pl.pallas_call(
        final_kernel,
        out_shape=jax.ShapeDtypeStruct((ROWS, RES, EMBED), bf16),
        in_specs=[VMEM] * 2,
        out_specs=VMEM,
        scratch_shapes=[pltpu.VMEM((EMBED, ROWS * SUB), bf16)],
        compiler_params=PARAMS,
    )(m, w)


def flip(x, axes, n, s):
    return lax.ppermute(x, axes, [(i, i ^ s) for i in range(n)])


def gather4(own):
    far = flip(own, "xl", 2, 1)
    return own, far, flip(own, "c", 2, 1), flip(far, "c", 2, 1)


def spread(pieces):
    got = {0: pieces[0]}
    for s in (1, 7, 2, 6, 3, 5, 4):
        got[s] = lax.ppermute(pieces[s], "z", [(i, (i + s) % Z) for i in range(Z)])
    return jnp.stack([got[s] for s in range(Z)])


def local(x, wq, wk, wv, wf):
    me = jnp.stack([lax.axis_index(("y", "xh")), lax.axis_index("c"), lax.axis_index("z")])
    me = me.astype(jnp.int32)
    n, k = key_chunks(me, x, wk)
    q = query_chunks(n, wq)
    v = value_chunks(me, n, wv)
    ks = gather4(spread(k))
    q = lax.all_to_all(q, ("z", "c"), 0, 0, tiled=True)
    v, scores = lax.optimization_barrier((v, score(me, q, ks)))
    parts = lax.all_to_all(scores, ("y", "xh"), 0, 0, tiled=True)
    vs = gather4(spread(v))
    full, half = total(parts)
    rows = ROWS * 2 * PEERS
    probs = softmax(1.0 / math.sqrt(DH * rows), full, half, flip(half, "z", Z, 1))
    probs = lax.all_to_all(probs, ("y", "xh"), 0, 0, tiled=True)
    mixed = lax.all_to_all(mix(me, vs, probs), ("z", "c"), 0, 0, tiled=True)
    return final(mixed, wf)


def solution(mesh):
    fine = Mesh(mesh.devices.reshape(4, 2, 2, 8, 2), ("y", "xh", "c", "z", "xl"))
    spec = P(("y", "xh", "c"), ("z", "xl"), None)
    return jax.shard_map(
        local,
        mesh=fine,
        in_specs=(spec, P(), P(), P(), P()),
        out_specs=spec,
        check_vma=False,
    )
```

```python
import functools
import math

import jax
import jax.numpy as jnp
from jax import lax
from jax.experimental import pallas as pl
from jax.experimental.pallas import tpu as pltpu
from jax.sharding import Mesh, PartitionSpec as P

H = 12
DH = 64
EMBED = 768
ROWS = 8
RES = 64
Z = 8
CHUNK = EMBED // Z
FULL = DH
HALF = CHUNK - DH
PEERS = 8
SUB = RES // 2
KSTEP = 2 * FULL + FULL
QUERIES = Z * SUB
KEYS = 2 * Z * RES

f32 = jnp.float32
bf16 = jnp.bfloat16
PARAMS = pltpu.CompilerParams(vmem_limit_bytes=8 * 1024 * 1024)
PROJECTION = pl.CostEstimate(
    flops=2 * ROWS * RES * EMBED * EMBED, bytes_accessed=2 * EMBED * (EMBED + 2 * ROWS * RES), transcendentals=0
)
LAYOUT = pl.CostEstimate(flops=0, bytes_accessed=16 * ROWS * RES * EMBED, transcendentals=0)
KEY_SHAPES = ((2 * ROWS * FULL, KEYS // 2), (2 * ROWS * FULL, KEYS // 4))
VMEM = pl.BlockSpec(memory_space=pltpu.VMEM)
SMEM = pl.BlockSpec(memory_space=pltpu.SMEM)


def chunk_pieces(z):
    base = z * CHUNK
    if z % 2 == 0:
        return (base, FULL), (base + FULL, HALF)
    return (base + HALF, FULL), (base, HALF)


def dot(a, b, ca, cb):
    return lax.dot_general(a, b, (((ca,), (cb,)), ((), ())), preferred_element_type=f32)


def chunk_rows(z):
    odd = lax.rem(z, 2)
    base = z * CHUNK
    return pl.multiple_of(base + odd * HALF, HALF), pl.multiple_of(base + (1 - odd) * FULL, HALF)


def send_pieces(z, t_ref, outs):
    for s, out in enumerate(outs):
        full, half = chunk_rows(lax.rem(z + s, Z))
        out[0:FULL, :] = t_ref[pl.ds(full, FULL), :]
        out[FULL:CHUNK, :] = t_ref[pl.ds(half, HALF), :]


def key_kernel(me_ref, x_ref, w_ref, n_ref, *rest):
    outs, t_ref = rest[:Z], rest[Z]
    x = x_ref[...].astype(f32)
    centred = x - jnp.mean(x, axis=-1, keepdims=True)
    var = jnp.mean(centred * centred, axis=-1, keepdims=True)
    n_ref[...] = (centred * lax.rsqrt(var + 1e-05)).astype(bf16)
    t_ref[...] = dot(w_ref[...], n_ref[...].reshape(ROWS * RES, EMBED), 0, 1).astype(bf16)
    for s, out in enumerate(outs):
        z = lax.rem(me_ref[2] + s, Z)
        out[0:FULL, :] = t_ref[pl.ds(chunk_rows(z)[0], FULL), :]
        if s % 2 == 0:
            shared = pl.multiple_of(lax.div(z, 2) * (2 * CHUNK) + FULL, FULL)
            out[FULL:, :] = t_ref[pl.ds(shared, FULL), :]


def key_chunks(me, x, w):
    n, *k = pl.pallas_call(
        key_kernel,
        out_shape=(jax.ShapeDtypeStruct((ROWS, RES, EMBED), bf16),)
        + tuple(jax.ShapeDtypeStruct((FULL * (2 - s % 2), ROWS * RES), bf16) for s in range(Z)),
        in_specs=[SMEM, VMEM, VMEM],
        out_specs=(VMEM,) * (Z + 1),
        scratch_shapes=[pltpu.VMEM((EMBED, ROWS * RES), bf16)],
        compiler_params=PARAMS,
    )(me, x, w)
    return n, k


def query_kernel(n_ref, w_ref, q_ref):
    for c in range(2):
        n = n_ref[:, c * SUB : (c + 1) * SUB, :].reshape(ROWS * SUB, EMBED)
        t = dot(w_ref[...], n, 0, 1).astype(bf16)
        for z in range(Z):
            (a, na), _ = chunk_pieces(z)
            b = (z // 2) * 2 * CHUNK + FULL
            q_ref[2 * z + c, 0:FULL, :] = t[a : a + na]
            q_ref[2 * z + c, FULL:, :] = t[b : b + FULL]


def query_chunks(n, w):
    return pl.pallas_call(
        query_kernel,
        out_shape=jax.ShapeDtypeStruct((2 * Z, 2 * FULL, ROWS * SUB), bf16),
        in_specs=[VMEM] * 2,
        out_specs=VMEM,
        compiler_params=PARAMS,
        cost_estimate=PROJECTION,
    )(n, w)


def value_kernel(me_ref, n_ref, w_ref, *rest):
    outs, t_ref = rest[:Z], rest[Z]
    t_ref[...] = dot(w_ref[...], n_ref[...].reshape(ROWS * RES, EMBED), 0, 1).astype(bf16)
    send_pieces(me_ref[2], t_ref, outs)


def value_chunks(me, n, w):
    return pl.pallas_call(
        value_kernel,
        out_shape=(jax.ShapeDtypeStruct((CHUNK, ROWS * RES), bf16),) * Z,
        in_specs=[SMEM, VMEM, VMEM],
        out_specs=(VMEM,) * Z,
        scratch_shapes=[pltpu.VMEM((EMBED, ROWS * RES), bf16)],
        compiler_params=PARAMS,
        cost_estimate=PROJECTION,
    )(me, n, w)


def widen(blocks, r):
    return jnp.concatenate([b[:, r * RES : (r + 1) * RES] for b in blocks], axis=1)


def lay_keys(z, own, other, kf, kh):
    def piece(ref, source, extra):
        s = lax.rem(z - source + Z, Z)
        first = lax.div(s, 2) * KSTEP + lax.rem(s, 2) * (2 * FULL) + extra
        return ref[pl.ds(pl.multiple_of(first, FULL), FULL), :]

    odd = lax.rem(z, 2)
    for cr, ref in enumerate((own, other)):
        whole = [piece(ref, source, 0) for source in range(Z)]
        shared = [piece(ref, 2 * source + odd, FULL) for source in range(Z // 2)]
        for r in range(ROWS):
            rows = slice((cr * ROWS + r) * FULL, (cr * ROWS + r + 1) * FULL)
            kf[rows, :] = widen(whole, r)
            kh[rows, :] = widen(shared, r)


def keys_kernel(me_ref, own, other, kf, kh):
    lay_keys(me_ref[2], own, other, kf, kh)


def keys_laid(me, own, other):
    return pl.pallas_call(
        keys_kernel,
        out_shape=tuple(jax.ShapeDtypeStruct(s, bf16) for s in KEY_SHAPES),
        in_specs=[SMEM, VMEM, VMEM],
        out_specs=(VMEM,) * 2,
        compiler_params=PARAMS,
        cost_estimate=LAYOUT,
    )(me, own, other)


def score_kernel(me_ref, q_ref, kf0, kh0, own, other, out, qf, qh, kf1, kh1):
    core = me_ref[1]
    lay_keys(me_ref[2], own, other, kf1, kh1)
    for cr in range(2):
        c = jnp.bitwise_xor(core, cr)
        queries = [q_ref[2 * p + c] for p in range(PEERS)]
        for r in range(ROWS):
            rows = slice((cr * ROWS + r) * FULL, (cr * ROWS + r + 1) * FULL)
            t = jnp.concatenate([b[:, r * SUB : (r + 1) * SUB] for b in queries], axis=1)
            qf[rows, :] = t[:FULL]
            qh[rows, :] = t[FULL:]
    first = 0
    for a, b in ((qf, kf0), (qf, kf1), (qh, kh0), (qh, kh1)):
        s = dot(a[...], b[...], 0, 0)
        for p in range(PEERS):
            out[p, :, first : first + s.shape[1]] = s[p * SUB : (p + 1) * SUB]
        first += s.shape[1]


def score(me, q, laid, own, other):
    rows = 2 * ROWS * FULL
    return pl.pallas_call(
        score_kernel,
        out_shape=jax.ShapeDtypeStruct((PEERS, SUB, KEYS + KEYS // 2), f32),
        in_specs=[SMEM] + [VMEM] * 5,
        out_specs=VMEM,
        scratch_shapes=[pltpu.VMEM((rows, QUERIES), bf16)] * 2 + [pltpu.VMEM(s, bf16) for s in KEY_SHAPES],
        compiler_params=PARAMS,
    )(me, q, *laid, own, other)


def total_kernel(parts, full, half):
    t = parts[0]
    for p in range(1, PEERS):
        t = t + parts[p]
    full[...] = t[:, :KEYS]
    half[...] = t[:, KEYS:]


def total(parts):
    return pl.pallas_call(
        total_kernel,
        out_shape=tuple(jax.ShapeDtypeStruct((SUB, n), f32) for n in (KEYS, KEYS // 2)),
        in_specs=[VMEM],
        out_specs=(VMEM,) * 2,
        compiler_params=PARAMS,
    )(parts)


def softmax_kernel(factor, full, half, other, out):
    for i, logits in enumerate((full[...], jnp.concatenate([half[...], other[...]], axis=1))):
        logits = logits * factor
        powered = jnp.exp(logits - jnp.max(logits, axis=-1, keepdims=True))
        probs = (powered / jnp.sum(powered, axis=-1, keepdims=True)).astype(bf16)
        for p in range(PEERS):
            out[p, i] = probs


def softmax(factor, full, half, other):
    return pl.pallas_call(
        functools.partial(softmax_kernel, factor),
        out_shape=jax.ShapeDtypeStruct((PEERS, 2, SUB, KEYS), bf16),
        in_specs=[VMEM] * 3,
        out_specs=VMEM,
        compiler_params=PARAMS,
    )(full, half, other)


def values_kernel(me_ref, v00, v01, v10, v11, vf, vh):
    z = me_ref[2]
    odd = lax.rem(z, 2)
    for cr, refs in enumerate(((v00, v01), (v10, v11))):
        blocks = [[ref[lax.rem(z - source + Z, Z)] for source in range(Z)] for ref in refs]
        shared = [
            ref[lax.rem(z - (2 * source + parity) + Z, Z), FULL:CHUNK, :]
            for parity in (odd, 1 - odd)
            for ref in refs
            for source in range(Z // 2)
        ]
        whole = [b[:FULL] for ref in blocks for b in ref]
        for r in range(ROWS):
            n = cr * ROWS + r
            vf[n * FULL : (n + 1) * FULL, :] = widen(whole, r)
            vh[n * HALF : (n + 1) * HALF, :] = widen(shared, r)


def values_laid(me, vs):
    return pl.pallas_call(
        values_kernel,
        out_shape=tuple(jax.ShapeDtypeStruct((2 * ROWS * n, KEYS), bf16) for n in (FULL, HALF)),
        in_specs=[SMEM] + [VMEM] * 4,
        out_specs=(VMEM,) * 2,
        compiler_params=PARAMS,
        cost_estimate=LAYOUT,
    )(me, *vs)


def mix_kernel(me_ref, vf, vh, p_ref, o_ref):
    core = me_ref[1]
    for i, (v, first, n) in enumerate(((vf, 0, FULL), (vh, FULL, HALF))):
        probs = p_ref[:, i].reshape(QUERIES, KEYS)
        for cr in range(2):
            c = jnp.bitwise_xor(core, cr)
            mixed = dot(v[cr * ROWS * n : (cr + 1) * ROWS * n, :], probs, 1, 1).astype(bf16)
            for s in range(PEERS):
                o_ref[2 * s + c, first : first + n, :] = jnp.concatenate(
                    [mixed[r * n : (r + 1) * n, s * SUB : (s + 1) * SUB] for r in range(ROWS)], axis=1
                )


def mix(me, laid, probs):
    return pl.pallas_call(
        mix_kernel,
        out_shape=jax.ShapeDtypeStruct((2 * Z, CHUNK, ROWS * SUB), bf16),
        in_specs=[SMEM] + [VMEM] * 3,
        out_specs=VMEM,
        compiler_params=PARAMS,
    )(me, *laid, probs)


def final_kernel(m_ref, w_ref, o_ref, t_ref):
    for c in range(2):
        for z in range(Z):
            (a, na), (b, nb) = chunk_pieces(z)
            t_ref[a : a + na, :] = m_ref[2 * z + c, 0:FULL, :]
            t_ref[b : b + nb, :] = m_ref[2 * z + c, FULL:CHUNK, :]
        attended = dot(t_ref[...], w_ref[...], 0, 0).astype(bf16)
        o_ref[:, c * SUB : (c + 1) * SUB, :] = attended.reshape(ROWS, SUB, EMBED)


def final(m, w):
    return pl.pallas_call(
        final_kernel,
        out_shape=jax.ShapeDtypeStruct((ROWS, RES, EMBED), bf16),
        in_specs=[VMEM] * 2,
        out_specs=VMEM,
        scratch_shapes=[pltpu.VMEM((EMBED, ROWS * SUB), bf16)],
        compiler_params=PARAMS,
    )(m, w)


def flip(x, axes, n, s):
    return lax.ppermute(x, axes, [(i, i ^ s) for i in range(n)])


def gather4(own):
    far = flip(own, "xl", 2, 1)
    return own, far, flip(own, "c", 2, 1), flip(far, "c", 2, 1)


ORDER = (1, 7, 2, 6, 3, 5, 4)


def spread(pieces):
    got = {0: pieces[0]}
    for s in ORDER:
        got[s] = lax.ppermute(pieces[s], "z", [(i, (i + s) % Z) for i in range(Z)])
    return [got[s] for s in range(Z)]


def local(x, wq, wk, wv, wf):
    me = jnp.stack([lax.axis_index(("y", "xh")), lax.axis_index("c"), lax.axis_index("z")])
    me = me.astype(jnp.int32)
    n, k = key_chunks(me, x, wk)
    q = query_chunks(n, wq)
    v = value_chunks(me, n, wv)
    k = spread(k)
    q, k[1] = lax.optimization_barrier((q, k[1]))
    q = lax.all_to_all(q, ("z", "c"), 0, 0, tiled=True)
    k00, k01, k10, k11 = gather4(jnp.concatenate(k))
    v, scores = lax.optimization_barrier((v, score(me, q, keys_laid(me, k00, k10), k01, k11)))
    parts = lax.all_to_all(scores, ("y", "xh"), 0, 0, tiled=True)
    laid = values_laid(me, gather4(jnp.stack(spread(v))))
    full, half = total(parts)
    rows = ROWS * 2 * PEERS
    probs = softmax(1.0 / math.sqrt(DH * rows), full, half, flip(half, "z", Z, 1))
    probs = lax.all_to_all(probs, ("y", "xh"), 0, 0, tiled=True)
    mixed = lax.all_to_all(mix(me, laid, probs), ("z", "c"), 0, 0, tiled=True)
    return final(mixed, wf)


def solution(mesh):
    fine = Mesh(mesh.devices.reshape(4, 2, 2, 8, 2), ("y", "xh", "c", "z", "xl"))
    spec = P(("y", "xh", "c"), ("z", "xl"), None)
    return jax.shard_map(
        local,
        mesh=fine,
        in_specs=(spec, P(), P(), P(), P()),
        out_specs=spec,
        check_vma=False,
    )
```

```python
import functools
import math

import jax
import jax.numpy as jnp
from jax import lax
from jax.experimental import pallas as pl
from jax.experimental.pallas import tpu as pltpu
from jax.sharding import Mesh, PartitionSpec as P

H = 12
DH = 64
EMBED = 768
ROWS = 8
RES = 64
Z = 8
CHUNK = EMBED // Z
FULL = DH
HALF = CHUNK - DH
PEERS = 8
SUB = RES // 2
TOKENS = ROWS * SUB
QUERIES = Z * SUB
KEYS = 2 * Z * RES

f32 = jnp.float32
bf16 = jnp.bfloat16
PARAMS = pltpu.CompilerParams(vmem_limit_bytes=8 * 1024 * 1024)
PROJECTION = pl.CostEstimate(
    flops=2 * ROWS * RES * EMBED * EMBED, bytes_accessed=2 * EMBED * (EMBED + 2 * ROWS * RES), transcendentals=0
)
LAYOUT = pl.CostEstimate(flops=0, bytes_accessed=16 * ROWS * RES * EMBED, transcendentals=0)
KEY_SHAPES = ((2 * ROWS * FULL, KEYS // 2), (2 * ROWS * FULL, KEYS // 4))
VMEM = pl.BlockSpec(memory_space=pltpu.VMEM)
SMEM = pl.BlockSpec(memory_space=pltpu.SMEM)


def chunk_pieces(z):
    base = z * CHUNK
    if z % 2 == 0:
        return (base, FULL), (base + FULL, HALF)
    return (base + HALF, FULL), (base, HALF)


def dot(a, b, ca, cb):
    return lax.dot_general(a, b, (((ca,), (cb,)), ((), ())), preferred_element_type=f32)


def shared_head(z):
    return z // 2 * (2 * CHUNK) + FULL if isinstance(z, int) else lax.div(z, 2) * (2 * CHUNK) + FULL


def chunk_rows(z):
    odd = lax.rem(z, 2)
    base = z * CHUNK
    return pl.multiple_of(base + odd * HALF, HALF), pl.multiple_of(base + (1 - odd) * FULL, HALF)


def key_kernel(me_ref, x_ref, w_ref, n_ref, give_ref, k_ref):
    x = x_ref[...].astype(f32)
    centred = x - jnp.mean(x, axis=-1, keepdims=True)
    var = jnp.mean(centred * centred, axis=-1, keepdims=True)
    normed = (centred * lax.rsqrt(var + 1e-05)).astype(bf16)
    for h in range(2):
        n_ref[h] = normed[:, h * SUB : (h + 1) * SUB, :]
    give_ref[...] = n_ref[1 - me_ref[1]]
    t = dot(w_ref[...], n_ref[...].reshape(ROWS * RES, EMBED), 0, 1).astype(bf16)
    for z in range(Z):
        (a, _), _ = chunk_pieces(z)
        b, lanes = shared_head(z), slice(z % 2 * TOKENS, (z % 2 + 1) * TOKENS)
        k_ref[z, 0:FULL, :] = t[a : a + FULL]
        k_ref[z, FULL:CHUNK, :TOKENS] = t[b : b + HALF, lanes]
        k_ref[z, FULL:CHUNK, TOKENS:] = t[b + HALF : b + FULL, lanes]


def key_chunks(me, x, w):
    return pl.pallas_call(
        key_kernel,
        out_shape=(
            jax.ShapeDtypeStruct((2, ROWS, SUB, EMBED), bf16),
            jax.ShapeDtypeStruct((ROWS, SUB, EMBED), bf16),
            jax.ShapeDtypeStruct((Z, CHUNK, ROWS * RES), bf16),
        ),
        in_specs=[SMEM, VMEM, VMEM],
        out_specs=(VMEM,) * 3,
        compiler_params=PARAMS,
    )(me, x, w)


def query_kernel(me_ref, n_ref, got_ref, w_ref, *rest):
    outs, t_ref = rest[:Z], rest[Z]
    for c, n in enumerate((n_ref[me_ref[1]], got_ref[...])):
        t = dot(w_ref[...], n.reshape(TOKENS, EMBED), 0, 1)
        t_ref[:, c * TOKENS : (c + 1) * TOKENS] = t.astype(bf16)
    for s, out in enumerate(outs):
        z = lax.rem(me_ref[2] + s, Z)
        out[0:FULL, :] = t_ref[pl.ds(chunk_rows(z)[0], FULL), :]
        out[FULL:, :] = t_ref[pl.ds(pl.multiple_of(shared_head(z), FULL), FULL), :]


def query_chunks(me, n, got, w):
    return pl.pallas_call(
        query_kernel,
        out_shape=(jax.ShapeDtypeStruct((2 * FULL, 2 * TOKENS), bf16),) * Z,
        in_specs=[SMEM] + [VMEM] * 3,
        out_specs=(VMEM,) * Z,
        scratch_shapes=[pltpu.VMEM((EMBED, 2 * TOKENS), bf16)],
        compiler_params=PARAMS,
        cost_estimate=PROJECTION,
    )(me, n, got, w)


def value_kernel(me_ref, n_ref, w_ref, *rest):
    outs, t_ref = rest[:Z], rest[Z]
    t_ref[...] = dot(w_ref[...], n_ref[...].reshape(ROWS * RES, EMBED), 0, 1).astype(bf16)
    for s, out in enumerate(outs):
        full, half = chunk_rows(lax.rem(me_ref[2] + s, Z))
        out[0:FULL, :] = t_ref[pl.ds(full, FULL), :]
        out[FULL:CHUNK, :] = t_ref[pl.ds(half, HALF), :]


def value_chunks(me, n, w):
    return pl.pallas_call(
        value_kernel,
        out_shape=(jax.ShapeDtypeStruct((CHUNK, ROWS * RES), bf16),) * Z,
        in_specs=[SMEM, VMEM, VMEM],
        out_specs=(VMEM,) * Z,
        scratch_shapes=[pltpu.VMEM((EMBED, ROWS * RES), bf16)],
        compiler_params=PARAMS,
        cost_estimate=PROJECTION,
    )(me, n, w)


def lay_keys(own, other, kf, kh):
    for cr, ref in enumerate((own, other)):
        for r in range(ROWS):
            n = (cr * ROWS + r) * FULL
            whole = [ref[z, 0:FULL, h * TOKENS + r * SUB : h * TOKENS + (r + 1) * SUB] for z in range(Z) for h in range(2)]
            kf[n : n + FULL, :] = jnp.concatenate(whole, axis=1)
            for d in range(2):
                first = d * TOKENS + r * SUB
                shared = [ref[z, FULL:CHUNK, first : first + SUB] for z in range(Z)]
                kh[n + d * HALF : n + (d + 1) * HALF, :] = jnp.concatenate(shared, axis=1)


def keys_laid(own, other):
    return pl.pallas_call(
        lay_keys,
        out_shape=tuple(jax.ShapeDtypeStruct(s, bf16) for s in KEY_SHAPES),
        in_specs=[VMEM, VMEM],
        out_specs=(VMEM,) * 2,
        compiler_params=PARAMS,
        cost_estimate=LAYOUT,
    )(own, other)


def score_kernel(me_ref, kf0, kh0, own, other, *rest):
    qs, out, (qf, qh, kf1, kh1) = rest[:Z], rest[Z], rest[Z + 1 :]
    lay_keys(own, other, kf1, kh1)
    for n in range(2 * ROWS):
        t = jnp.concatenate([q[:, n * SUB : (n + 1) * SUB] for q in qs], axis=1)
        qf[n * FULL : (n + 1) * FULL, :] = t[:FULL]
        qh[n * FULL : (n + 1) * FULL, :] = t[FULL:]
    first = 0
    for a, b in ((qf, kf0), (qf, kf1), (qh, kh0), (qh, kh1)):
        t = dot(a[...], b[...], 0, 0)
        for s in range(Z):
            source = lax.rem(me_ref[2] - s + Z, Z)
            out[source, :, first : first + t.shape[1]] = t[s * SUB : (s + 1) * SUB]
        first += t.shape[1]


def score(me, qs, laid, own, other):
    rows = 2 * ROWS * FULL
    return pl.pallas_call(
        score_kernel,
        out_shape=jax.ShapeDtypeStruct((PEERS, SUB, KEYS + KEYS // 2), f32),
        in_specs=[SMEM] + [VMEM] * (4 + Z),
        out_specs=VMEM,
        scratch_shapes=[pltpu.VMEM((rows, QUERIES), bf16)] * 2 + [pltpu.VMEM(s, bf16) for s in KEY_SHAPES],
        compiler_params=PARAMS,
    )(me, *laid, own, other, *qs)


def total_kernel(parts, full, half):
    t = parts[0]
    for p in range(1, PEERS):
        t = t + parts[p]
    full[...] = t[:, :KEYS]
    half[...] = t[:, KEYS:]


def total(parts):
    return pl.pallas_call(
        total_kernel,
        out_shape=tuple(jax.ShapeDtypeStruct((SUB, n), f32) for n in (KEYS, KEYS // 2)),
        in_specs=[VMEM],
        out_specs=(VMEM,) * 2,
        compiler_params=PARAMS,
    )(parts)


def softmax_kernel(factor, full, half, other, out):
    for i, logits in enumerate((full[...], jnp.concatenate([half[...], other[...]], axis=1))):
        logits = logits * factor
        powered = jnp.exp(logits - jnp.max(logits, axis=-1, keepdims=True))
        probs = (powered / jnp.sum(powered, axis=-1, keepdims=True)).astype(bf16)
        for p in range(PEERS):
            out[p, i] = probs


def softmax(factor, full, half, other):
    return pl.pallas_call(
        functools.partial(softmax_kernel, factor),
        out_shape=jax.ShapeDtypeStruct((PEERS, 2, SUB, KEYS), bf16),
        in_specs=[VMEM] * 3,
        out_specs=VMEM,
        compiler_params=PARAMS,
    )(full, half, other)


def values_kernel(me_ref, v00, v01, v10, v11, vf, vh):
    z = me_ref[2]
    odd = lax.rem(z, 2)
    where = [lax.rem(z - source + Z, Z) for source in range(Z)]
    for cr, refs in enumerate(((v00, v01), (v10, v11))):
        halves = [
            ref[i, FULL:CHUNK, pl.ds(pl.multiple_of(h * TOKENS, TOKENS), TOKENS)]
            for h in (odd, 1 - odd)
            for ref in refs
            for i in where
        ]
        whole = [ref[i, 0:FULL, h * TOKENS : (h + 1) * TOKENS] for ref in refs for i in where for h in range(2)]
        for r in range(ROWS):
            n = cr * ROWS + r
            lanes = slice(r * SUB, (r + 1) * SUB)
            vf[n * FULL : (n + 1) * FULL, :] = jnp.concatenate([b[:, lanes] for b in whole], axis=1)
            vh[n * HALF : (n + 1) * HALF, :] = jnp.concatenate([b[:, lanes] for b in halves], axis=1)


def values_laid(me, vs):
    return pl.pallas_call(
        values_kernel,
        out_shape=tuple(jax.ShapeDtypeStruct((2 * ROWS * n, KEYS), bf16) for n in (FULL, HALF)),
        in_specs=[SMEM] + [VMEM] * 4,
        out_specs=(VMEM,) * 2,
        compiler_params=PARAMS,
        cost_estimate=LAYOUT,
    )(me, *vs)


def mix_kernel(me_ref, vf, vh, p_ref, o_ref):
    core = me_ref[1]
    for i, (v, first, n) in enumerate(((vf, 0, FULL), (vh, FULL, HALF))):
        probs = p_ref[:, i].reshape(QUERIES, KEYS)
        for cr in range(2):
            c = jnp.bitwise_xor(core, cr)
            mixed = dot(v[cr * ROWS * n : (cr + 1) * ROWS * n, :], probs, 1, 1).astype(bf16)
            for s in range(PEERS):
                o_ref[2 * s + c, first : first + n, :] = jnp.concatenate(
                    [mixed[r * n : (r + 1) * n, s * SUB : (s + 1) * SUB] for r in range(ROWS)], axis=1
                )


def mix(me, laid, probs):
    return pl.pallas_call(
        mix_kernel,
        out_shape=jax.ShapeDtypeStruct((2 * Z, CHUNK, ROWS * SUB), bf16),
        in_specs=[SMEM] + [VMEM] * 3,
        out_specs=VMEM,
        compiler_params=PARAMS,
    )(me, *laid, probs)


def final_kernel(m_ref, w_ref, o_ref, t_ref):
    for c in range(2):
        for z in range(Z):
            (a, na), (b, nb) = chunk_pieces(z)
            t_ref[a : a + na, :] = m_ref[2 * z + c, 0:FULL, :]
            t_ref[b : b + nb, :] = m_ref[2 * z + c, FULL:CHUNK, :]
        attended = dot(t_ref[...], w_ref[...], 0, 0).astype(bf16)
        o_ref[:, c * SUB : (c + 1) * SUB, :] = attended.reshape(ROWS, SUB, EMBED)


def final(m, w):
    return pl.pallas_call(
        final_kernel,
        out_shape=jax.ShapeDtypeStruct((ROWS, RES, EMBED), bf16),
        in_specs=[VMEM] * 2,
        out_specs=VMEM,
        scratch_shapes=[pltpu.VMEM((EMBED, ROWS * SUB), bf16)],
        compiler_params=PARAMS,
    )(m, w)


def flip(x, axes, n, s):
    return lax.ppermute(x, axes, [(i, i ^ s) for i in range(n)])


def gather4(own):
    far = flip(own, "xl", 2, 1)
    return own, far, flip(own, "c", 2, 1), flip(far, "c", 2, 1)


ORDER = (1, 7, 2, 6, 3, 5, 4)
WINDOW = 4


class Stream:
    def __init__(self):
        self.got = []

    def send(self, x, axis, permutation):
        if len(self.got) >= WINDOW:
            x, self.got[-WINDOW] = lax.optimization_barrier((x, self.got[-WINDOW]))
        self.got.append(lax.ppermute(x, axis, permutation))
        return len(self.got) - 1

    def spread(self, pieces):
        return {s: self.send(pieces[s], "z", [(i, (i + s) % Z) for i in range(Z)]) for s in ORDER}

    def arrived(self, own, places):
        return [own] + [self.got[places[s]] for s in range(1, Z)]


def local(x, wq, wk, wv, wf):
    me = jnp.stack([lax.axis_index(("y", "xh")), lax.axis_index("c"), lax.axis_index("z")])
    me = me.astype(jnp.int32)
    n, give, k = key_chunks(me, x, wk)
    k = lax.all_to_all(k, "z", 0, 0, tiled=True)
    q = query_chunks(me, n, flip(give, "c", 2, 1), wq)
    v = value_chunks(me, n, wv)
    stream = Stream()
    q_places = stream.spread(q)
    first = q_places[ORDER[0]]
    k, stream.got[first] = lax.optimization_barrier((k, stream.got[first]))
    far = flip(k, "xl", 2, 1)
    near = stream.send(k, "c", [(0, 1), (1, 0)])
    v_places = stream.spread(v)
    k_near = stream.got[near]
    scores = score(me, stream.arrived(q[0], q_places), keys_laid(k, k_near), far, flip(far, "c", 2, 1))
    parts = lax.all_to_all(scores, ("y", "xh"), 0, 0, tiled=True)
    vs = gather4(jnp.stack(stream.arrived(v[0], v_places)))
    full, half = total(parts)
    rows = ROWS * 2 * PEERS
    probs = softmax(1.0 / math.sqrt(DH * rows), full, half, flip(half, "z", Z, 1))
    probs = lax.all_to_all(probs, ("y", "xh"), 0, 0, tiled=True)
    mixed = lax.all_to_all(mix(me, values_laid(me, vs), probs), ("z", "c"), 0, 0, tiled=True)
    return final(mixed, wf)


def solution(mesh):
    fine = Mesh(mesh.devices.reshape(4, 2, 2, 8, 2), ("y", "xh", "c", "z", "xl"))
    spec = P(("y", "xh", "c"), ("z", "xl"), None)
    return jax.shard_map(
        local,
        mesh=fine,
        in_specs=(spec, P(), P(), P(), P()),
        out_specs=spec,
        check_vma=False,
    )
```

```python
import functools
import math

import jax
import jax.numpy as jnp
from jax import lax
from jax.experimental import pallas as pl
from jax.experimental.pallas import tpu as pltpu
from jax.sharding import Mesh, PartitionSpec as P

H = 12
DH = 64
EMBED = 768
ROWS = 8
RES = 64
Z = 8
CHUNK = EMBED // Z
FULL = DH
HALF = CHUNK - DH
PEERS = 8
SUB = RES // 2
TOKENS = ROWS * SUB
QUERIES = Z * SUB
KEYS = 2 * Z * RES
LOGITS = KEYS + KEYS // 2

f32 = jnp.float32
bf16 = jnp.bfloat16
PARAMS = pltpu.CompilerParams(vmem_limit_bytes=8 * 1024 * 1024)
PROJECTION = pl.CostEstimate(
    flops=2 * ROWS * RES * EMBED * EMBED, bytes_accessed=2 * EMBED * (EMBED + 2 * ROWS * RES), transcendentals=0
)
LAYOUT = pl.CostEstimate(flops=0, bytes_accessed=16 * ROWS * RES * EMBED, transcendentals=0)
KEY_SHAPES = ((2 * ROWS * FULL, KEYS // 2), (2 * ROWS * FULL, KEYS // 4))
WIDE = pltpu.CompilerParams(vmem_limit_bytes=16 * 1024 * 1024)
VMEM = pl.BlockSpec(memory_space=pltpu.VMEM)
SMEM = pl.BlockSpec(memory_space=pltpu.SMEM)
ANY = pl.BlockSpec(memory_space=pl.ANY)
HBM = pl.BlockSpec(memory_space=pltpu.HBM)


def chunk_pieces(z):
    base = z * CHUNK
    if z % 2 == 0:
        return (base, FULL), (base + FULL, HALF)
    return (base + HALF, FULL), (base, HALF)


def dot(a, b, ca, cb):
    return lax.dot_general(a, b, (((ca,), (cb,)), ((), ())), preferred_element_type=f32)


def shared_head(z):
    return z // 2 * (2 * CHUNK) + FULL


def fetches(sources, buffers, sems):
    copies = [pltpu.make_async_copy(a, b, sems.at[i]) for i, (a, b) in enumerate(zip(sources, buffers))]
    for copy in copies:
        copy.start()
    return copies


def key_kernel(x_hbm, w_hbm, n_ref, k_ref, x_ref, w_ref, sems):
    copy_x, copy_w = fetches((x_hbm, w_hbm), (x_ref, w_ref), sems)
    copy_x.wait()
    x = x_ref[...].astype(f32)
    centred = x - jnp.mean(x, axis=-1, keepdims=True)
    var = jnp.mean(centred * centred, axis=-1, keepdims=True)
    normed = (centred * lax.rsqrt(var + 1e-05)).astype(bf16)
    for h in range(2):
        n_ref[h] = normed[:, h * SUB : (h + 1) * SUB, :]
    copy_w.wait()
    t = dot(w_ref[...], n_ref[...].reshape(ROWS * RES, EMBED), 0, 1).astype(bf16)
    for z in range(Z):
        (a, _), _ = chunk_pieces(z)
        b, lanes = shared_head(z), slice(z % 2 * TOKENS, (z % 2 + 1) * TOKENS)
        k_ref[z, 0:FULL, :] = t[a : a + FULL]
        k_ref[z, FULL:CHUNK, :TOKENS] = t[b : b + HALF, lanes]
        k_ref[z, FULL:CHUNK, TOKENS:] = t[b + HALF : b + FULL, lanes]


def key_chunks(x, w):
    return pl.pallas_call(
        key_kernel,
        out_shape=(
            jax.ShapeDtypeStruct((2, ROWS, SUB, EMBED), bf16),
            jax.ShapeDtypeStruct((Z, CHUNK, ROWS * RES), bf16),
        ),
        in_specs=[HBM, HBM],
        out_specs=(VMEM,) * 2,
        scratch_shapes=[
            pltpu.VMEM((ROWS, RES, EMBED), bf16),
            pltpu.VMEM((EMBED, EMBED), bf16),
            pltpu.SemaphoreType.DMA((2,)),
        ],
        compiler_params=PARAMS,
    )(x, w)


def query_kernel(n_ref, w_ref, q_ref):
    for c in range(2):
        t = dot(w_ref[...], n_ref[c].reshape(TOKENS, EMBED), 0, 1).astype(bf16)
        for z in range(Z):
            a, b = chunk_pieces(z)[0][0], shared_head(z)
            q_ref[2 * z + c, 0:FULL, :] = t[a : a + FULL]
            q_ref[2 * z + c, FULL:, :] = t[b : b + FULL]


def query_chunks(n, w):
    return pl.pallas_call(
        query_kernel,
        out_shape=jax.ShapeDtypeStruct((2 * Z, 2 * FULL, TOKENS), bf16),
        in_specs=[VMEM] * 2,
        out_specs=VMEM,
        compiler_params=PARAMS,
        cost_estimate=PROJECTION,
    )(n, w)


def value_kernel(n_ref, w_ref, v_ref):
    t = dot(w_ref[...], n_ref[...].reshape(ROWS * RES, EMBED), 0, 1).astype(bf16)
    for z in range(Z):
        (a, na), (b, nb) = chunk_pieces(z)
        v_ref[z, 0:FULL, :] = t[a : a + na]
        v_ref[z, FULL:CHUNK, :] = t[b : b + nb]


def value_chunks(n, w):
    return pl.pallas_call(
        value_kernel,
        out_shape=jax.ShapeDtypeStruct((Z, CHUNK, ROWS * RES), bf16),
        in_specs=[VMEM, VMEM],
        out_specs=VMEM,
        compiler_params=PARAMS,
        cost_estimate=PROJECTION,
    )(n, w)


def lay_keys(own, other, kf, kh):
    for cr, ref in enumerate((own, other)):
        for r in range(ROWS):
            n = (cr * ROWS + r) * FULL
            whole = [ref[z, 0:FULL, h * TOKENS + r * SUB : h * TOKENS + (r + 1) * SUB] for z in range(Z) for h in range(2)]
            kf[n : n + FULL, :] = jnp.concatenate(whole, axis=1)
            for d in range(2):
                first = d * TOKENS + r * SUB
                shared = [ref[z, FULL:CHUNK, first : first + SUB] for z in range(Z)]
                kh[n + d * HALF : n + (d + 1) * HALF, :] = jnp.concatenate(shared, axis=1)


def keys_kernel(own, other, kf, kh, a, b, sems):
    for copy in fetches((own, other), (a, b), sems):
        copy.wait()
    lay_keys(a, b, kf, kh)


def keys_laid(own, other):
    return pl.pallas_call(
        keys_kernel,
        out_shape=tuple(jax.ShapeDtypeStruct(s, bf16) for s in KEY_SHAPES),
        in_specs=[ANY, ANY],
        out_specs=(VMEM,) * 2,
        scratch_shapes=[pltpu.VMEM(own.shape, bf16)] * 2 + [pltpu.SemaphoreType.DMA((2,))],
        compiler_params=PARAMS,
        cost_estimate=LAYOUT,
    )(own, other)


def score_kernel(me_ref, *refs):
    sources, results, rest = refs[:5], refs[5:9], refs[9:]
    outs, (qf, qh, kf1, kh1), sems = rest[5], rest[6:10], rest[10]
    own, other, q_ref, kf0, kh0 = rest[:5]
    copies = fetches(sources, rest[:5], sems)
    for copy in copies[:2]:
        copy.wait()
    lay_keys(own, other, kf1, kh1)
    for copy in copies[2:]:
        copy.wait()
    peers = [jnp.bitwise_xor(me_ref[0], 2 * s + t) for s in range(4) for t in range(2)]
    for cr in range(2):
        c = jnp.bitwise_xor(me_ref[1], cr)
        queries = [q_ref[2 * p + c] for p in peers]
        for r in range(ROWS):
            n = (cr * ROWS + r) * FULL
            t = jnp.concatenate([b[:, r * SUB : (r + 1) * SUB] for b in queries], axis=1)
            qf[n : n + FULL, :] = t[:FULL]
            qh[n : n + FULL, :] = t[FULL:]
    first = 0
    for a, b in ((qf, kf0), (qf, kf1), (qh, kh0), (qh, kh1)):
        t = dot(a[...], b[...], 0, 0)
        for p in range(PEERS):
            outs[p // 2, p % 2, :, first : first + t.shape[1]] = t[p * SUB : (p + 1) * SUB]
        first += t.shape[1]
    for copy in fetches([outs.at[s] for s in range(4)], results, sems):
        copy.wait()


def score(me, q, laid, own, other):
    rows = 2 * ROWS * FULL
    return pl.pallas_call(
        score_kernel,
        out_shape=(pltpu.HBM((2, SUB, LOGITS), f32),) * 4,
        in_specs=[SMEM] + [ANY] * 5,
        out_specs=(HBM,) * 4,
        scratch_shapes=[pltpu.VMEM(a.shape, bf16) for a in (own, other, q, *laid)]
        + [pltpu.VMEM((4, 2, SUB, LOGITS), f32)]
        + [pltpu.VMEM((rows, QUERIES), bf16)] * 2
        + [pltpu.VMEM(s, bf16) for s in KEY_SHAPES]
        + [pltpu.SemaphoreType.DMA((5,))],
        compiler_params=WIDE,
    )(me, own, other, q, *laid)


def total_kernel(p0, p1, p2, p3, own, shared, give, give_shared):
    t = p0[...] + p1[...] + (p2[...] + p3[...])
    own[...] = t[0]
    shared[...] = t[0, :, KEYS:]
    give[...] = t[1]
    give_shared[...] = t[1, :, KEYS:]


def total(parts):
    return pl.pallas_call(
        total_kernel,
        out_shape=tuple(jax.ShapeDtypeStruct((SUB, n), f32) for n in (LOGITS, KEYS // 2) * 2),
        in_specs=[VMEM] * 4,
        out_specs=(VMEM,) * 4,
        compiler_params=PARAMS,
    )(*parts)


def softmax_kernel(factor, own, got, near, far, out):
    whole = (own[...] + got[...]) * factor
    shared = jnp.concatenate([whole[:, KEYS:], (near[...] + far[...]) * factor], axis=1)
    for i, logits in enumerate((whole[:, :KEYS], shared)):
        powered = jnp.exp(logits - jnp.max(logits, axis=-1, keepdims=True))
        probs = (powered / jnp.sum(powered, axis=-1, keepdims=True)).astype(bf16)
        for p in range(PEERS):
            out[p, i] = probs


def softmax(factor, *parts):
    return pl.pallas_call(
        functools.partial(softmax_kernel, factor),
        out_shape=jax.ShapeDtypeStruct((PEERS, 2, SUB, KEYS), bf16),
        in_specs=[VMEM] * 4,
        out_specs=VMEM,
        compiler_params=PARAMS,
    )(*parts)


def values_kernel(me_ref, *refs):
    (vf, vh), (v00, v01, v10, v11), sems = refs[4:6], refs[6:10], refs[10]
    for copy in fetches(refs[:4], refs[6:10], sems):
        copy.wait()
    odd = lax.rem(me_ref[2], 2)
    for cr, refs in enumerate(((v00, v01), (v10, v11))):
        halves = [
            ref[i, FULL:CHUNK, pl.ds(pl.multiple_of(h * TOKENS, TOKENS), TOKENS)]
            for h in (odd, 1 - odd)
            for ref in refs
            for i in range(Z)
        ]
        whole = [ref[i, 0:FULL, h * TOKENS : (h + 1) * TOKENS] for ref in refs for i in range(Z) for h in range(2)]
        for r in range(ROWS):
            n = cr * ROWS + r
            lanes = slice(r * SUB, (r + 1) * SUB)
            vf[n * FULL : (n + 1) * FULL, :] = jnp.concatenate([b[:, lanes] for b in whole], axis=1)
            vh[n * HALF : (n + 1) * HALF, :] = jnp.concatenate([b[:, lanes] for b in halves], axis=1)


def values_laid(me, vs):
    return pl.pallas_call(
        values_kernel,
        out_shape=tuple(jax.ShapeDtypeStruct((2 * ROWS * n, KEYS), bf16) for n in (FULL, HALF)),
        in_specs=[SMEM] + [ANY] * 4,
        out_specs=(VMEM,) * 2,
        scratch_shapes=[pltpu.VMEM(v.shape, bf16) for v in vs] + [pltpu.SemaphoreType.DMA((4,))],
        compiler_params=WIDE,
        cost_estimate=LAYOUT,
    )(me, *vs)


def mix_kernel(me_ref, p_hbm, vf_hbm, vh_hbm, o_ref, p_ref, vf, vh, sems):
    core = me_ref[1]
    copies = fetches((p_hbm, vf_hbm, vh_hbm), (p_ref, vf, vh), sems)
    copies[0].wait()
    for i, (v, first, n) in enumerate(((vf, 0, FULL), (vh, FULL, HALF))):
        copies[1 + i].wait()
        probs = p_ref[:, i].reshape(QUERIES, KEYS)
        for cr in range(2):
            c = jnp.bitwise_xor(core, cr)
            mixed = dot(v[cr * ROWS * n : (cr + 1) * ROWS * n, :], probs, 1, 1).astype(bf16)
            for s in range(PEERS):
                o_ref[2 * s + c, first : first + n, :] = jnp.concatenate(
                    [mixed[r * n : (r + 1) * n, s * SUB : (s + 1) * SUB] for r in range(ROWS)], axis=1
                )


def mix(me, laid, probs):
    return pl.pallas_call(
        mix_kernel,
        out_shape=jax.ShapeDtypeStruct((2 * Z, CHUNK, ROWS * SUB), bf16),
        in_specs=[SMEM] + [ANY] * 3,
        out_specs=VMEM,
        scratch_shapes=[pltpu.VMEM(a.shape, bf16) for a in (probs, *laid)] + [pltpu.SemaphoreType.DMA((3,))],
        compiler_params=WIDE,
    )(me, probs, *laid)


def final_kernel(m_ref, w_ref, o_ref, t_ref):
    for c in range(2):
        for z in range(Z):
            (a, na), (b, nb) = chunk_pieces(z)
            t_ref[a : a + na, :] = m_ref[2 * z + c, 0:FULL, :]
            t_ref[b : b + nb, :] = m_ref[2 * z + c, FULL:CHUNK, :]
        attended = dot(t_ref[...], w_ref[...], 0, 0).astype(bf16)
        o_ref[:, c * SUB : (c + 1) * SUB, :] = attended.reshape(ROWS, SUB, EMBED)


def final(m, w):
    return pl.pallas_call(
        final_kernel,
        out_shape=jax.ShapeDtypeStruct((ROWS, RES, EMBED), bf16),
        in_specs=[VMEM] * 2,
        out_specs=VMEM,
        scratch_shapes=[pltpu.VMEM((EMBED, ROWS * SUB), bf16)],
        compiler_params=PARAMS,
    )(m, w)


def flip(x, axes, n, s):
    return lax.ppermute(x, axes, [(i, i ^ s) for i in range(n)])


def gather4(own):
    far = flip(own, "xl", 2, 1)
    return own, far, flip(own, "c", 2, 1), flip(far, "c", 2, 1)


def local(x, wq, wk, wv, wf):
    me = jnp.stack([lax.axis_index(("y", "xh")), lax.axis_index("c"), lax.axis_index("z")])
    me = me.astype(jnp.int32)
    n, k = key_chunks(x, wk)
    q = query_chunks(n, wq)
    v = value_chunks(n, wv)
    k = lax.all_to_all(k, "z", 0, 0, tiled=True)
    q, k = lax.optimization_barrier((q, k))
    q = lax.all_to_all(q, ("z", "c"), 0, 0, tiled=True)
    k00, k01, k10, k11 = gather4(k)
    parts = score(me, q, keys_laid(k00, k10), k01, k11)
    v, kept = lax.optimization_barrier((v, parts[0]))
    parts = [kept] + [flip(parts[s], "y", 4, s) for s in range(1, 4)]
    v = lax.all_to_all(v, "z", 0, 0, tiled=True)
    own, shared, give, give_shared = total(parts)
    v, own = lax.optimization_barrier((v, own))
    vs = gather4(v)
    rows = ROWS * 2 * PEERS
    probs = softmax(
        1.0 / math.sqrt(DH * rows),
        own,
        flip(give, "xh", 2, 1),
        flip(shared, "z", Z, 1),
        flip(give_shared, ("xh", "z"), 2 * Z, Z + 1),
    )
    probs = lax.all_to_all(probs, ("y", "xh"), 0, 0, tiled=True)
    mixed = lax.all_to_all(mix(me, values_laid(me, vs), probs), ("z", "c"), 0, 0, tiled=True)
    return final(mixed, wf)


def solution(mesh):
    fine = Mesh(mesh.devices.reshape(4, 2, 2, 8, 2), ("y", "xh", "c", "z", "xl"))
    spec = P(("y", "xh", "c"), ("z", "xl"), None)
    return jax.shard_map(
        local,
        mesh=fine,
        in_specs=(spec, P(), P(), P(), P()),
        out_specs=spec,
        check_vma=False,
    )
```

```python
import functools
import math

import jax
import jax.numpy as jnp
from jax import lax
from jax.experimental import pallas as pl
from jax.experimental.pallas import tpu as pltpu
from jax.sharding import Mesh, PartitionSpec as P

H = 12
DH = 64
EMBED = 768
ROWS = 8
RES = 64
Z = 8
CHUNK = EMBED // Z
FULL = DH
HALF = CHUNK - DH
PEERS = 8
SUB = RES // 2
TOKENS = ROWS * SUB
QUERIES = Z * SUB
KEYS = 2 * Z * RES
LOGITS = KEYS + KEYS // 2

f32 = jnp.float32
bf16 = jnp.bfloat16
PARAMS = pltpu.CompilerParams(vmem_limit_bytes=8 * 1024 * 1024)
PROJECTION = pl.CostEstimate(
    flops=2 * ROWS * RES * EMBED * EMBED, bytes_accessed=2 * EMBED * (EMBED + 2 * ROWS * RES), transcendentals=0
)
LAYOUT = pl.CostEstimate(flops=0, bytes_accessed=16 * ROWS * RES * EMBED, transcendentals=0)
KEY_SHAPES = ((2 * ROWS * FULL, KEYS // 2), (2 * ROWS * FULL, KEYS // 4))
WIDE = pltpu.CompilerParams(vmem_limit_bytes=16 * 1024 * 1024)
VMEM = pl.BlockSpec(memory_space=pltpu.VMEM)
SMEM = pl.BlockSpec(memory_space=pltpu.SMEM)
ANY = pl.BlockSpec(memory_space=pl.ANY)
HBM = pl.BlockSpec(memory_space=pltpu.HBM)


def chunk_pieces(z):
    base = z * CHUNK
    if z % 2 == 0:
        return (base, FULL), (base + FULL, HALF)
    return (base + HALF, FULL), (base, HALF)


def dot(a, b, ca, cb):
    return lax.dot_general(a, b, (((ca,), (cb,)), ((), ())), preferred_element_type=f32)


def shared_head(z):
    return z // 2 * (2 * CHUNK) + FULL


def chunk_rows(z):
    odd = lax.rem(z, 2)
    base = z * CHUNK
    return pl.multiple_of(base + odd * HALF, HALF), pl.multiple_of(base + (1 - odd) * FULL, HALF)


def fetches(sources, buffers, sems):
    copies = [pltpu.make_async_copy(a, b, sems.at[i]) for i, (a, b) in enumerate(zip(sources, buffers))]
    for copy in copies:
        copy.start()
    return copies


def in_hbm(*arrays):
    return [pltpu.with_memory_space_constraint(a, pltpu.HBM) for a in arrays]


def key_kernel(me_ref, x_hbm, w_hbm, n_ref, *rest):
    outs, (x_ref, w_ref, t_ref, sems) = rest[:Z], rest[Z:]
    copy_x, copy_w = fetches((x_hbm, w_hbm), (x_ref, w_ref), sems)
    copy_x.wait()
    x = x_ref[...].astype(f32)
    centred = x - jnp.mean(x, axis=-1, keepdims=True)
    var = jnp.mean(centred * centred, axis=-1, keepdims=True)
    normed = (centred * lax.rsqrt(var + 1e-05)).astype(bf16)
    for h in range(2):
        n_ref[h] = normed[:, h * SUB : (h + 1) * SUB, :]
    copy_w.wait()
    t_ref[...] = dot(w_ref[...], n_ref[...].reshape(ROWS * RES, EMBED), 0, 1).astype(bf16)
    for s, out in enumerate(outs):
        z = lax.rem(me_ref[2] + s, Z)
        first, odd = shared_head(z), lax.rem(z, 2)
        lanes = pl.ds(pl.multiple_of(odd * TOKENS, TOKENS), TOKENS)
        out[0:FULL, :] = t_ref[pl.ds(chunk_rows(z)[0], FULL), :]
        for d in range(2):
            rows = pl.ds(pl.multiple_of(first + d * HALF, HALF), HALF)
            out[FULL:CHUNK, d * TOKENS : (d + 1) * TOKENS] = t_ref[rows, lanes]


def key_chunks(me, x, w):
    n, *k = pl.pallas_call(
        key_kernel,
        out_shape=(jax.ShapeDtypeStruct((2, ROWS, SUB, EMBED), bf16),)
        + (jax.ShapeDtypeStruct((CHUNK, ROWS * RES), bf16),) * Z,
        in_specs=[SMEM, ANY, ANY],
        out_specs=(VMEM,) * (1 + Z),
        scratch_shapes=[
            pltpu.VMEM((ROWS, RES, EMBED), bf16),
            pltpu.VMEM((EMBED, EMBED), bf16),
            pltpu.VMEM((EMBED, ROWS * RES), bf16),
            pltpu.SemaphoreType.DMA((2,)),
        ],
        compiler_params=PARAMS,
    )(me, *in_hbm(x, w))
    return n, k


def query_kernel(n_ref, w_ref, q_ref):
    for c in range(2):
        t = dot(w_ref[...], n_ref[c].reshape(TOKENS, EMBED), 0, 1).astype(bf16)
        for z in range(Z):
            a, b = chunk_pieces(z)[0][0], shared_head(z)
            q_ref[2 * z + c, 0:FULL, :] = t[a : a + FULL]
            q_ref[2 * z + c, FULL:, :] = t[b : b + FULL]


def query_chunks(n, w):
    return pl.pallas_call(
        query_kernel,
        out_shape=jax.ShapeDtypeStruct((2 * Z, 2 * FULL, TOKENS), bf16),
        in_specs=[VMEM] * 2,
        out_specs=VMEM,
        compiler_params=PARAMS,
        cost_estimate=PROJECTION,
    )(n, w)


def value_kernel(n_ref, w_ref, v_ref):
    t = dot(w_ref[...], n_ref[...].reshape(ROWS * RES, EMBED), 0, 1).astype(bf16)
    for z in range(Z):
        (a, na), (b, nb) = chunk_pieces(z)
        v_ref[z, 0:FULL, :] = t[a : a + na]
        v_ref[z, FULL:CHUNK, :] = t[b : b + nb]


def value_chunks(n, w):
    return pl.pallas_call(
        value_kernel,
        out_shape=jax.ShapeDtypeStruct((Z, CHUNK, ROWS * RES), bf16),
        in_specs=[VMEM, VMEM],
        out_specs=VMEM,
        compiler_params=PARAMS,
        cost_estimate=PROJECTION,
    )(n, w)


def lay_keys(me, own, other, kf, kh):
    where = [lax.rem(me - z + Z, Z) for z in range(Z)]
    for cr, ref in enumerate((own, other)):
        for r in range(ROWS):
            n = (cr * ROWS + r) * FULL
            whole = [ref[z, 0:FULL, h * TOKENS + r * SUB : h * TOKENS + (r + 1) * SUB] for z in where for h in range(2)]
            kf[n : n + FULL, :] = jnp.concatenate(whole, axis=1)
            for d in range(2):
                first = d * TOKENS + r * SUB
                shared = [ref[z, FULL:CHUNK, first : first + SUB] for z in where]
                kh[n + d * HALF : n + (d + 1) * HALF, :] = jnp.concatenate(shared, axis=1)


def keys_kernel(me_ref, own, other, kf, kh, a, b, sems):
    for copy in fetches((own, other), (a, b), sems):
        copy.wait()
    lay_keys(me_ref[2], a, b, kf, kh)


def keys_laid(me, own, other):
    return pl.pallas_call(
        keys_kernel,
        out_shape=tuple(jax.ShapeDtypeStruct(s, bf16) for s in KEY_SHAPES),
        in_specs=[SMEM, ANY, ANY],
        out_specs=(VMEM,) * 2,
        scratch_shapes=[pltpu.VMEM(own.shape, bf16)] * 2 + [pltpu.SemaphoreType.DMA((2,))],
        compiler_params=PARAMS,
        cost_estimate=LAYOUT,
    )(me, own, other)


def score_kernel(me_ref, *refs):
    sources, results, rest = refs[:5], refs[5:9], refs[9:]
    outs, (qf, qh, kf1, kh1), sems = rest[5], rest[6:10], rest[10]
    own, other, q_ref, kf0, kh0 = rest[:5]
    copies = fetches(sources, rest[:5], sems)
    for copy in copies[:2]:
        copy.wait()
    lay_keys(me_ref[2], own, other, kf1, kh1)
    for copy in copies[2:]:
        copy.wait()
    peers = [jnp.bitwise_xor(me_ref[0], 2 * s + t) for s in range(4) for t in range(2)]
    for cr in range(2):
        c = jnp.bitwise_xor(me_ref[1], cr)
        queries = [q_ref[2 * p + c] for p in peers]
        for r in range(ROWS):
            n = (cr * ROWS + r) * FULL
            t = jnp.concatenate([b[:, r * SUB : (r + 1) * SUB] for b in queries], axis=1)
            qf[n : n + FULL, :] = t[:FULL]
            qh[n : n + FULL, :] = t[FULL:]
    first = 0
    for a, b in ((qf, kf0), (qf, kf1), (qh, kh0), (qh, kh1)):
        t = dot(a[...], b[...], 0, 0)
        for p in range(PEERS):
            outs[p // 2, p % 2, :, first : first + t.shape[1]] = t[p * SUB : (p + 1) * SUB]
        first += t.shape[1]
    for copy in fetches([outs.at[s] for s in range(4)], results, sems):
        copy.wait()


def score(me, q, laid, own, other):
    rows = 2 * ROWS * FULL
    return pl.pallas_call(
        score_kernel,
        out_shape=(pltpu.HBM((2, SUB, LOGITS), f32),) * 4,
        in_specs=[SMEM] + [ANY] * 5,
        out_specs=(HBM,) * 4,
        scratch_shapes=[pltpu.VMEM(a.shape, bf16) for a in (own, other, q, *laid)]
        + [pltpu.VMEM((4, 2, SUB, LOGITS), f32)]
        + [pltpu.VMEM((rows, QUERIES), bf16)] * 2
        + [pltpu.VMEM(s, bf16) for s in KEY_SHAPES]
        + [pltpu.SemaphoreType.DMA((5,))],
        compiler_params=WIDE,
    )(me, own, other, q, *laid)


def total_kernel(p0, p1, p2, p3, own, shared, give, give_shared):
    t = p0[...] + p1[...] + (p2[...] + p3[...])
    own[...] = t[0]
    shared[...] = t[0, :, KEYS:]
    give[...] = t[1]
    give_shared[...] = t[1, :, KEYS:]


def total(parts):
    return pl.pallas_call(
        total_kernel,
        out_shape=tuple(jax.ShapeDtypeStruct((SUB, n), f32) for n in (LOGITS, KEYS // 2) * 2),
        in_specs=[VMEM] * 4,
        out_specs=(VMEM,) * 4,
        compiler_params=PARAMS,
    )(*parts)


def softmax_kernel(factor, own, got, near, far, out):
    whole = (own[...] + got[...]) * factor
    shared = jnp.concatenate([whole[:, KEYS:], (near[...] + far[...]) * factor], axis=1)
    for i, logits in enumerate((whole[:, :KEYS], shared)):
        powered = jnp.exp(logits - jnp.max(logits, axis=-1, keepdims=True))
        probs = (powered / jnp.sum(powered, axis=-1, keepdims=True)).astype(bf16)
        for p in range(PEERS):
            out[p, i] = probs


def softmax(factor, *parts):
    return pl.pallas_call(
        functools.partial(softmax_kernel, factor),
        out_shape=jax.ShapeDtypeStruct((PEERS, 2, SUB, KEYS), bf16),
        in_specs=[VMEM] * 4,
        out_specs=VMEM,
        compiler_params=PARAMS,
    )(*parts)


def values_kernel(me_ref, own_hbm, far_hbm, vf, vh, own, far, sems):
    for copy in fetches((own_hbm, far_hbm), (own, far), sems):
        copy.wait()
    odd = lax.rem(me_ref[2], 2)
    halves = [
        ref[z, FULL:CHUNK, pl.ds(pl.multiple_of(h * TOKENS, TOKENS), TOKENS)]
        for h in (odd, 1 - odd)
        for ref in (own, far)
        for z in range(Z)
    ]
    whole = [ref[z, 0:FULL, h * TOKENS : (h + 1) * TOKENS] for ref in (own, far) for z in range(Z) for h in range(2)]
    for r in range(ROWS):
        lanes = slice(r * SUB, (r + 1) * SUB)
        vf[r * FULL : (r + 1) * FULL, :] = jnp.concatenate([b[:, lanes] for b in whole], axis=1)
        vh[r * HALF : (r + 1) * HALF, :] = jnp.concatenate([b[:, lanes] for b in halves], axis=1)


def values_laid(me, own, far):
    return pl.pallas_call(
        values_kernel,
        out_shape=tuple(jax.ShapeDtypeStruct((ROWS * n, KEYS), bf16) for n in (FULL, HALF)),
        in_specs=[SMEM] + [ANY] * 2,
        out_specs=(VMEM,) * 2,
        scratch_shapes=[pltpu.VMEM(own.shape, bf16)] * 2 + [pltpu.SemaphoreType.DMA((2,))],
        compiler_params=WIDE,
        cost_estimate=LAYOUT,
    )(me, own, far)


def mix_kernel(me_ref, own_hbm, other_hbm, vf_hbm, vh_hbm, *rest):
    outs, (p_ref, vf, vh, sems) = rest[:Z], rest[Z:]
    core, z = me_ref[1], me_ref[2]
    copies = fetches(
        (own_hbm, other_hbm, vf_hbm, vh_hbm), (p_ref.at[core], p_ref.at[1 - core], vf, vh), sems
    )
    for copy in copies:
        copy.wait()
    for i, (v, first, n) in enumerate(((vf, 0, FULL), (vh, FULL, HALF))):
        for h in range(2):
            probs = jnp.concatenate([p_ref[h, lax.rem(z + s, Z), i] for s in range(Z)], axis=0)
            mixed = dot(v[...], probs, 1, 1).astype(bf16)
            for s, out in enumerate(outs):
                out[first : first + n, h * TOKENS : (h + 1) * TOKENS] = jnp.concatenate(
                    [mixed[r * n : (r + 1) * n, s * SUB : (s + 1) * SUB] for r in range(ROWS)], axis=1
                )


def mix(me, laid, own, other):
    return pl.pallas_call(
        mix_kernel,
        out_shape=(jax.ShapeDtypeStruct((CHUNK, ROWS * RES), bf16),) * Z,
        in_specs=[SMEM] + [ANY] * 4,
        out_specs=(VMEM,) * Z,
        scratch_shapes=[pltpu.VMEM((2, *own.shape), bf16)]
        + [pltpu.VMEM(a.shape, bf16) for a in laid]
        + [pltpu.SemaphoreType.DMA((4,))],
        compiler_params=WIDE,
    )(me, own, other, *laid)


def final_kernel(me_ref, *refs):
    pieces, w_ref, o_ref, t_ref = refs[:Z], refs[Z], refs[Z + 1], refs[Z + 2]
    for s, piece in enumerate(pieces):
        full, half = chunk_rows(lax.rem(me_ref[2] - s + Z, Z))
        t_ref[pl.ds(full, FULL), :] = piece[0:FULL, :]
        t_ref[pl.ds(half, HALF), :] = piece[FULL:CHUNK, :]
    for h in range(2):
        attended = dot(t_ref[:, h * TOKENS : (h + 1) * TOKENS], w_ref[...], 0, 0).astype(bf16)
        o_ref[:, h * SUB : (h + 1) * SUB, :] = attended.reshape(ROWS, SUB, EMBED)


def final(me, pieces, w):
    return pl.pallas_call(
        final_kernel,
        out_shape=jax.ShapeDtypeStruct((ROWS, RES, EMBED), bf16),
        in_specs=[SMEM] + [VMEM] * (Z + 1),
        out_specs=VMEM,
        scratch_shapes=[pltpu.VMEM((EMBED, ROWS * RES), bf16)],
        compiler_params=PARAMS,
    )(me, *pieces, w)


def flip(x, axes, n, s):
    return lax.ppermute(x, axes, [(i, i ^ s) for i in range(n)])


def gather4(own):
    far = flip(own, "xl", 2, 1)
    return own, far, flip(own, "c", 2, 1), flip(far, "c", 2, 1)


def spread(pieces):
    got = {0: pieces[0]}
    for s in (1, 7, 2, 6, 3, 5, 4):
        got[s] = lax.ppermute(pieces[s], "z", [(i, (i + s) % Z) for i in range(Z)])
    return [got[s] for s in range(Z)]


def local(x, wq, wk, wv, wf):
    me = jnp.stack([lax.axis_index(("y", "xh")), lax.axis_index("c"), lax.axis_index("z")])
    me = me.astype(jnp.int32)
    n, k = key_chunks(me, x, wk)
    q = query_chunks(n, wq)
    v = value_chunks(n, wv)
    k = jnp.stack(spread(k))
    q, v, k = lax.optimization_barrier((q, v, k))
    q = lax.all_to_all(q, ("z", "c"), 0, 0, tiled=True)
    k00, k01, k10, k11 = gather4(k)
    parts = score(me, q, keys_laid(me, k00, k10), k01, k11)
    v, kept = lax.optimization_barrier((v, parts[0]))
    parts = [kept] + [flip(parts[s], "y", 4, s) for s in range(1, 4)]
    v = lax.all_to_all(v, "z", 0, 0, tiled=True)
    own, shared, give, give_shared = total(parts)
    got = flip(give, "xh", 2, 1)
    near = flip(shared, "z", Z, 1)
    far = flip(give_shared, ("xh", "z"), 2 * Z, Z + 1)
    v, got = lax.optimization_barrier((v, got))
    whole, shared = values_laid(me, v, flip(v, "xl", 2, 1))
    probs = softmax(1.0 / math.sqrt(DH * ROWS * 2 * PEERS), own, got, near, far)
    probs = lax.all_to_all(probs, ("y", "xh"), 0, 0, tiled=True)
    shared, probs = lax.optimization_barrier((shared, probs))
    return final(me, spread(mix(me, (whole, shared), probs, flip(probs, "c", 2, 1))), wf)


def solution(mesh):
    fine = Mesh(mesh.devices.reshape(4, 2, 2, 8, 2), ("y", "xh", "c", "z", "xl"))
    spec = P(("y", "xh", "c"), ("z", "xl"), None)
    return jax.shard_map(
        local,
        mesh=fine,
        in_specs=(spec, P(), P(), P(), P()),
        out_specs=spec,
        check_vma=False,
    )
```

```python
import functools
import math

import jax
import jax.numpy as jnp
from jax import lax
from jax.experimental import pallas as pl
from jax.experimental.pallas import tpu as pltpu
from jax.sharding import Mesh, PartitionSpec as P

H = 12
DH = 64
EMBED = 768
ROWS = 8
RES = 64
Z = 8
CHUNK = EMBED // Z
FULL = DH
HALF = CHUNK - DH
PEERS = 8
SUB = RES // 2
TOKENS = ROWS * SUB
QUERIES = Z * SUB
KEYS = 2 * Z * RES
LOGITS = KEYS + KEYS // 2

f32 = jnp.float32
bf16 = jnp.bfloat16
PARAMS = pltpu.CompilerParams(vmem_limit_bytes=8 * 1024 * 1024)
PROJECTION = pl.CostEstimate(
    flops=2 * ROWS * RES * EMBED * EMBED, bytes_accessed=2 * EMBED * (EMBED + 2 * ROWS * RES), transcendentals=0
)
LAYOUT = pl.CostEstimate(flops=0, bytes_accessed=16 * ROWS * RES * EMBED, transcendentals=0)
KEY_SHAPES = ((2 * ROWS * FULL, KEYS // 2), (2 * ROWS * FULL, KEYS // 4))
WIDE = pltpu.CompilerParams(vmem_limit_bytes=16 * 1024 * 1024)
VMEM = pl.BlockSpec(memory_space=pltpu.VMEM)
SMEM = pl.BlockSpec(memory_space=pltpu.SMEM)
ANY = pl.BlockSpec(memory_space=pl.ANY)


def chunk_pieces(z):
    base = z * CHUNK
    if z % 2 == 0:
        return (base, FULL), (base + FULL, HALF)
    return (base + HALF, FULL), (base, HALF)


def dot(a, b, ca, cb):
    return lax.dot_general(a, b, (((ca,), (cb,)), ((), ())), preferred_element_type=f32)


def shared_head(z):
    return z // 2 * (2 * CHUNK) + FULL


def chunk_rows(z):
    odd = lax.rem(z, 2)
    base = z * CHUNK
    return pl.multiple_of(base + odd * HALF, HALF), pl.multiple_of(base + (1 - odd) * FULL, HALF)


def fetches(sources, buffers, sems):
    copies = [pltpu.make_async_copy(a, b, sems.at[i]) for i, (a, b) in enumerate(zip(sources, buffers))]
    for copy in copies:
        copy.start()
    return copies


def in_hbm(*arrays):
    return [pltpu.with_memory_space_constraint(a, pltpu.HBM) for a in arrays]


def key_kernel(me_ref, x_hbm, w_hbm, n_ref, *rest):
    outs, (x_ref, w_ref, t_ref, sems) = rest[:Z], rest[Z:]
    copy_x, copy_w = fetches((x_hbm, w_hbm), (x_ref, w_ref), sems)
    copy_x.wait()
    x = x_ref[...].astype(f32)
    centred = x - jnp.mean(x, axis=-1, keepdims=True)
    var = jnp.mean(centred * centred, axis=-1, keepdims=True)
    normed = (centred * lax.rsqrt(var + 1e-05)).astype(bf16)
    for h in range(2):
        n_ref[h] = normed[:, h * SUB : (h + 1) * SUB, :]
    copy_w.wait()
    t_ref[...] = dot(w_ref[...], n_ref[...].reshape(ROWS * RES, EMBED), 0, 1).astype(bf16)
    for s, out in enumerate(outs):
        z = lax.rem(me_ref[2] + s, Z)
        first, odd = shared_head(z), lax.rem(z, 2)
        lanes = pl.ds(pl.multiple_of(odd * TOKENS, TOKENS), TOKENS)
        out[0:FULL, :] = t_ref[pl.ds(chunk_rows(z)[0], FULL), :]
        for d in range(2):
            rows = pl.ds(pl.multiple_of(first + d * HALF, HALF), HALF)
            out[FULL:CHUNK, d * TOKENS : (d + 1) * TOKENS] = t_ref[rows, lanes]


def key_chunks(me, x, w):
    n, *k = pl.pallas_call(
        key_kernel,
        out_shape=(jax.ShapeDtypeStruct((2, ROWS, SUB, EMBED), bf16),)
        + (jax.ShapeDtypeStruct((CHUNK, ROWS * RES), bf16),) * Z,
        in_specs=[SMEM, ANY, ANY],
        out_specs=(VMEM,) * (1 + Z),
        scratch_shapes=[
            pltpu.VMEM((ROWS, RES, EMBED), bf16),
            pltpu.VMEM((EMBED, EMBED), bf16),
            pltpu.VMEM((EMBED, ROWS * RES), bf16),
            pltpu.SemaphoreType.DMA((2,)),
        ],
        compiler_params=PARAMS,
    )(me, *in_hbm(x, w))
    return n, k


def query_kernel(n_ref, w_ref, q_ref):
    for c in range(2):
        t = dot(w_ref[...], n_ref[c].reshape(TOKENS, EMBED), 0, 1).astype(bf16)
        for z in range(Z):
            a, b = chunk_pieces(z)[0][0], shared_head(z)
            q_ref[2 * z + c, 0:FULL, :] = t[a : a + FULL]
            q_ref[2 * z + c, FULL:, :] = t[b : b + FULL]


def query_chunks(n, w):
    return pl.pallas_call(
        query_kernel,
        out_shape=jax.ShapeDtypeStruct((2 * Z, 2 * FULL, TOKENS), bf16),
        in_specs=[VMEM] * 2,
        out_specs=VMEM,
        compiler_params=PARAMS,
        cost_estimate=PROJECTION,
    )(n, w)


def value_kernel(me_ref, n_ref, w_ref, *rest):
    outs, t_ref = rest[:Z], rest[Z]
    t_ref[...] = dot(w_ref[...], n_ref[...].reshape(ROWS * RES, EMBED), 0, 1).astype(bf16)
    for s, out in enumerate(outs):
        full, half = chunk_rows(lax.rem(me_ref[2] + s, Z))
        out[0:FULL, :] = t_ref[pl.ds(full, FULL), :]
        out[FULL:CHUNK, :] = t_ref[pl.ds(half, HALF), :]


def value_chunks(me, n, w):
    return pl.pallas_call(
        value_kernel,
        out_shape=(jax.ShapeDtypeStruct((CHUNK, ROWS * RES), bf16),) * Z,
        in_specs=[SMEM, VMEM, VMEM],
        out_specs=(VMEM,) * Z,
        scratch_shapes=[pltpu.VMEM((EMBED, ROWS * RES), bf16)],
        compiler_params=PARAMS,
        cost_estimate=PROJECTION,
    )(me, n, w)


def lay_keys(me, own, other, kf, kh):
    where = [lax.rem(me - z + Z, Z) for z in range(Z)]
    for cr, ref in enumerate((own, other)):
        for r in range(ROWS):
            n = (cr * ROWS + r) * FULL
            whole = [ref[z, 0:FULL, h * TOKENS + r * SUB : h * TOKENS + (r + 1) * SUB] for z in where for h in range(2)]
            kf[n : n + FULL, :] = jnp.concatenate(whole, axis=1)
            for d in range(2):
                first = d * TOKENS + r * SUB
                shared = [ref[z, FULL:CHUNK, first : first + SUB] for z in where]
                kh[n + d * HALF : n + (d + 1) * HALF, :] = jnp.concatenate(shared, axis=1)


def keys_kernel(me_ref, own, other, kf, kh, a, b, sems):
    for copy in fetches((own, other), (a, b), sems):
        copy.wait()
    lay_keys(me_ref[2], a, b, kf, kh)


def keys_laid(me, own, other):
    return pl.pallas_call(
        keys_kernel,
        out_shape=tuple(jax.ShapeDtypeStruct(s, bf16) for s in KEY_SHAPES),
        in_specs=[SMEM, ANY, ANY],
        out_specs=(VMEM,) * 2,
        scratch_shapes=[pltpu.VMEM(own.shape, bf16)] * 2 + [pltpu.SemaphoreType.DMA((2,))],
        compiler_params=PARAMS,
        cost_estimate=LAYOUT,
    )(me, own, other)


def score_kernel(me_ref, *refs):
    sources, outs, rest = refs[:5], refs[5:9], refs[9:]
    (qf, qh, kf1, kh1), sems = rest[5:9], rest[9]
    own, other, q_ref, kf0, kh0 = rest[:5]
    copies = fetches(sources, rest[:5], sems)
    for copy in copies[:2]:
        copy.wait()
    lay_keys(me_ref[2], own, other, kf1, kh1)
    for copy in copies[2:]:
        copy.wait()
    peers = [jnp.bitwise_xor(me_ref[0], 2 * s + t) for s in range(4) for t in range(2)]
    for cr in range(2):
        c = jnp.bitwise_xor(me_ref[1], cr)
        queries = [q_ref[2 * p + c] for p in peers]
        for r in range(ROWS):
            n = (cr * ROWS + r) * FULL
            t = jnp.concatenate([b[:, r * SUB : (r + 1) * SUB] for b in queries], axis=1)
            qf[n : n + FULL, :] = t[:FULL]
            qh[n : n + FULL, :] = t[FULL:]
    first = 0
    for a, b in ((qf, kf0), (qf, kf1), (qh, kh0), (qh, kh1)):
        t = dot(a[...], b[...], 0, 0)
        for p in range(PEERS):
            outs[p // 2][p % 2, :, first : first + t.shape[1]] = t[p * SUB : (p + 1) * SUB]
        first += t.shape[1]


def score(me, q, laid, own, other):
    rows = 2 * ROWS * FULL
    return pl.pallas_call(
        score_kernel,
        out_shape=(jax.ShapeDtypeStruct((2, SUB, LOGITS), f32),) * 4,
        in_specs=[SMEM] + [ANY] * 5,
        out_specs=(VMEM,) * 4,
        scratch_shapes=[pltpu.VMEM(a.shape, bf16) for a in (own, other, q, *laid)]
        + [pltpu.VMEM((rows, QUERIES), bf16)] * 2
        + [pltpu.VMEM(s, bf16) for s in KEY_SHAPES]
        + [pltpu.SemaphoreType.DMA((5,))],
        compiler_params=WIDE,
    )(me, own, other, q, *laid)


def total_kernel(p0, p1, p2, p3, own, shared, give, give_shared):
    t = p0[...] + p1[...] + (p2[...] + p3[...])
    own[...] = t[0]
    shared[...] = t[0, :, KEYS:]
    give[...] = t[1]
    give_shared[...] = t[1, :, KEYS:]


def total(parts):
    return pl.pallas_call(
        total_kernel,
        out_shape=tuple(jax.ShapeDtypeStruct((SUB, n), f32) for n in (LOGITS, KEYS // 2) * 2),
        in_specs=[VMEM] * 4,
        out_specs=(VMEM,) * 4,
        compiler_params=PARAMS,
    )(*parts)


def softmax_kernel(factor, own, got, near, far, out):
    whole = (own[...] + got[...]) * factor
    shared = jnp.concatenate([whole[:, KEYS:], (near[...] + far[...]) * factor], axis=1)
    for i, logits in enumerate((whole[:, :KEYS], shared)):
        powered = jnp.exp(logits - jnp.max(logits, axis=-1, keepdims=True))
        probs = (powered / jnp.sum(powered, axis=-1, keepdims=True)).astype(bf16)
        for p in range(PEERS):
            out[p, i] = probs


def softmax(factor, *parts):
    return pl.pallas_call(
        functools.partial(softmax_kernel, factor),
        out_shape=jax.ShapeDtypeStruct((PEERS, 2, SUB, KEYS), bf16),
        in_specs=[VMEM] * 4,
        out_specs=VMEM,
        compiler_params=PARAMS,
    )(*parts)


def values_kernel(me_ref, v_hbm, vf, vh, v, sems):
    fetches((v_hbm,), (v,), sems)[0].wait()
    z = me_ref[2]
    odd = lax.rem(z, 2)
    where = [lax.rem(z - source + Z, Z) for source in range(Z)]
    halves = [
        v[i, FULL:CHUNK, pl.ds(pl.multiple_of(h * TOKENS, TOKENS), TOKENS)] for h in (odd, 1 - odd) for i in where
    ]
    whole = [v[i, 0:FULL, h * TOKENS : (h + 1) * TOKENS] for i in where for h in range(2)]
    for r in range(ROWS):
        lanes = slice(r * SUB, (r + 1) * SUB)
        vf[r * FULL : (r + 1) * FULL, :] = jnp.concatenate([b[:, lanes] for b in whole], axis=1)
        vh[r * HALF : (r + 1) * HALF, :] = jnp.concatenate([b[:, lanes] for b in halves], axis=1)


def values_laid(me, v):
    return pl.pallas_call(
        values_kernel,
        out_shape=tuple(jax.ShapeDtypeStruct((ROWS * n, KEYS // 2), bf16) for n in (FULL, HALF)),
        in_specs=[SMEM, ANY],
        out_specs=(VMEM,) * 2,
        scratch_shapes=[pltpu.VMEM(v.shape, bf16), pltpu.SemaphoreType.DMA((1,))],
        compiler_params=PARAMS,
        cost_estimate=LAYOUT,
    )(me, v)


def mix_kernel(me_ref, own_hbm, other_hbm, *rest):
    laid, outs, (p_ref, vf0, vh0, vf1, vh1, sems) = rest[:4], rest[4 : 4 + Z], rest[4 + Z :]
    core, z = me_ref[1], me_ref[2]
    copies = fetches(
        (own_hbm, other_hbm, *laid), (p_ref.at[core], p_ref.at[1 - core], vf0, vh0, vf1, vh1), sems
    )
    for copy in copies:
        copy.wait()
    quarter = KEYS // 4
    for i, (near, far, first, n) in enumerate(((vf0, vf1, 0, FULL), (vh0, vh1, FULL, HALF))):
        for h in range(2):
            probs = jnp.concatenate([p_ref[h, lax.rem(z + s, Z), i] for s in range(Z)], axis=0)
            quarters = [probs[:, k * quarter : (k + 1) * quarter] for k in range(4)]
            a, b = (quarters[:2], quarters[2:]) if i == 0 else (quarters[::2], quarters[1::2])
            mixed = dot(near[...], jnp.concatenate(a, axis=1), 1, 1) + dot(far[...], jnp.concatenate(b, axis=1), 1, 1)
            mixed = mixed.astype(bf16)
            for s, out in enumerate(outs):
                out[first : first + n, h * TOKENS : (h + 1) * TOKENS] = jnp.concatenate(
                    [mixed[r * n : (r + 1) * n, s * SUB : (s + 1) * SUB] for r in range(ROWS)], axis=1
                )


def mix(me, laid, own, other):
    return pl.pallas_call(
        mix_kernel,
        out_shape=(jax.ShapeDtypeStruct((CHUNK, ROWS * RES), bf16),) * Z,
        in_specs=[SMEM] + [ANY] * 6,
        out_specs=(VMEM,) * Z,
        scratch_shapes=[pltpu.VMEM((2, *own.shape), bf16)]
        + [pltpu.VMEM(a.shape, bf16) for a in laid]
        + [pltpu.SemaphoreType.DMA((6,))],
        compiler_params=WIDE,
    )(me, own, other, *laid)


def final_kernel(me_ref, *refs):
    pieces, w_ref, o_ref, t_ref = refs[:Z], refs[Z], refs[Z + 1], refs[Z + 2]
    for s, piece in enumerate(pieces):
        full, half = chunk_rows(lax.rem(me_ref[2] - s + Z, Z))
        t_ref[pl.ds(full, FULL), :] = piece[0:FULL, :]
        t_ref[pl.ds(half, HALF), :] = piece[FULL:CHUNK, :]
    for h in range(2):
        attended = dot(t_ref[:, h * TOKENS : (h + 1) * TOKENS], w_ref[...], 0, 0).astype(bf16)
        o_ref[:, h * SUB : (h + 1) * SUB, :] = attended.reshape(ROWS, SUB, EMBED)


def final(me, pieces, w):
    return pl.pallas_call(
        final_kernel,
        out_shape=jax.ShapeDtypeStruct((ROWS, RES, EMBED), bf16),
        in_specs=[SMEM] + [VMEM] * (Z + 1),
        out_specs=VMEM,
        scratch_shapes=[pltpu.VMEM((EMBED, ROWS * RES), bf16)],
        compiler_params=PARAMS,
    )(me, *pieces, w)


def flip(x, axes, n, s):
    return lax.ppermute(x, axes, [(i, i ^ s) for i in range(n)])


def gather4(own):
    far = flip(own, "xl", 2, 1)
    return own, far, flip(own, "c", 2, 1), flip(far, "c", 2, 1)


def spread(pieces):
    got = {0: pieces[0]}
    for s in (1, 7, 2, 6, 3, 5, 4):
        got[s] = lax.ppermute(pieces[s], "z", [(i, (i + s) % Z) for i in range(Z)])
    return [got[s] for s in range(Z)]


def local(x, wq, wk, wv, wf):
    me = jnp.stack([lax.axis_index(("y", "xh")), lax.axis_index("c"), lax.axis_index("z")])
    me = me.astype(jnp.int32)
    n, k = key_chunks(me, x, wk)
    k = spread(k)
    n, k[2] = lax.optimization_barrier((n, k[2]))
    q = query_chunks(n, wq)
    k = jnp.stack(k)
    q, k = lax.optimization_barrier((q, k))
    q = lax.all_to_all(q, ("z", "c"), 0, 0, tiled=True)
    k00, k01, k10, k11 = gather4(k)
    parts = score(me, q, keys_laid(me, k00, k10), k01, k11)
    parts = [parts[0]] + [flip(parts[s], "y", 4, s) for s in range(1, 4)]
    n, parts[1] = lax.optimization_barrier((n, parts[1]))
    v = jnp.stack(spread(value_chunks(me, n, wv)))
    own, shared, give, give_shared = total(parts)
    got = flip(give, "xh", 2, 1)
    near = flip(shared, "z", Z, 1)
    far = flip(give_shared, ("xh", "z"), 2 * Z, Z + 1)
    probs = softmax(1.0 / math.sqrt(DH * ROWS * 2 * PEERS), own, got, near, far)
    probs = lax.all_to_all(probs, ("y", "xh"), 0, 0, tiled=True)
    laid = [*values_laid(me, v), *values_laid(me, flip(v, "xl", 2, 1))]
    laid[3], probs = lax.optimization_barrier((laid[3], probs))
    return final(me, spread(mix(me, laid, probs, flip(probs, "c", 2, 1))), wf)


def solution(mesh):
    fine = Mesh(mesh.devices.reshape(4, 2, 2, 8, 2), ("y", "xh", "c", "z", "xl"))
    spec = P(("y", "xh", "c"), ("z", "xl"), None)
    return jax.shard_map(
        local,
        mesh=fine,
        in_specs=(spec, P(), P(), P(), P()),
        out_specs=spec,
        check_vma=False,
    )
```

```python
import functools
import math

import jax
import jax.numpy as jnp
from jax import lax
from jax.experimental import pallas as pl
from jax.experimental.pallas import tpu as pltpu
from jax.sharding import Mesh, PartitionSpec as P

H = 12
DH = 64
EMBED = 768
ROWS = 8
RES = 64
Z = 8
CHUNK = EMBED // Z
FULL = DH
HALF = CHUNK - DH
PEERS = 8
SUB = RES // 2
TOKENS = ROWS * SUB
QUERIES = Z * SUB
KEYS = 2 * Z * RES
LOGITS = KEYS + KEYS // 2

f32 = jnp.float32
bf16 = jnp.bfloat16
PARAMS = pltpu.CompilerParams(vmem_limit_bytes=8 * 1024 * 1024)
PROJECTION = pl.CostEstimate(
    flops=2 * ROWS * RES * EMBED * EMBED, bytes_accessed=2 * EMBED * (EMBED + 2 * ROWS * RES), transcendentals=0
)
LAYOUT = pl.CostEstimate(flops=0, bytes_accessed=16 * ROWS * RES * EMBED, transcendentals=0)
KEY_SHAPES = ((2 * ROWS * FULL, KEYS // 2), (2 * ROWS * FULL, KEYS // 4))
WIDE = pltpu.CompilerParams(vmem_limit_bytes=16 * 1024 * 1024)
VMEM = pl.BlockSpec(memory_space=pltpu.VMEM)
SMEM = pl.BlockSpec(memory_space=pltpu.SMEM)
ANY = pl.BlockSpec(memory_space=pl.ANY)


def chunk_pieces(z):
    base = z * CHUNK
    if z % 2 == 0:
        return (base, FULL), (base + FULL, HALF)
    return (base + HALF, FULL), (base, HALF)


def dot(a, b, ca, cb):
    return lax.dot_general(a, b, (((ca,), (cb,)), ((), ())), preferred_element_type=f32)


def shared_head(z):
    return z // 2 * (2 * CHUNK) + FULL


def chunk_rows(z):
    odd = lax.rem(z, 2)
    base = z * CHUNK
    return pl.multiple_of(base + odd * HALF, HALF), pl.multiple_of(base + (1 - odd) * FULL, HALF)


def fetches(sources, buffers, sems):
    copies = [pltpu.make_async_copy(a, b, sems.at[i]) for i, (a, b) in enumerate(zip(sources, buffers))]
    for copy in copies:
        copy.start()
    return copies


def in_hbm(*arrays):
    return [pltpu.with_memory_space_constraint(a, pltpu.HBM) for a in arrays]


def key_kernel(me_ref, x_hbm, w_hbm, n_ref, give_ref, *rest):
    outs, (x_ref, w_ref, t_ref, sems) = rest[:Z], rest[Z:]
    copy_x, copy_w = fetches((x_hbm, w_hbm), (x_ref, w_ref), sems)
    copy_x.wait()
    x = x_ref[...].astype(f32)
    centred = x - jnp.mean(x, axis=-1, keepdims=True)
    var = jnp.mean(centred * centred, axis=-1, keepdims=True)
    normed = (centred * lax.rsqrt(var + 1e-05)).astype(bf16)
    for h in range(2):
        n_ref[h] = normed[:, h * SUB : (h + 1) * SUB, :]
    give_ref[...] = n_ref[1 - me_ref[1]]
    copy_w.wait()
    t_ref[...] = dot(w_ref[...], n_ref[...].reshape(ROWS * RES, EMBED), 0, 1).astype(bf16)
    for s, out in enumerate(outs):
        z = lax.rem(me_ref[2] + s, Z)
        first, odd = shared_head(z), lax.rem(z, 2)
        lanes = pl.ds(pl.multiple_of(odd * TOKENS, TOKENS), TOKENS)
        out[0:FULL, :] = t_ref[pl.ds(chunk_rows(z)[0], FULL), :]
        for d in range(2):
            rows = pl.ds(pl.multiple_of(first + d * HALF, HALF), HALF)
            out[FULL:CHUNK, d * TOKENS : (d + 1) * TOKENS] = t_ref[rows, lanes]


def key_chunks(me, x, w):
    n, give, *k = pl.pallas_call(
        key_kernel,
        out_shape=(jax.ShapeDtypeStruct((2, ROWS, SUB, EMBED), bf16), jax.ShapeDtypeStruct((ROWS, SUB, EMBED), bf16))
        + (jax.ShapeDtypeStruct((CHUNK, ROWS * RES), bf16),) * Z,
        in_specs=[SMEM, ANY, ANY],
        out_specs=(VMEM,) * (2 + Z),
        scratch_shapes=[
            pltpu.VMEM((ROWS, RES, EMBED), bf16),
            pltpu.VMEM((EMBED, EMBED), bf16),
            pltpu.VMEM((EMBED, ROWS * RES), bf16),
            pltpu.SemaphoreType.DMA((2,)),
        ],
        compiler_params=PARAMS,
    )(me, *in_hbm(x, w))
    return n, give, k


def query_kernel(me_ref, n_ref, got_ref, w_ref, *rest):
    outs, t_ref = rest[:Z], rest[Z]
    for c, n in enumerate((n_ref[me_ref[1]], got_ref[...])):
        t = dot(w_ref[...], n.reshape(TOKENS, EMBED), 0, 1)
        t_ref[:, c * TOKENS : (c + 1) * TOKENS] = t.astype(bf16)
    for s, out in enumerate(outs):
        z = lax.rem(me_ref[2] + s, Z)
        out[0:FULL, :] = t_ref[pl.ds(chunk_rows(z)[0], FULL), :]
        out[FULL:, :] = t_ref[pl.ds(pl.multiple_of(shared_head(z), FULL), FULL), :]


def query_chunks(me, n, got, w):
    return pl.pallas_call(
        query_kernel,
        out_shape=(jax.ShapeDtypeStruct((2 * FULL, 2 * TOKENS), bf16),) * Z,
        in_specs=[SMEM] + [VMEM] * 3,
        out_specs=(VMEM,) * Z,
        scratch_shapes=[pltpu.VMEM((EMBED, 2 * TOKENS), bf16)],
        compiler_params=PARAMS,
        cost_estimate=PROJECTION,
    )(me, n, got, w)


def value_kernel(me_ref, n_ref, w_ref, *rest):
    outs, t_ref = rest[:Z], rest[Z]
    t_ref[...] = dot(w_ref[...], n_ref[...].reshape(ROWS * RES, EMBED), 0, 1).astype(bf16)
    for s, out in enumerate(outs):
        full, half = chunk_rows(lax.rem(me_ref[2] + s, Z))
        out[0:FULL, :] = t_ref[pl.ds(full, FULL), :]
        out[FULL:CHUNK, :] = t_ref[pl.ds(half, HALF), :]


def value_chunks(me, n, w):
    return pl.pallas_call(
        value_kernel,
        out_shape=(jax.ShapeDtypeStruct((CHUNK, ROWS * RES), bf16),) * Z,
        in_specs=[SMEM, VMEM, VMEM],
        out_specs=(VMEM,) * Z,
        scratch_shapes=[pltpu.VMEM((EMBED, ROWS * RES), bf16)],
        compiler_params=PARAMS,
        cost_estimate=PROJECTION,
    )(me, n, w)


def lay_keys(me, own, other, kf, kh):
    where = [lax.rem(me - z + Z, Z) for z in range(Z)]
    for cr, ref in enumerate((own, other)):
        for r in range(ROWS):
            n = (cr * ROWS + r) * FULL
            whole = [ref[z, 0:FULL, h * TOKENS + r * SUB : h * TOKENS + (r + 1) * SUB] for z in where for h in range(2)]
            kf[n : n + FULL, :] = jnp.concatenate(whole, axis=1)
            for d in range(2):
                first = d * TOKENS + r * SUB
                shared = [ref[z, FULL:CHUNK, first : first + SUB] for z in where]
                kh[n + d * HALF : n + (d + 1) * HALF, :] = jnp.concatenate(shared, axis=1)


def keys_kernel(me_ref, own, other, kf, kh, a, b, sems):
    for copy in fetches((own, other), (a, b), sems):
        copy.wait()
    lay_keys(me_ref[2], a, b, kf, kh)


def keys_laid(me, own, other):
    return pl.pallas_call(
        keys_kernel,
        out_shape=tuple(jax.ShapeDtypeStruct(s, bf16) for s in KEY_SHAPES),
        in_specs=[SMEM, ANY, ANY],
        out_specs=(VMEM,) * 2,
        scratch_shapes=[pltpu.VMEM(own.shape, bf16)] * 2 + [pltpu.SemaphoreType.DMA((2,))],
        compiler_params=PARAMS,
        cost_estimate=LAYOUT,
    )(me, own, other)


def score_kernel(me_ref, *refs):
    sources, outs, rest = refs[: 4 + Z], refs[4 + Z : 8 + Z], refs[8 + Z :]
    own, other, kf0, kh0, q_ref, qf, qh, kf1, kh1, sems = rest
    copies = fetches(sources, [own, other, kf0, kh0] + [q_ref.at[s] for s in range(Z)], sems)
    for copy in copies[:2]:
        copy.wait()
    z = me_ref[2]
    lay_keys(z, own, other, kf1, kh1)
    for copy in copies[2:]:
        copy.wait()
    peers = [jnp.bitwise_xor(me_ref[0], 2 * s + t) for s in range(4) for t in range(2)]
    queries = [q_ref[lax.rem(z - p + Z, Z)] for p in peers]
    for n in range(2 * ROWS):
        t = jnp.concatenate([b[:, n * SUB : (n + 1) * SUB] for b in queries], axis=1)
        qf[n * FULL : (n + 1) * FULL, :] = t[:FULL]
        qh[n * FULL : (n + 1) * FULL, :] = t[FULL:]
    first = 0
    for a, b in ((qf, kf0), (qf, kf1), (qh, kh0), (qh, kh1)):
        t = dot(a[...], b[...], 0, 0)
        for p in range(PEERS):
            outs[p // 2][p % 2, :, first : first + t.shape[1]] = t[p * SUB : (p + 1) * SUB]
        first += t.shape[1]


def score(me, qs, laid, own, other):
    rows = 2 * ROWS * FULL
    return pl.pallas_call(
        score_kernel,
        out_shape=(jax.ShapeDtypeStruct((2, SUB, LOGITS), f32),) * 4,
        in_specs=[SMEM] + [ANY] * (4 + Z),
        out_specs=(VMEM,) * 4,
        scratch_shapes=[pltpu.VMEM(a.shape, bf16) for a in (own, other, *laid)]
        + [pltpu.VMEM((Z, 2 * FULL, 2 * TOKENS), bf16)]
        + [pltpu.VMEM((rows, QUERIES), bf16)] * 2
        + [pltpu.VMEM(s, bf16) for s in KEY_SHAPES]
        + [pltpu.SemaphoreType.DMA((4 + Z,))],
        compiler_params=WIDE,
    )(me, own, other, *laid, *qs)


def total_kernel(p0, p1, p2, p3, own, shared, give, give_shared):
    t = p0[...] + p1[...] + (p2[...] + p3[...])
    own[...] = t[0]
    shared[...] = t[0, :, KEYS:]
    give[...] = t[1]
    give_shared[...] = t[1, :, KEYS:]


def total(parts):
    return pl.pallas_call(
        total_kernel,
        out_shape=tuple(jax.ShapeDtypeStruct((SUB, n), f32) for n in (LOGITS, KEYS // 2) * 2),
        in_specs=[VMEM] * 4,
        out_specs=(VMEM,) * 4,
        compiler_params=PARAMS,
    )(*parts)


def softmax_kernel(factor, own, got, near, far, out):
    whole = (own[...] + got[...]) * factor
    shared = jnp.concatenate([whole[:, KEYS:], (near[...] + far[...]) * factor], axis=1)
    for i, logits in enumerate((whole[:, :KEYS], shared)):
        powered = jnp.exp(logits - jnp.max(logits, axis=-1, keepdims=True))
        probs = (powered / jnp.sum(powered, axis=-1, keepdims=True)).astype(bf16)
        for p in range(PEERS):
            out[p, i] = probs


def softmax(factor, *parts):
    return pl.pallas_call(
        functools.partial(softmax_kernel, factor),
        out_shape=jax.ShapeDtypeStruct((PEERS, 2, SUB, KEYS), bf16),
        in_specs=[VMEM] * 4,
        out_specs=VMEM,
        compiler_params=PARAMS,
    )(*parts)


def values_kernel(me_ref, v_hbm, vf, vh, v, sems):
    fetches((v_hbm,), (v,), sems)[0].wait()
    z = me_ref[2]
    odd = lax.rem(z, 2)
    where = [lax.rem(z - source + Z, Z) for source in range(Z)]
    halves = [
        v[i, FULL:CHUNK, pl.ds(pl.multiple_of(h * TOKENS, TOKENS), TOKENS)] for h in (odd, 1 - odd) for i in where
    ]
    whole = [v[i, 0:FULL, h * TOKENS : (h + 1) * TOKENS] for i in where for h in range(2)]
    for r in range(ROWS):
        lanes = slice(r * SUB, (r + 1) * SUB)
        vf[r * FULL : (r + 1) * FULL, :] = jnp.concatenate([b[:, lanes] for b in whole], axis=1)
        vh[r * HALF : (r + 1) * HALF, :] = jnp.concatenate([b[:, lanes] for b in halves], axis=1)


def values_laid(me, v):
    return pl.pallas_call(
        values_kernel,
        out_shape=tuple(jax.ShapeDtypeStruct((ROWS * n, KEYS // 2), bf16) for n in (FULL, HALF)),
        in_specs=[SMEM, ANY],
        out_specs=(VMEM,) * 2,
        scratch_shapes=[pltpu.VMEM(v.shape, bf16), pltpu.SemaphoreType.DMA((1,))],
        compiler_params=PARAMS,
        cost_estimate=LAYOUT,
    )(me, v)


def mix_kernel(me_ref, own_hbm, other_hbm, *rest):
    laid, outs, (p_ref, vf0, vh0, vf1, vh1, sems) = rest[:4], rest[4 : 4 + Z], rest[4 + Z :]
    core, z = me_ref[1], me_ref[2]
    copies = fetches(
        (own_hbm, other_hbm, *laid), (p_ref.at[core], p_ref.at[1 - core], vf0, vh0, vf1, vh1), sems
    )
    for copy in copies:
        copy.wait()
    quarter = KEYS // 4
    for i, (near, far, first, n) in enumerate(((vf0, vf1, 0, FULL), (vh0, vh1, FULL, HALF))):
        for h in range(2):
            probs = jnp.concatenate([p_ref[h, lax.rem(z + s, Z), i] for s in range(Z)], axis=0)
            quarters = [probs[:, k * quarter : (k + 1) * quarter] for k in range(4)]
            a, b = (quarters[:2], quarters[2:]) if i == 0 else (quarters[::2], quarters[1::2])
            mixed = dot(near[...], jnp.concatenate(a, axis=1), 1, 1) + dot(far[...], jnp.concatenate(b, axis=1), 1, 1)
            mixed = mixed.astype(bf16)
            for s, out in enumerate(outs):
                out[first : first + n, h * TOKENS : (h + 1) * TOKENS] = jnp.concatenate(
                    [mixed[r * n : (r + 1) * n, s * SUB : (s + 1) * SUB] for r in range(ROWS)], axis=1
                )


def mix(me, laid, own, other):
    return pl.pallas_call(
        mix_kernel,
        out_shape=(jax.ShapeDtypeStruct((CHUNK, ROWS * RES), bf16),) * Z,
        in_specs=[SMEM] + [ANY] * 6,
        out_specs=(VMEM,) * Z,
        scratch_shapes=[pltpu.VMEM((2, *own.shape), bf16)]
        + [pltpu.VMEM(a.shape, bf16) for a in laid]
        + [pltpu.SemaphoreType.DMA((6,))],
        compiler_params=WIDE,
    )(me, own, other, *laid)


def final_kernel(me_ref, *refs):
    pieces, w_ref, o_ref, t_ref = refs[:Z], refs[Z], refs[Z + 1], refs[Z + 2]
    for s, piece in enumerate(pieces):
        full, half = chunk_rows(lax.rem(me_ref[2] - s + Z, Z))
        t_ref[pl.ds(full, FULL), :] = piece[0:FULL, :]
        t_ref[pl.ds(half, HALF), :] = piece[FULL:CHUNK, :]
    for h in range(2):
        attended = dot(t_ref[:, h * TOKENS : (h + 1) * TOKENS], w_ref[...], 0, 0).astype(bf16)
        o_ref[:, h * SUB : (h + 1) * SUB, :] = attended.reshape(ROWS, SUB, EMBED)


def final(me, pieces, w):
    return pl.pallas_call(
        final_kernel,
        out_shape=jax.ShapeDtypeStruct((ROWS, RES, EMBED), bf16),
        in_specs=[SMEM] + [VMEM] * (Z + 1),
        out_specs=VMEM,
        scratch_shapes=[pltpu.VMEM((EMBED, ROWS * RES), bf16)],
        compiler_params=PARAMS,
    )(me, *pieces, w)


def flip(x, axes, n, s):
    return lax.ppermute(x, axes, [(i, i ^ s) for i in range(n)])


def shift(x, s):
    return lax.ppermute(x, "z", [(i, (i + s) % Z) for i in range(Z)])


def spread(pieces):
    got = {s: shift(pieces[s], s) for s in (4, 3, 5, 2, 6, 1, 7)}
    return [pieces[0]] + [got[s] for s in range(1, Z)]


def local(x, wq, wk, wv, wf):
    me = jnp.stack([lax.axis_index(("y", "xh")), lax.axis_index("c"), lax.axis_index("z")])
    me = me.astype(jnp.int32)
    n, give, k = key_chunks(me, x, wk)
    k = spread(k)
    n, k[4] = lax.optimization_barrier((n, k[4]))
    q = list(query_chunks(me, n, flip(give, "c", 2, 1), wq))
    k, q[7] = lax.optimization_barrier((jnp.stack(k), q[7]))
    q = spread(q)
    k_far = flip(k, "xl", 2, 1)
    k_far, q[4], q[3], q[5], q[2] = lax.optimization_barrier((k_far, q[4], q[3], q[5], q[2]))
    parts = score(me, q, keys_laid(me, k, flip(k, "c", 2, 1)), k_far, flip(k_far, "c", 2, 1))
    parts = [parts[0]] + [flip(parts[s], "y", 4, s) for s in range(1, 4)]
    n, parts[1] = lax.optimization_barrier((n, parts[1]))
    v = list(value_chunks(me, n, wv))
    v[7], parts[2] = lax.optimization_barrier((v[7], parts[2]))
    long = [shift(v[s], s) for s in (4, 3, 5)]
    parts[3], *long = lax.optimization_barrier((parts[3], *long))
    own, shared, give, give_shared = total(parts)
    got = flip(give, "xh", 2, 1)
    near = flip(shared, "z", Z, 1)
    far = flip(give_shared, ("xh", "z"), 2 * Z, Z + 1)
    *short, near = lax.optimization_barrier((v[2], v[6], v[1], v[7], near))
    short = [shift(a, s) for a, s in zip(short, (2, 6, 1, 7))]
    v = jnp.stack([v[0], short[2], short[0], long[1], long[0], long[2], short[1], short[3]])
    probs = softmax(1.0 / math.sqrt(DH * ROWS * 2 * PEERS), own, got, near, far)
    probs = lax.all_to_all(probs, ("y", "xh"), 0, 0, tiled=True)
    laid = [*values_laid(me, v), *values_laid(me, flip(v, "xl", 2, 1))]
    laid[3], probs = lax.optimization_barrier((laid[3], probs))
    return final(me, spread(mix(me, laid, probs, flip(probs, "c", 2, 1))), wf)


def solution(mesh):
    fine = Mesh(mesh.devices.reshape(4, 2, 2, 8, 2), ("y", "xh", "c", "z", "xl"))
    spec = P(("y", "xh", "c"), ("z", "xl"), None)
    return jax.shard_map(
        local,
        mesh=fine,
        in_specs=(spec, P(), P(), P(), P()),
        out_specs=spec,
        check_vma=False,
    )
```

```python
import functools
import math

import jax
import jax.numpy as jnp
from jax import lax
from jax.experimental import pallas as pl
from jax.experimental.pallas import tpu as pltpu
from jax.sharding import Mesh, PartitionSpec as P

H = 12
DH = 64
EMBED = 768
ROWS = 8
RES = 64
Z = 8
CHUNK = EMBED // Z
FULL = DH
HALF = CHUNK - DH
PEERS = 8
SUB = RES // 2
QUERIES = Z * SUB
KEYS = 2 * Z * RES

f32 = jnp.float32
bf16 = jnp.bfloat16
PARAMS = pltpu.CompilerParams(vmem_limit_bytes=16 * 1024 * 1024)
PROJECTION = pl.CostEstimate(
    flops=2 * ROWS * RES * EMBED * EMBED, bytes_accessed=2 * EMBED * (EMBED + 2 * ROWS * RES), transcendentals=0
)
VMEM = pl.BlockSpec(memory_space=pltpu.VMEM)
SMEM = pl.BlockSpec(memory_space=pltpu.SMEM)
ANY = pl.BlockSpec(memory_space=pl.ANY)
LAYOUT = pl.CostEstimate(flops=0, bytes_accessed=16 * ROWS * RES * EMBED, transcendentals=0)


def chunk_pieces(z):
    base = z * CHUNK
    if z % 2 == 0:
        return (base, FULL), (base + FULL, HALF)
    return (base + HALF, FULL), (base, HALF)


def dot(a, b, ca, cb):
    return lax.dot_general(a, b, (((ca,), (cb,)), ((), ())), preferred_element_type=f32)


def chunk_rows(z):
    odd = lax.rem(z, 2)
    base = z * CHUNK
    return pl.multiple_of(base + odd * HALF, HALF), pl.multiple_of(base + (1 - odd) * FULL, HALF)


def send_pieces(z, t_ref, outs):
    for s, out in enumerate(outs):
        full, half = chunk_rows(lax.rem(z + s, Z))
        out[0:FULL, :] = t_ref[pl.ds(full, FULL), :]
        out[FULL:CHUNK, :] = t_ref[pl.ds(half, HALF), :]


def fetches(sources, buffers, sems):
    copies = [pltpu.make_async_copy(a, b, sems.at[i]) for i, (a, b) in enumerate(zip(sources, buffers))]
    for copy in copies:
        copy.start()
    return copies


def in_hbm(*arrays):
    return [pltpu.with_memory_space_constraint(a, pltpu.HBM) for a in arrays]


def key_kernel(me_ref, x_hbm, w_hbm, n_ref, *rest):
    outs, (x_ref, w_ref, t_ref, sems) = rest[:Z], rest[Z:]
    copy_x, copy_w = fetches((x_hbm, w_hbm), (x_ref, w_ref), sems)
    copy_x.wait()
    x = x_ref[...].astype(f32)
    centred = x - jnp.mean(x, axis=-1, keepdims=True)
    var = jnp.mean(centred * centred, axis=-1, keepdims=True)
    n_ref[...] = (centred * lax.rsqrt(var + 1e-05)).astype(bf16)
    copy_w.wait()
    t_ref[...] = dot(w_ref[...], n_ref[...].reshape(ROWS * RES, EMBED), 0, 1).astype(bf16)
    send_pieces(me_ref[2], t_ref, outs)


def key_chunks(me, x, w):
    n, *k = pl.pallas_call(
        key_kernel,
        out_shape=(jax.ShapeDtypeStruct((ROWS, RES, EMBED), bf16),)
        + (jax.ShapeDtypeStruct((CHUNK, ROWS * RES), bf16),) * Z,
        in_specs=[SMEM, ANY, ANY],
        out_specs=(VMEM,) * (Z + 1),
        scratch_shapes=[
            pltpu.VMEM((ROWS, RES, EMBED), bf16),
            pltpu.VMEM((EMBED, EMBED), bf16),
            pltpu.VMEM((EMBED, ROWS * RES), bf16),
            pltpu.SemaphoreType.DMA((2,)),
        ],
        compiler_params=PARAMS,
    )(me, *in_hbm(x, w))
    return n, k


def query_kernel(n_ref, w_ref, q_ref):
    for c in range(2):
        n = n_ref[:, c * SUB : (c + 1) * SUB, :].reshape(ROWS * SUB, EMBED)
        t = dot(w_ref[...], n, 0, 1).astype(bf16)
        for z in range(Z):
            (a, na), (b, nb) = chunk_pieces(z)
            q_ref[2 * z + c, 0:FULL, :] = t[a : a + na]
            q_ref[2 * z + c, FULL:CHUNK, :] = t[b : b + nb]


def query_chunks(n, w):
    return pl.pallas_call(
        query_kernel,
        out_shape=jax.ShapeDtypeStruct((2 * Z, CHUNK, ROWS * SUB), bf16),
        in_specs=[VMEM] * 2,
        out_specs=VMEM,
        compiler_params=PARAMS,
        cost_estimate=PROJECTION,
    )(n, w)


def value_kernel(me_ref, n_ref, w_ref, *rest):
    outs, t_ref = rest[:Z], rest[Z]
    t_ref[...] = dot(w_ref[...], n_ref[...].reshape(ROWS * RES, EMBED), 0, 1).astype(bf16)
    send_pieces(me_ref[2], t_ref, outs)


def value_chunks(me, n, w):
    return pl.pallas_call(
        value_kernel,
        out_shape=(jax.ShapeDtypeStruct((CHUNK, ROWS * RES), bf16),) * Z,
        in_specs=[SMEM, VMEM, VMEM],
        out_specs=(VMEM,) * Z,
        scratch_shapes=[pltpu.VMEM((EMBED, ROWS * RES), bf16)],
        compiler_params=PARAMS,
        cost_estimate=PROJECTION,
    )(me, n, w)


def arrived(z, refs):
    return [ref[lax.rem(z - source + Z, Z)] for ref in refs for source in range(Z)]


def widen(blocks, r):
    return jnp.concatenate([b[:, r * RES : (r + 1) * RES] for b in blocks], axis=1)


def score_kernel(me_ref, q_ref, k00, k01, k10, k11, out, qf, qh, kf, kh):
    core, z = me_ref[1], me_ref[2]
    for cr, ks in ((0, (k00, k01)), (1, (k10, k11))):
        c = jnp.bitwise_xor(core, cr)
        queries = [q_ref[2 * p + c] for p in range(PEERS)]
        keys = arrived(z, ks)
        for r in range(ROWS):
            n = cr * ROWS + r
            t = jnp.concatenate([b[:, r * SUB : (r + 1) * SUB] for b in queries], axis=1)
            qf[n * FULL : (n + 1) * FULL, :] = t[:FULL]
            qh[n * HALF : (n + 1) * HALF, :] = t[FULL:]
            t = widen(keys, r)
            kf[n * FULL : (n + 1) * FULL, :] = t[:FULL]
            kh[n * HALF : (n + 1) * HALF, :] = t[FULL:]
    for i, (a, b) in enumerate(((qf, kf), (qh, kh))):
        s = dot(a[...], b[...], 0, 0)
        for p in range(PEERS):
            out[p, i] = s[p * SUB : (p + 1) * SUB]


def score(me, q, ks):
    rows = 2 * ROWS
    return pl.pallas_call(
        score_kernel,
        out_shape=jax.ShapeDtypeStruct((PEERS, 2, SUB, KEYS), f32),
        in_specs=[SMEM] + [VMEM] * 5,
        out_specs=VMEM,
        scratch_shapes=[
            pltpu.VMEM((rows * FULL, QUERIES), bf16),
            pltpu.VMEM((rows * HALF, QUERIES), bf16),
            pltpu.VMEM((rows * FULL, KEYS), bf16),
            pltpu.VMEM((rows * HALF, KEYS), bf16),
        ],
        compiler_params=PARAMS,
    )(me, q, *ks)


def total_kernel(parts, full, half):
    for i, out in enumerate((full, half)):
        t = parts[0, i]
        for p in range(1, PEERS):
            t = t + parts[p, i]
        out[...] = t


def total(parts):
    return pl.pallas_call(
        total_kernel,
        out_shape=(jax.ShapeDtypeStruct((SUB, KEYS), f32),) * 2,
        in_specs=[VMEM],
        out_specs=(VMEM,) * 2,
        compiler_params=PARAMS,
    )(parts)


def softmax_kernel(factor, full, half, other, out):
    for i, logits in enumerate((full[...], half[...] + other[...])):
        logits = logits * factor
        powered = jnp.exp(logits - jnp.max(logits, axis=-1, keepdims=True))
        probs = (powered / jnp.sum(powered, axis=-1, keepdims=True)).astype(bf16)
        for p in range(PEERS):
            out[p, i] = probs


def softmax(factor, full, half, other):
    return pl.pallas_call(
        functools.partial(softmax_kernel, factor),
        out_shape=jax.ShapeDtypeStruct((PEERS, 2, SUB, KEYS), bf16),
        in_specs=[VMEM] * 3,
        out_specs=VMEM,
        compiler_params=PARAMS,
    )(full, half, other)


def values_kernel(me_ref, v00, v01, v10, v11, vf, vh):
    for cr, vs in enumerate(((v00, v01), (v10, v11))):
        values = arrived(me_ref[2], vs)
        for r in range(ROWS):
            n = cr * ROWS + r
            t = widen(values, r)
            vf[n * FULL : (n + 1) * FULL, :] = t[:FULL]
            vh[n * HALF : (n + 1) * HALF, :] = t[FULL:]


def values_laid(me, vs):
    return pl.pallas_call(
        values_kernel,
        out_shape=tuple(jax.ShapeDtypeStruct((2 * ROWS * n, KEYS), bf16) for n in (FULL, HALF)),
        in_specs=[SMEM] + [VMEM] * 4,
        out_specs=(VMEM,) * 2,
        compiler_params=PARAMS,
        cost_estimate=LAYOUT,
    )(me, *vs)


def mix_kernel(me_ref, vf, vh, p_ref, o_ref):
    core = me_ref[1]
    for i, (v, first, n) in enumerate(((vf, 0, FULL), (vh, FULL, HALF))):
        probs = p_ref[:, i].reshape(QUERIES, KEYS)
        for cr in range(2):
            c = jnp.bitwise_xor(core, cr)
            mixed = dot(v[cr * ROWS * n : (cr + 1) * ROWS * n, :], probs, 1, 1).astype(bf16)
            for s in range(PEERS):
                o_ref[2 * s + c, first : first + n, :] = jnp.concatenate(
                    [mixed[r * n : (r + 1) * n, s * SUB : (s + 1) * SUB] for r in range(ROWS)], axis=1
                )


def mix(me, laid, probs):
    return pl.pallas_call(
        mix_kernel,
        out_shape=jax.ShapeDtypeStruct((2 * Z, CHUNK, ROWS * SUB), bf16),
        in_specs=[SMEM] + [VMEM] * 3,
        out_specs=VMEM,
        compiler_params=PARAMS,
    )(me, *laid, probs)


def final_kernel(m_ref, w_ref, o_ref, t_ref):
    for c in range(2):
        for z in range(Z):
            (a, na), (b, nb) = chunk_pieces(z)
            t_ref[a : a + na, :] = m_ref[2 * z + c, 0:FULL, :]
            t_ref[b : b + nb, :] = m_ref[2 * z + c, FULL:CHUNK, :]
        attended = dot(t_ref[...], w_ref[...], 0, 0).astype(bf16)
        o_ref[:, c * SUB : (c + 1) * SUB, :] = attended.reshape(ROWS, SUB, EMBED)


def final(m, w):
    return pl.pallas_call(
        final_kernel,
        out_shape=jax.ShapeDtypeStruct((ROWS, RES, EMBED), bf16),
        in_specs=[VMEM] * 2,
        out_specs=VMEM,
        scratch_shapes=[pltpu.VMEM((EMBED, ROWS * SUB), bf16)],
        compiler_params=PARAMS,
    )(m, w)


def flip(x, axes, n, s):
    return lax.ppermute(x, axes, [(i, i ^ s) for i in range(n)])


def gather4(own):
    far = flip(own, "xl", 2, 1)
    return own, far, flip(own, "c", 2, 1), flip(far, "c", 2, 1)


def shift(x, s):
    return lax.ppermute(x, "z", [(i, (i + s) % Z) for i in range(Z)])


def local(x, wq, wk, wv, wf):
    me = jnp.stack([lax.axis_index(("y", "xh")), lax.axis_index("c"), lax.axis_index("z")])
    me = me.astype(jnp.int32)
    n, k = key_chunks(me, x, wk)
    for s in (1, 7, 2, 6, 3, 5, 4):
        k[s] = shift(k[s], s)
    q, k[2] = lax.optimization_barrier((query_chunks(n, wq), k[2]))
    q = lax.all_to_all(q, ("z", "c"), 0, 0, tiled=True)
    v = list(value_chunks(me, n, wv))
    k = jnp.stack(k)
    k_far, v[4] = lax.optimization_barrier((flip(k, "xl", 2, 1), v[4]))
    scores = score(me, q, (k, k_far, flip(k, "c", 2, 1), flip(k_far, "c", 2, 1)))
    *v, scores = lax.optimization_barrier((*v, scores))
    parts = lax.all_to_all(scores, ("y", "xh"), 0, 0, tiled=True)
    for s in (3, 5, 4, 2, 6, 1, 7):
        v[s] = shift(v[s], s)
    full, half = total(parts)
    rows = ROWS * 2 * PEERS
    probs = softmax(1.0 / math.sqrt(DH * rows), full, half, flip(half, "z", Z, 1))
    probs = lax.all_to_all(probs, ("y", "xh"), 0, 0, tiled=True)
    laid = values_laid(me, gather4(jnp.stack(v)))
    mixed = lax.all_to_all(mix(me, laid, probs), ("z", "c"), 0, 0, tiled=True)
    return final(mixed, wf)


def solution(mesh):
    fine = Mesh(mesh.devices.reshape(4, 2, 2, 8, 2), ("y", "xh", "c", "z", "xl"))
    spec = P(("y", "xh", "c"), ("z", "xl"), None)
    return jax.shard_map(
        local,
        mesh=fine,
        in_specs=(spec, P(), P(), P(), P()),
        out_specs=spec,
        check_vma=False,
    )
```

```python
import functools
import math

import jax
import jax.numpy as jnp
from jax import lax
from jax.experimental import pallas as pl
from jax.experimental.pallas import tpu as pltpu
from jax.sharding import Mesh, PartitionSpec as P

H = 12
DH = 64
EMBED = 768
ROWS = 8
RES = 64
Z = 8
CHUNK = EMBED // Z
FULL = DH
HALF = CHUNK - DH
PEERS = 8
SUB = RES // 2
QUERIES = Z * SUB
KEYS = 2 * Z * RES

f32 = jnp.float32
bf16 = jnp.bfloat16
PARAMS = pltpu.CompilerParams(vmem_limit_bytes=16 * 1024 * 1024)
PROJECTION = pl.CostEstimate(
    flops=2 * ROWS * RES * EMBED * EMBED, bytes_accessed=2 * EMBED * (EMBED + 2 * ROWS * RES), transcendentals=0
)
VMEM = pl.BlockSpec(memory_space=pltpu.VMEM)
SMEM = pl.BlockSpec(memory_space=pltpu.SMEM)
ANY = pl.BlockSpec(memory_space=pl.ANY)
LAYOUT = pl.CostEstimate(flops=0, bytes_accessed=16 * ROWS * RES * EMBED, transcendentals=0)


def chunk_pieces(z):
    base = z * CHUNK
    if z % 2 == 0:
        return (base, FULL), (base + FULL, HALF)
    return (base + HALF, FULL), (base, HALF)


def dot(a, b, ca, cb):
    return lax.dot_general(a, b, (((ca,), (cb,)), ((), ())), preferred_element_type=f32)


def chunk_rows(z):
    odd = lax.rem(z, 2)
    base = z * CHUNK
    return pl.multiple_of(base + odd * HALF, HALF), pl.multiple_of(base + (1 - odd) * FULL, HALF)


def send_pieces(z, t_ref, outs):
    for s, out in enumerate(outs):
        full, half = chunk_rows(lax.rem(z + s, Z))
        out[0:FULL, :] = t_ref[pl.ds(full, FULL), :]
        out[FULL:CHUNK, :] = t_ref[pl.ds(half, HALF), :]


def fetches(sources, buffers, sems):
    copies = [pltpu.make_async_copy(a, b, sems.at[i]) for i, (a, b) in enumerate(zip(sources, buffers))]
    for copy in copies:
        copy.start()
    return copies


def in_hbm(*arrays):
    return [pltpu.with_memory_space_constraint(a, pltpu.HBM) for a in arrays]


def key_kernel(me_ref, x_hbm, w_hbm, n_ref, *rest):
    outs, (x_ref, w_ref, t_ref, sems) = rest[:Z], rest[Z:]
    copy_x, copy_w = fetches((x_hbm, w_hbm), (x_ref, w_ref), sems)
    copy_x.wait()
    x = x_ref[...].astype(f32)
    centred = x - jnp.mean(x, axis=-1, keepdims=True)
    var = jnp.mean(centred * centred, axis=-1, keepdims=True)
    n_ref[...] = (centred * lax.rsqrt(var + 1e-05)).astype(bf16)
    copy_w.wait()
    t_ref[...] = dot(w_ref[...], n_ref[...].reshape(ROWS * RES, EMBED), 0, 1).astype(bf16)
    send_pieces(me_ref[2], t_ref, outs)


def key_chunks(me, x, w):
    n, *k = pl.pallas_call(
        key_kernel,
        out_shape=(jax.ShapeDtypeStruct((ROWS, RES, EMBED), bf16),)
        + (jax.ShapeDtypeStruct((CHUNK, ROWS * RES), bf16),) * Z,
        in_specs=[SMEM, ANY, ANY],
        out_specs=(VMEM,) * (Z + 1),
        scratch_shapes=[
            pltpu.VMEM((ROWS, RES, EMBED), bf16),
            pltpu.VMEM((EMBED, EMBED), bf16),
            pltpu.VMEM((EMBED, ROWS * RES), bf16),
            pltpu.SemaphoreType.DMA((2,)),
        ],
        compiler_params=PARAMS,
    )(me, *in_hbm(x, w))
    return n, k


def query_kernel(n_ref, w_ref, q_ref):
    for c in range(2):
        n = n_ref[:, c * SUB : (c + 1) * SUB, :].reshape(ROWS * SUB, EMBED)
        t = dot(w_ref[...], n, 0, 1).astype(bf16)
        for z in range(Z):
            (a, na), (b, nb) = chunk_pieces(z)
            q_ref[2 * z + c, 0:FULL, :] = t[a : a + na]
            q_ref[2 * z + c, FULL:CHUNK, :] = t[b : b + nb]


def query_chunks(n, w):
    return pl.pallas_call(
        query_kernel,
        out_shape=jax.ShapeDtypeStruct((2 * Z, CHUNK, ROWS * SUB), bf16),
        in_specs=[VMEM] * 2,
        out_specs=VMEM,
        compiler_params=PARAMS,
        cost_estimate=PROJECTION,
    )(n, w)


def value_kernel(me_ref, n_ref, w_ref, *rest):
    outs, t_ref = rest[:Z], rest[Z]
    t_ref[...] = dot(w_ref[...], n_ref[...].reshape(ROWS * RES, EMBED), 0, 1).astype(bf16)
    send_pieces(me_ref[2], t_ref, outs)


def value_chunks(me, n, w):
    return pl.pallas_call(
        value_kernel,
        out_shape=(jax.ShapeDtypeStruct((CHUNK, ROWS * RES), bf16),) * Z,
        in_specs=[SMEM, VMEM, VMEM],
        out_specs=(VMEM,) * Z,
        scratch_shapes=[pltpu.VMEM((EMBED, ROWS * RES), bf16)],
        compiler_params=PARAMS,
        cost_estimate=PROJECTION,
    )(me, n, w)


def arrived(z, refs):
    return [ref[lax.rem(z - source + Z, Z)] for ref in refs for source in range(Z)]


def widen(blocks, r):
    return jnp.concatenate([b[:, r * RES : (r + 1) * RES] for b in blocks], axis=1)


def score_kernel(me_ref, q_ref, k00, k01, k10, k11, out, qf, qh, kf, kh):
    core, z = me_ref[1], me_ref[2]
    for cr, ks in ((0, (k00, k01)), (1, (k10, k11))):
        c = jnp.bitwise_xor(core, cr)
        queries = [q_ref[2 * p + c] for p in range(PEERS)]
        keys = arrived(z, ks)
        for r in range(ROWS):
            n = cr * ROWS + r
            t = jnp.concatenate([b[:, r * SUB : (r + 1) * SUB] for b in queries], axis=1)
            qf[n * FULL : (n + 1) * FULL, :] = t[:FULL]
            qh[n * HALF : (n + 1) * HALF, :] = t[FULL:]
            t = widen(keys, r)
            kf[n * FULL : (n + 1) * FULL, :] = t[:FULL]
            kh[n * HALF : (n + 1) * HALF, :] = t[FULL:]
    for i, (a, b) in enumerate(((qf, kf), (qh, kh))):
        s = dot(a[...], b[...], 0, 0)
        for p in range(PEERS):
            out[p, i] = s[p * SUB : (p + 1) * SUB]


def score(me, q, ks):
    rows = 2 * ROWS
    return pl.pallas_call(
        score_kernel,
        out_shape=jax.ShapeDtypeStruct((PEERS, 2, SUB, KEYS), f32),
        in_specs=[SMEM] + [VMEM] * 5,
        out_specs=VMEM,
        scratch_shapes=[
            pltpu.VMEM((rows * FULL, QUERIES), bf16),
            pltpu.VMEM((rows * HALF, QUERIES), bf16),
            pltpu.VMEM((rows * FULL, KEYS), bf16),
            pltpu.VMEM((rows * HALF, KEYS), bf16),
        ],
        compiler_params=PARAMS,
    )(me, q, *ks)


def total_kernel(parts, full, half):
    for i, out in enumerate((full, half)):
        t = parts[0, i]
        for p in range(1, PEERS):
            t = t + parts[p, i]
        out[...] = t


def total(parts):
    return pl.pallas_call(
        total_kernel,
        out_shape=(jax.ShapeDtypeStruct((SUB, KEYS), f32),) * 2,
        in_specs=[VMEM],
        out_specs=(VMEM,) * 2,
        compiler_params=PARAMS,
    )(parts)


def softmax_kernel(factor, full, half, other, out):
    for i, logits in enumerate((full[...], half[...] + other[...])):
        logits = logits * factor
        powered = jnp.exp(logits - jnp.max(logits, axis=-1, keepdims=True))
        probs = (powered / jnp.sum(powered, axis=-1, keepdims=True)).astype(bf16)
        for p in range(PEERS):
            out[p, i] = probs


def softmax(factor, full, half, other):
    return pl.pallas_call(
        functools.partial(softmax_kernel, factor),
        out_shape=jax.ShapeDtypeStruct((PEERS, 2, SUB, KEYS), bf16),
        in_specs=[VMEM] * 3,
        out_specs=VMEM,
        compiler_params=PARAMS,
    )(full, half, other)


def values_kernel(me_ref, v00, v01, v10, v11, vf, vh):
    for cr, vs in enumerate(((v00, v01), (v10, v11))):
        values = arrived(me_ref[2], vs)
        for r in range(ROWS):
            n = cr * ROWS + r
            t = widen(values, r)
            vf[n * FULL : (n + 1) * FULL, :] = t[:FULL]
            vh[n * HALF : (n + 1) * HALF, :] = t[FULL:]


def values_laid(me, vs):
    return pl.pallas_call(
        values_kernel,
        out_shape=tuple(jax.ShapeDtypeStruct((2 * ROWS * n, KEYS), bf16) for n in (FULL, HALF)),
        in_specs=[SMEM] + [VMEM] * 4,
        out_specs=(VMEM,) * 2,
        compiler_params=PARAMS,
        cost_estimate=LAYOUT,
    )(me, *vs)


def mix_kernel(me_ref, vf, vh, p_ref, o_ref):
    core = me_ref[1]
    for i, (v, first, n) in enumerate(((vf, 0, FULL), (vh, FULL, HALF))):
        probs = p_ref[:, i].reshape(QUERIES, KEYS)
        for cr in range(2):
            c = jnp.bitwise_xor(core, cr)
            mixed = dot(v[cr * ROWS * n : (cr + 1) * ROWS * n, :], probs, 1, 1).astype(bf16)
            for s in range(PEERS):
                o_ref[2 * s + c, first : first + n, :] = jnp.concatenate(
                    [mixed[r * n : (r + 1) * n, s * SUB : (s + 1) * SUB] for r in range(ROWS)], axis=1
                )


def mix(me, laid, probs):
    return pl.pallas_call(
        mix_kernel,
        out_shape=jax.ShapeDtypeStruct((2 * Z, CHUNK, ROWS * SUB), bf16),
        in_specs=[SMEM] + [VMEM] * 3,
        out_specs=VMEM,
        compiler_params=PARAMS,
    )(me, *laid, probs)


def final_kernel(m_ref, w_ref, o_ref, t_ref):
    for c in range(2):
        for z in range(Z):
            (a, na), (b, nb) = chunk_pieces(z)
            t_ref[a : a + na, :] = m_ref[2 * z + c, 0:FULL, :]
            t_ref[b : b + nb, :] = m_ref[2 * z + c, FULL:CHUNK, :]
        attended = dot(t_ref[...], w_ref[...], 0, 0).astype(bf16)
        o_ref[:, c * SUB : (c + 1) * SUB, :] = attended.reshape(ROWS, SUB, EMBED)


def final(m, w):
    return pl.pallas_call(
        final_kernel,
        out_shape=jax.ShapeDtypeStruct((ROWS, RES, EMBED), bf16),
        in_specs=[VMEM] * 2,
        out_specs=VMEM,
        scratch_shapes=[pltpu.VMEM((EMBED, ROWS * SUB), bf16)],
        compiler_params=PARAMS,
    )(m, w)


def flip(x, axes, n, s):
    return lax.ppermute(x, axes, [(i, i ^ s) for i in range(n)])


def gather4(own):
    far = flip(own, "xl", 2, 1)
    return own, far, flip(own, "c", 2, 1), flip(far, "c", 2, 1)


def shift(x, s):
    return lax.ppermute(x, "z", [(i, (i + s) % Z) for i in range(Z)])


def local(x, wq, wk, wv, wf):
    me = jnp.stack([lax.axis_index(("y", "xh")), lax.axis_index("c"), lax.axis_index("z")])
    me = me.astype(jnp.int32)
    n, k = key_chunks(me, x, wk)
    for s in (1, 7, 2, 6, 3, 5, 4):
        k[s] = shift(k[s], s)
    q, k[2] = lax.optimization_barrier((query_chunks(n, wq), k[2]))
    q = lax.all_to_all(q, ("z", "c"), 0, 0, tiled=True)
    v = list(value_chunks(me, n, wv))
    k = jnp.stack(k)
    k_far, v[4] = lax.optimization_barrier((flip(k, "xl", 2, 1), v[4]))
    for s in (3, 5):
        v[s] = shift(v[s], s)
    scores = score(me, q, (k, k_far, flip(k, "c", 2, 1), flip(k_far, "c", 2, 1)))
    *v, scores = lax.optimization_barrier((*v, scores))
    parts = lax.all_to_all(scores, ("y", "xh"), 0, 0, tiled=True)
    for s in (4, 2, 6, 1, 7):
        v[s] = shift(v[s], s)
    full, half = total(parts)
    rows = ROWS * 2 * PEERS
    probs = softmax(1.0 / math.sqrt(DH * rows), full, half, flip(half, "z", Z, 1))
    probs = lax.all_to_all(probs, ("y", "xh"), 0, 0, tiled=True)
    laid = values_laid(me, gather4(jnp.stack(v)))
    mixed = lax.all_to_all(mix(me, laid, probs), ("z", "c"), 0, 0, tiled=True)
    return final(mixed, wf)


def solution(mesh):
    fine = Mesh(mesh.devices.reshape(4, 2, 2, 8, 2), ("y", "xh", "c", "z", "xl"))
    spec = P(("y", "xh", "c"), ("z", "xl"), None)
    return jax.shard_map(
        local,
        mesh=fine,
        in_specs=(spec, P(), P(), P(), P()),
        out_specs=spec,
        check_vma=False,
    )
```

```python
import functools
import math

import jax
import jax.numpy as jnp
from jax import lax
from jax.experimental import pallas as pl
from jax.experimental.pallas import tpu as pltpu
from jax.sharding import Mesh, PartitionSpec as P

H = 12
DH = 64
EMBED = 768
ROWS = 8
RES = 64
Z = 8
CHUNK = EMBED // Z
FULL = DH
HALF = CHUNK - DH
PEERS = 8
SUB = RES // 2
TOKENS = ROWS * SUB
QUERIES = Z * SUB
KEYS = 2 * Z * RES
LOGITS = KEYS + KEYS // 2

f32 = jnp.float32
bf16 = jnp.bfloat16
PARAMS = pltpu.CompilerParams(vmem_limit_bytes=16 * 1024 * 1024)
PROJECTION = pl.CostEstimate(
    flops=2 * ROWS * RES * EMBED * EMBED, bytes_accessed=2 * EMBED * (EMBED + 2 * ROWS * RES), transcendentals=0
)
LAYOUT = pl.CostEstimate(flops=0, bytes_accessed=16 * ROWS * RES * EMBED, transcendentals=0)
KEY_SHAPES = ((2 * ROWS * FULL, KEYS // 2), (2 * ROWS * FULL, KEYS // 4))
WIDE = pltpu.CompilerParams(vmem_limit_bytes=16 * 1024 * 1024)
VMEM = pl.BlockSpec(memory_space=pltpu.VMEM)
SMEM = pl.BlockSpec(memory_space=pltpu.SMEM)
ANY = pl.BlockSpec(memory_space=pl.ANY)
HBM = pl.BlockSpec(memory_space=pltpu.HBM)


def chunk_pieces(z):
    base = z * CHUNK
    if z % 2 == 0:
        return (base, FULL), (base + FULL, HALF)
    return (base + HALF, FULL), (base, HALF)


def dot(a, b, ca, cb):
    return lax.dot_general(a, b, (((ca,), (cb,)), ((), ())), preferred_element_type=f32)


def shared_head(z):
    return z // 2 * (2 * CHUNK) + FULL


def chunk_rows(z):
    odd = lax.rem(z, 2)
    base = z * CHUNK
    return pl.multiple_of(base + odd * HALF, HALF), pl.multiple_of(base + (1 - odd) * FULL, HALF)


def fetches(sources, buffers, sems):
    copies = [pltpu.make_async_copy(a, b, sems.at[i]) for i, (a, b) in enumerate(zip(sources, buffers))]
    for copy in copies:
        copy.start()
    return copies


def in_hbm(*arrays):
    return [pltpu.with_memory_space_constraint(a, pltpu.HBM) for a in arrays]


def key_kernel(me_ref, x_hbm, w_hbm, n_ref, *rest):
    outs, (x_ref, w_ref, t_ref, sems) = rest[:Z], rest[Z:]
    copy_x, copy_w = fetches((x_hbm, w_hbm), (x_ref, w_ref), sems)
    copy_x.wait()
    x = x_ref[...].astype(f32)
    centred = x - jnp.mean(x, axis=-1, keepdims=True)
    var = jnp.mean(centred * centred, axis=-1, keepdims=True)
    normed = (centred * lax.rsqrt(var + 1e-05)).astype(bf16)
    for h in range(2):
        n_ref[h] = normed[:, h * SUB : (h + 1) * SUB, :]
    copy_w.wait()
    t_ref[...] = dot(w_ref[...], n_ref[...].reshape(ROWS * RES, EMBED), 0, 1).astype(bf16)
    for s, out in enumerate(outs):
        z = lax.rem(me_ref[2] + s, Z)
        first, odd = shared_head(z), lax.rem(z, 2)
        lanes = pl.ds(pl.multiple_of(odd * TOKENS, TOKENS), TOKENS)
        out[0:FULL, :] = t_ref[pl.ds(chunk_rows(z)[0], FULL), :]
        for d in range(2):
            rows = pl.ds(pl.multiple_of(first + d * HALF, HALF), HALF)
            out[FULL:CHUNK, d * TOKENS : (d + 1) * TOKENS] = t_ref[rows, lanes]


def key_chunks(me, x, w):
    n, *k = pl.pallas_call(
        key_kernel,
        out_shape=(jax.ShapeDtypeStruct((2, ROWS, SUB, EMBED), bf16),)
        + (jax.ShapeDtypeStruct((CHUNK, ROWS * RES), bf16),) * Z,
        in_specs=[SMEM, ANY, ANY],
        out_specs=(VMEM,) * (1 + Z),
        scratch_shapes=[
            pltpu.VMEM((ROWS, RES, EMBED), bf16),
            pltpu.VMEM((EMBED, EMBED), bf16),
            pltpu.VMEM((EMBED, ROWS * RES), bf16),
            pltpu.SemaphoreType.DMA((2,)),
        ],
        compiler_params=PARAMS,
    )(me, *in_hbm(x, w))
    return n, k


def query_kernel(n_ref, w_ref, q_ref):
    for c in range(2):
        t = dot(w_ref[...], n_ref[c].reshape(TOKENS, EMBED), 0, 1).astype(bf16)
        for z in range(Z):
            a, b = chunk_pieces(z)[0][0], shared_head(z)
            q_ref[2 * z + c, 0:FULL, :] = t[a : a + FULL]
            q_ref[2 * z + c, FULL:, :] = t[b : b + FULL]


def query_chunks(n, w):
    return pl.pallas_call(
        query_kernel,
        out_shape=jax.ShapeDtypeStruct((2 * Z, 2 * FULL, TOKENS), bf16),
        in_specs=[VMEM] * 2,
        out_specs=VMEM,
        compiler_params=PARAMS,
        cost_estimate=PROJECTION,
    )(n, w)


def value_kernel(me_ref, n_ref, w_ref, *rest):
    outs, t_ref = rest[:Z], rest[Z]
    t_ref[...] = dot(w_ref[...], n_ref[...].reshape(ROWS * RES, EMBED), 0, 1).astype(bf16)
    for s, out in enumerate(outs):
        full, half = chunk_rows(lax.rem(me_ref[2] + s, Z))
        out[0:FULL, :] = t_ref[pl.ds(full, FULL), :]
        out[FULL:CHUNK, :] = t_ref[pl.ds(half, HALF), :]


def value_chunks(me, n, w):
    return pl.pallas_call(
        value_kernel,
        out_shape=(jax.ShapeDtypeStruct((CHUNK, ROWS * RES), bf16),) * Z,
        in_specs=[SMEM, VMEM, VMEM],
        out_specs=(VMEM,) * Z,
        scratch_shapes=[pltpu.VMEM((EMBED, ROWS * RES), bf16)],
        compiler_params=PARAMS,
        cost_estimate=PROJECTION,
    )(me, n, w)


def lay_keys(me, own, other, kf, kh):
    where = [lax.rem(me - z + Z, Z) for z in range(Z)]
    for cr, ref in enumerate((own, other)):
        for r in range(ROWS):
            n = (cr * ROWS + r) * FULL
            whole = [ref[z, 0:FULL, h * TOKENS + r * SUB : h * TOKENS + (r + 1) * SUB] for z in where for h in range(2)]
            kf[n : n + FULL, :] = jnp.concatenate(whole, axis=1)
            for d in range(2):
                first = d * TOKENS + r * SUB
                shared = [ref[z, FULL:CHUNK, first : first + SUB] for z in where]
                kh[n + d * HALF : n + (d + 1) * HALF, :] = jnp.concatenate(shared, axis=1)


def keys_kernel(me_ref, own, other, kf, kh):
    lay_keys(me_ref[2], own, other, kf, kh)


def keys_laid(me, own, other):
    return pl.pallas_call(
        keys_kernel,
        out_shape=tuple(jax.ShapeDtypeStruct(s, bf16) for s in KEY_SHAPES),
        in_specs=[SMEM, VMEM, VMEM],
        out_specs=(VMEM,) * 2,
        compiler_params=PARAMS,
        cost_estimate=LAYOUT,
    )(me, own, other)


def score_kernel(me_ref, q_ref, kf0, kh0, own, other, out, qf, qh, kf1, kh1):
    lay_keys(me_ref[2], own, other, kf1, kh1)
    for cr in range(2):
        c = jnp.bitwise_xor(me_ref[1], cr)
        queries = [q_ref[2 * p + c] for p in range(PEERS)]
        for r in range(ROWS):
            n = (cr * ROWS + r) * FULL
            t = jnp.concatenate([b[:, r * SUB : (r + 1) * SUB] for b in queries], axis=1)
            qf[n : n + FULL, :] = t[:FULL]
            qh[n : n + FULL, :] = t[FULL:]
    first = 0
    for a, b in ((qf, kf0), (qf, kf1), (qh, kh0), (qh, kh1)):
        t = dot(a[...], b[...], 0, 0)
        for p in range(PEERS):
            out[p, :, first : first + t.shape[1]] = t[p * SUB : (p + 1) * SUB]
        first += t.shape[1]


def score(me, q, laid, own, other):
    rows = 2 * ROWS * FULL
    return pl.pallas_call(
        score_kernel,
        out_shape=jax.ShapeDtypeStruct((PEERS, SUB, LOGITS), f32),
        in_specs=[SMEM] + [VMEM] * 5,
        out_specs=VMEM,
        scratch_shapes=[pltpu.VMEM((rows, QUERIES), bf16)] * 2 + [pltpu.VMEM(s, bf16) for s in KEY_SHAPES],
        compiler_params=PARAMS,
    )(me, q, *laid, own, other)


def total_kernel(parts, full, half):
    t = parts[0]
    for p in range(1, PEERS):
        t = t + parts[p]
    full[...] = t[:, :KEYS]
    half[...] = t[:, KEYS:]


def total(parts):
    return pl.pallas_call(
        total_kernel,
        out_shape=tuple(jax.ShapeDtypeStruct((SUB, n), f32) for n in (KEYS, KEYS // 2)),
        in_specs=[VMEM],
        out_specs=(VMEM,) * 2,
        compiler_params=PARAMS,
    )(parts)


def softmax_kernel(factor, full, half, other, out):
    for i, logits in enumerate((full[...], jnp.concatenate([half[...], other[...]], axis=1))):
        logits = logits * factor
        powered = jnp.exp(logits - jnp.max(logits, axis=-1, keepdims=True))
        probs = (powered / jnp.sum(powered, axis=-1, keepdims=True)).astype(bf16)
        for p in range(PEERS):
            out[p, i] = probs


def softmax(factor, full, half, other):
    return pl.pallas_call(
        functools.partial(softmax_kernel, factor),
        out_shape=jax.ShapeDtypeStruct((PEERS, 2, SUB, KEYS), bf16),
        in_specs=[VMEM] * 3,
        out_specs=VMEM,
        compiler_params=PARAMS,
    )(full, half, other)


def values_kernel(me_ref, v00, v01, v10, v11, vf, vh):
    z = me_ref[2]
    odd = lax.rem(z, 2)
    where = [lax.rem(z - source + Z, Z) for source in range(Z)]
    for cr, refs in enumerate(((v00, v01), (v10, v11))):
        halves = [
            ref[i, FULL:CHUNK, pl.ds(pl.multiple_of(h * TOKENS, TOKENS), TOKENS)]
            for h in (odd, 1 - odd)
            for ref in refs
            for i in where
        ]
        whole = [ref[i, 0:FULL, h * TOKENS : (h + 1) * TOKENS] for ref in refs for i in where for h in range(2)]
        for r in range(ROWS):
            n = cr * ROWS + r
            lanes = slice(r * SUB, (r + 1) * SUB)
            vf[n * FULL : (n + 1) * FULL, :] = jnp.concatenate([b[:, lanes] for b in whole], axis=1)
            vh[n * HALF : (n + 1) * HALF, :] = jnp.concatenate([b[:, lanes] for b in halves], axis=1)


def values_laid(me, vs):
    return pl.pallas_call(
        values_kernel,
        out_shape=tuple(jax.ShapeDtypeStruct((2 * ROWS * n, KEYS), bf16) for n in (FULL, HALF)),
        in_specs=[SMEM] + [VMEM] * 4,
        out_specs=(VMEM,) * 2,
        compiler_params=PARAMS,
        cost_estimate=LAYOUT,
    )(me, *vs)


def mix_kernel(me_ref, vf, vh, p_ref, o_ref):
    core = me_ref[1]
    for i, (v, first, n) in enumerate(((vf, 0, FULL), (vh, FULL, HALF))):
        probs = p_ref[:, i].reshape(QUERIES, KEYS)
        for cr in range(2):
            c = jnp.bitwise_xor(core, cr)
            mixed = dot(v[cr * ROWS * n : (cr + 1) * ROWS * n, :], probs, 1, 1).astype(bf16)
            for s in range(PEERS):
                o_ref[2 * s + c, first : first + n, :] = jnp.concatenate(
                    [mixed[r * n : (r + 1) * n, s * SUB : (s + 1) * SUB] for r in range(ROWS)], axis=1
                )


def mix(me, laid, probs):
    return pl.pallas_call(
        mix_kernel,
        out_shape=jax.ShapeDtypeStruct((2 * Z, CHUNK, ROWS * SUB), bf16),
        in_specs=[SMEM] + [VMEM] * 3,
        out_specs=VMEM,
        compiler_params=PARAMS,
    )(me, *laid, probs)


def final_kernel(m_ref, w_ref, o_ref, t_ref):
    for c in range(2):
        for z in range(Z):
            (a, na), (b, nb) = chunk_pieces(z)
            t_ref[a : a + na, :] = m_ref[2 * z + c, 0:FULL, :]
            t_ref[b : b + nb, :] = m_ref[2 * z + c, FULL:CHUNK, :]
        attended = dot(t_ref[...], w_ref[...], 0, 0).astype(bf16)
        o_ref[:, c * SUB : (c + 1) * SUB, :] = attended.reshape(ROWS, SUB, EMBED)


def final(m, w):
    return pl.pallas_call(
        final_kernel,
        out_shape=jax.ShapeDtypeStruct((ROWS, RES, EMBED), bf16),
        in_specs=[VMEM] * 2,
        out_specs=VMEM,
        scratch_shapes=[pltpu.VMEM((EMBED, ROWS * SUB), bf16)],
        compiler_params=PARAMS,
    )(m, w)


def flip(x, axes, n, s):
    return lax.ppermute(x, axes, [(i, i ^ s) for i in range(n)])


def gather4(own):
    far = flip(own, "xl", 2, 1)
    return own, far, flip(own, "c", 2, 1), flip(far, "c", 2, 1)


def shift(x, s):
    return lax.ppermute(x, "z", [(i, (i + s) % Z) for i in range(Z)])


def local(x, wq, wk, wv, wf):
    me = jnp.stack([lax.axis_index(("y", "xh")), lax.axis_index("c"), lax.axis_index("z")])
    me = me.astype(jnp.int32)
    n, k = key_chunks(me, x, wk)
    for s in (1, 7, 2, 6, 3, 5, 4):
        k[s] = shift(k[s], s)
    q, k[1], k[7], k[2], k[6] = lax.optimization_barrier((query_chunks(n, wq), k[1], k[7], k[2], k[6]))
    q = lax.all_to_all(q, ("z", "c"), 0, 0, tiled=True)
    v = list(value_chunks(me, n, wv))
    k = jnp.stack(k)
    k_far, v[4] = lax.optimization_barrier((flip(k, "xl", 2, 1), v[4]))
    for s in (3, 5):
        v[s] = shift(v[s], s)
    scores = score(me, q, keys_laid(me, k, flip(k, "c", 2, 1)), k_far, flip(k_far, "c", 2, 1))
    *v, scores = lax.optimization_barrier((*v, scores))
    parts = lax.all_to_all(scores, ("y", "xh"), 0, 0, tiled=True)
    for s in (4, 2, 6, 1, 7):
        v[s] = shift(v[s], s)
    full, half = total(parts)
    rows = ROWS * 2 * PEERS
    probs = softmax(1.0 / math.sqrt(DH * rows), full, half, flip(half, "z", Z, 1))
    probs = lax.all_to_all(probs, ("y", "xh"), 0, 0, tiled=True)
    laid = values_laid(me, gather4(jnp.stack(v)))
    mixed = lax.all_to_all(mix(me, laid, probs), ("z", "c"), 0, 0, tiled=True)
    return final(mixed, wf)


def solution(mesh):
    fine = Mesh(mesh.devices.reshape(4, 2, 2, 8, 2), ("y", "xh", "c", "z", "xl"))
    spec = P(("y", "xh", "c"), ("z", "xl"), None)
    return jax.shard_map(
        local,
        mesh=fine,
        in_specs=(spec, P(), P(), P(), P()),
        out_specs=spec,
        check_vma=False,
    )
```

```python
import functools
import math

import jax
import jax.numpy as jnp
from jax import lax
from jax.experimental import pallas as pl
from jax.experimental.pallas import tpu as pltpu
from jax.sharding import Mesh, PartitionSpec as P

H = 12
DH = 64
EMBED = 768
ROWS = 8
RES = 64
Z = 8
CHUNK = EMBED // Z
FULL = DH
HALF = CHUNK - DH
PEERS = 8
SUB = RES // 2
TOKENS = ROWS * SUB
QUERIES = Z * SUB
KEYS = 2 * Z * RES
LOGITS = KEYS + KEYS // 2

f32 = jnp.float32
bf16 = jnp.bfloat16
PARAMS = pltpu.CompilerParams(vmem_limit_bytes=16 * 1024 * 1024)
PROJECTION = pl.CostEstimate(
    flops=2 * ROWS * RES * EMBED * EMBED, bytes_accessed=2 * EMBED * (EMBED + 2 * ROWS * RES), transcendentals=0
)
LAYOUT = pl.CostEstimate(flops=0, bytes_accessed=16 * ROWS * RES * EMBED, transcendentals=0)
KEY_SHAPES = ((2 * ROWS * FULL, KEYS // 2), (2 * ROWS * FULL, KEYS // 4))
WIDE = pltpu.CompilerParams(vmem_limit_bytes=16 * 1024 * 1024)
VMEM = pl.BlockSpec(memory_space=pltpu.VMEM)
SMEM = pl.BlockSpec(memory_space=pltpu.SMEM)
ANY = pl.BlockSpec(memory_space=pl.ANY)
HBM = pl.BlockSpec(memory_space=pltpu.HBM)


def chunk_pieces(z):
    base = z * CHUNK
    if z % 2 == 0:
        return (base, FULL), (base + FULL, HALF)
    return (base + HALF, FULL), (base, HALF)


def dot(a, b, ca, cb):
    return lax.dot_general(a, b, (((ca,), (cb,)), ((), ())), preferred_element_type=f32)


def shared_head(z):
    return z // 2 * (2 * CHUNK) + FULL


def chunk_rows(z):
    odd = lax.rem(z, 2)
    base = z * CHUNK
    return pl.multiple_of(base + odd * HALF, HALF), pl.multiple_of(base + (1 - odd) * FULL, HALF)


def fetches(sources, buffers, sems):
    copies = [pltpu.make_async_copy(a, b, sems.at[i]) for i, (a, b) in enumerate(zip(sources, buffers))]
    for copy in copies:
        copy.start()
    return copies


def in_hbm(*arrays):
    return [pltpu.with_memory_space_constraint(a, pltpu.HBM) for a in arrays]


def key_kernel(me_ref, x_hbm, w_hbm, n_ref, *rest):
    outs, (x_ref, w_ref, t_ref, sems) = rest[:Z], rest[Z:]
    copy_x, copy_w = fetches((x_hbm, w_hbm), (x_ref, w_ref), sems)
    copy_x.wait()
    x = x_ref[...].astype(f32)
    centred = x - jnp.mean(x, axis=-1, keepdims=True)
    var = jnp.mean(centred * centred, axis=-1, keepdims=True)
    normed = (centred * lax.rsqrt(var + 1e-05)).astype(bf16)
    for h in range(2):
        n_ref[h] = normed[:, h * SUB : (h + 1) * SUB, :]
    copy_w.wait()
    t_ref[...] = dot(w_ref[...], n_ref[...].reshape(ROWS * RES, EMBED), 0, 1).astype(bf16)
    for s, out in enumerate(outs):
        z = lax.rem(me_ref[2] + s, Z)
        first, odd = shared_head(z), lax.rem(z, 2)
        lanes = pl.ds(pl.multiple_of(odd * TOKENS, TOKENS), TOKENS)
        out[0:FULL, :] = t_ref[pl.ds(chunk_rows(z)[0], FULL), :]
        for d in range(2):
            rows = pl.ds(pl.multiple_of(first + d * HALF, HALF), HALF)
            out[FULL:CHUNK, d * TOKENS : (d + 1) * TOKENS] = t_ref[rows, lanes]


def key_chunks(me, x, w):
    n, *k = pl.pallas_call(
        key_kernel,
        out_shape=(jax.ShapeDtypeStruct((2, ROWS, SUB, EMBED), bf16),)
        + (jax.ShapeDtypeStruct((CHUNK, ROWS * RES), bf16),) * Z,
        in_specs=[SMEM, ANY, ANY],
        out_specs=(VMEM,) * (1 + Z),
        scratch_shapes=[
            pltpu.VMEM((ROWS, RES, EMBED), bf16),
            pltpu.VMEM((EMBED, EMBED), bf16),
            pltpu.VMEM((EMBED, ROWS * RES), bf16),
            pltpu.SemaphoreType.DMA((2,)),
        ],
        compiler_params=PARAMS,
    )(me, *in_hbm(x, w))
    return n, k


def query_kernel(n_ref, w_ref, q_ref):
    for c in range(2):
        t = dot(w_ref[...], n_ref[c].reshape(TOKENS, EMBED), 0, 1).astype(bf16)
        for z in range(Z):
            a, b = chunk_pieces(z)[0][0], shared_head(z)
            q_ref[2 * z + c, 0:FULL, :] = t[a : a + FULL]
            q_ref[2 * z + c, FULL:, :] = t[b : b + FULL]


def query_chunks(n, w):
    return pl.pallas_call(
        query_kernel,
        out_shape=jax.ShapeDtypeStruct((2 * Z, 2 * FULL, TOKENS), bf16),
        in_specs=[VMEM] * 2,
        out_specs=VMEM,
        compiler_params=PARAMS,
        cost_estimate=PROJECTION,
    )(n, w)


def value_kernel(me_ref, n_ref, w_ref, *rest):
    outs, t_ref = rest[:Z], rest[Z]
    t_ref[...] = dot(w_ref[...], n_ref[...].reshape(ROWS * RES, EMBED), 0, 1).astype(bf16)
    for s, out in enumerate(outs):
        full, half = chunk_rows(lax.rem(me_ref[2] + s, Z))
        out[0:FULL, :] = t_ref[pl.ds(full, FULL), :]
        out[FULL:CHUNK, :] = t_ref[pl.ds(half, HALF), :]


def value_chunks(me, n, w):
    return pl.pallas_call(
        value_kernel,
        out_shape=(jax.ShapeDtypeStruct((CHUNK, ROWS * RES), bf16),) * Z,
        in_specs=[SMEM, VMEM, VMEM],
        out_specs=(VMEM,) * Z,
        scratch_shapes=[pltpu.VMEM((EMBED, ROWS * RES), bf16)],
        compiler_params=PARAMS,
        cost_estimate=PROJECTION,
    )(me, n, w)


def lay_keys(me, own, other, kf, kh):
    where = [lax.rem(me - z + Z, Z) for z in range(Z)]
    for cr, ref in enumerate((own, other)):
        for r in range(ROWS):
            n = (cr * ROWS + r) * FULL
            whole = [ref[z, 0:FULL, h * TOKENS + r * SUB : h * TOKENS + (r + 1) * SUB] for z in where for h in range(2)]
            kf[n : n + FULL, :] = jnp.concatenate(whole, axis=1)
            for d in range(2):
                first = d * TOKENS + r * SUB
                shared = [ref[z, FULL:CHUNK, first : first + SUB] for z in where]
                kh[n + d * HALF : n + (d + 1) * HALF, :] = jnp.concatenate(shared, axis=1)


def keys_kernel(me_ref, own, other, kf, kh):
    lay_keys(me_ref[2], own, other, kf, kh)


def keys_laid(me, own, other):
    return pl.pallas_call(
        keys_kernel,
        out_shape=tuple(jax.ShapeDtypeStruct(s, bf16) for s in KEY_SHAPES),
        in_specs=[SMEM, VMEM, VMEM],
        out_specs=(VMEM,) * 2,
        compiler_params=PARAMS,
        cost_estimate=LAYOUT,
    )(me, own, other)


def score_kernel(me_ref, q_hbm, kf_hbm, kh_hbm, own_hbm, other_hbm, out, qf, qh, kf1, kh1, *rest):
    own, other, q_ref, kf0, kh0, sems = rest
    copies = fetches((own_hbm, other_hbm, q_hbm, kf_hbm, kh_hbm), rest[:5], sems)
    for copy in copies[:2]:
        copy.wait()
    lay_keys(me_ref[2], own, other, kf1, kh1)
    for copy in copies[2:]:
        copy.wait()
    for cr in range(2):
        c = jnp.bitwise_xor(me_ref[1], cr)
        queries = [q_ref[2 * p + c] for p in range(PEERS)]
        for r in range(ROWS):
            n = (cr * ROWS + r) * FULL
            t = jnp.concatenate([b[:, r * SUB : (r + 1) * SUB] for b in queries], axis=1)
            qf[n : n + FULL, :] = t[:FULL]
            qh[n : n + FULL, :] = t[FULL:]
    first = 0
    for a, b in ((qf, kf0), (qf, kf1), (qh, kh0), (qh, kh1)):
        t = dot(a[...], b[...], 0, 0)
        for p in range(PEERS):
            out[p, :, first : first + t.shape[1]] = t[p * SUB : (p + 1) * SUB]
        first += t.shape[1]


def score(me, q, laid, own, other):
    rows = 2 * ROWS * FULL
    return pl.pallas_call(
        score_kernel,
        out_shape=jax.ShapeDtypeStruct((PEERS, SUB, LOGITS), f32),
        in_specs=[SMEM] + [ANY] * 5,
        out_specs=VMEM,
        scratch_shapes=[pltpu.VMEM((rows, QUERIES), bf16)] * 2
        + [pltpu.VMEM(s, bf16) for s in KEY_SHAPES]
        + [pltpu.VMEM(a.shape, bf16) for a in (own, other, q, *laid)]
        + [pltpu.SemaphoreType.DMA((5,))],
        compiler_params=PARAMS,
    )(me, *in_hbm(q), *laid, *in_hbm(own), other)


def total_kernel(parts, full, half):
    t = parts[0]
    for p in range(1, PEERS):
        t = t + parts[p]
    full[...] = t[:, :KEYS]
    half[...] = t[:, KEYS:]


def total(parts):
    return pl.pallas_call(
        total_kernel,
        out_shape=tuple(jax.ShapeDtypeStruct((SUB, n), f32) for n in (KEYS, KEYS // 2)),
        in_specs=[VMEM],
        out_specs=(VMEM,) * 2,
        compiler_params=PARAMS,
    )(parts)


def softmax_kernel(factor, full, half, other, out):
    for i, logits in enumerate((full[...], jnp.concatenate([half[...], other[...]], axis=1))):
        logits = logits * factor
        powered = jnp.exp(logits - jnp.max(logits, axis=-1, keepdims=True))
        probs = (powered / jnp.sum(powered, axis=-1, keepdims=True)).astype(bf16)
        for p in range(PEERS):
            out[p, i] = probs


def softmax(factor, full, half, other):
    return pl.pallas_call(
        functools.partial(softmax_kernel, factor),
        out_shape=jax.ShapeDtypeStruct((PEERS, 2, SUB, KEYS), bf16),
        in_specs=[VMEM] * 3,
        out_specs=VMEM,
        compiler_params=PARAMS,
    )(full, half, other)


def values_kernel(me_ref, *refs):
    (vf, vh), (v00, v01, v10, v11), sems = refs[4:6], refs[6:10], refs[10]
    for copy in fetches(refs[:4], refs[6:10], sems):
        copy.wait()
    z = me_ref[2]
    odd = lax.rem(z, 2)
    where = [lax.rem(z - source + Z, Z) for source in range(Z)]
    for cr, refs in enumerate(((v00, v01), (v10, v11))):
        halves = [
            ref[i, FULL:CHUNK, pl.ds(pl.multiple_of(h * TOKENS, TOKENS), TOKENS)]
            for h in (odd, 1 - odd)
            for ref in refs
            for i in where
        ]
        whole = [ref[i, 0:FULL, h * TOKENS : (h + 1) * TOKENS] for ref in refs for i in where for h in range(2)]
        for r in range(ROWS):
            n = cr * ROWS + r
            lanes = slice(r * SUB, (r + 1) * SUB)
            vf[n * FULL : (n + 1) * FULL, :] = jnp.concatenate([b[:, lanes] for b in whole], axis=1)
            vh[n * HALF : (n + 1) * HALF, :] = jnp.concatenate([b[:, lanes] for b in halves], axis=1)


def values_laid(me, vs):
    return pl.pallas_call(
        values_kernel,
        out_shape=tuple(jax.ShapeDtypeStruct((2 * ROWS * n, KEYS), bf16) for n in (FULL, HALF)),
        in_specs=[SMEM] + [ANY] * 4,
        out_specs=(VMEM,) * 2,
        scratch_shapes=[pltpu.VMEM(v.shape, bf16) for v in vs] + [pltpu.SemaphoreType.DMA((4,))],
        compiler_params=PARAMS,
        cost_estimate=LAYOUT,
    )(me, *in_hbm(*vs[:2]), *vs[2:])


def mix_kernel(me_ref, vf, vh, p_ref, o_ref):
    core = me_ref[1]
    for i, (v, first, n) in enumerate(((vf, 0, FULL), (vh, FULL, HALF))):
        probs = p_ref[:, i].reshape(QUERIES, KEYS)
        for cr in range(2):
            c = jnp.bitwise_xor(core, cr)
            mixed = dot(v[cr * ROWS * n : (cr + 1) * ROWS * n, :], probs, 1, 1).astype(bf16)
            for s in range(PEERS):
                o_ref[2 * s + c, first : first + n, :] = jnp.concatenate(
                    [mixed[r * n : (r + 1) * n, s * SUB : (s + 1) * SUB] for r in range(ROWS)], axis=1
                )


def mix(me, laid, probs):
    return pl.pallas_call(
        mix_kernel,
        out_shape=jax.ShapeDtypeStruct((2 * Z, CHUNK, ROWS * SUB), bf16),
        in_specs=[SMEM] + [VMEM] * 3,
        out_specs=VMEM,
        compiler_params=PARAMS,
    )(me, *laid, probs)


def final_kernel(m_ref, w_ref, o_ref, t_ref):
    for c in range(2):
        for z in range(Z):
            (a, na), (b, nb) = chunk_pieces(z)
            t_ref[a : a + na, :] = m_ref[2 * z + c, 0:FULL, :]
            t_ref[b : b + nb, :] = m_ref[2 * z + c, FULL:CHUNK, :]
        attended = dot(t_ref[...], w_ref[...], 0, 0).astype(bf16)
        o_ref[:, c * SUB : (c + 1) * SUB, :] = attended.reshape(ROWS, SUB, EMBED)


def final(m, w):
    return pl.pallas_call(
        final_kernel,
        out_shape=jax.ShapeDtypeStruct((ROWS, RES, EMBED), bf16),
        in_specs=[VMEM] * 2,
        out_specs=VMEM,
        scratch_shapes=[pltpu.VMEM((EMBED, ROWS * SUB), bf16)],
        compiler_params=PARAMS,
    )(m, w)


def flip(x, axes, n, s):
    return lax.ppermute(x, axes, [(i, i ^ s) for i in range(n)])


def gather4(own):
    far = flip(own, "xl", 2, 1)
    return own, far, flip(own, "c", 2, 1), flip(far, "c", 2, 1)


def shift(x, s):
    return lax.ppermute(x, "z", [(i, (i + s) % Z) for i in range(Z)])


def local(x, wq, wk, wv, wf):
    me = jnp.stack([lax.axis_index(("y", "xh")), lax.axis_index("c"), lax.axis_index("z")])
    me = me.astype(jnp.int32)
    n, k = key_chunks(me, x, wk)
    for s in (1, 7, 2, 6, 3, 5, 4):
        k[s] = shift(k[s], s)
    q, k[1], k[7], k[2], k[6] = lax.optimization_barrier((query_chunks(n, wq), k[1], k[7], k[2], k[6]))
    q = lax.all_to_all(q, ("z", "c"), 0, 0, tiled=True)
    v = list(value_chunks(me, n, wv))
    k = jnp.stack(k)
    near, shared = keys_laid(me, k, flip(k, "c", 2, 1))
    k_far, v[4], shared = lax.optimization_barrier((flip(k, "xl", 2, 1), v[4], shared))
    for s in (3, 5):
        v[s] = shift(v[s], s)
    scores = score(me, q, (near, shared), k_far, flip(k_far, "c", 2, 1))
    *v, scores = lax.optimization_barrier((*v, scores))
    parts = lax.all_to_all(scores, ("y", "xh"), 0, 0, tiled=True)
    for s in (4, 2, 6, 1, 7):
        v[s] = shift(v[s], s)
    full, half = total(parts)
    rows = ROWS * 2 * PEERS
    probs = softmax(1.0 / math.sqrt(DH * rows), full, half, flip(half, "z", Z, 1))
    probs = lax.all_to_all(probs, ("y", "xh"), 0, 0, tiled=True)
    laid = values_laid(me, gather4(jnp.stack(v)))
    mixed = lax.all_to_all(mix(me, laid, probs), ("z", "c"), 0, 0, tiled=True)
    return final(mixed, wf)


def solution(mesh):
    fine = Mesh(mesh.devices.reshape(4, 2, 2, 8, 2), ("y", "xh", "c", "z", "xl"))
    spec = P(("y", "xh", "c"), ("z", "xl"), None)
    return jax.shard_map(
        local,
        mesh=fine,
        in_specs=(spec, P(), P(), P(), P()),
        out_specs=spec,
        check_vma=False,
    )
```

```python
import functools
import math

import jax
import jax.numpy as jnp
from jax import lax
from jax.experimental import pallas as pl
from jax.experimental.pallas import tpu as pltpu
from jax.sharding import Mesh, PartitionSpec as P

H = 12
DH = 64
EMBED = 768
ROWS = 8
RES = 64
Z = 8
CHUNK = EMBED // Z
FULL = DH
HALF = CHUNK - DH
PEERS = 8
SUB = RES // 2
TOKENS = ROWS * SUB
QUERIES = Z * SUB
KEYS = 2 * Z * RES
LOGITS = KEYS + KEYS // 2

f32 = jnp.float32
bf16 = jnp.bfloat16
PARAMS = pltpu.CompilerParams(vmem_limit_bytes=16 * 1024 * 1024)
PROJECTION = pl.CostEstimate(
    flops=2 * ROWS * RES * EMBED * EMBED, bytes_accessed=2 * EMBED * (EMBED + 2 * ROWS * RES), transcendentals=0
)
LAYOUT = pl.CostEstimate(flops=0, bytes_accessed=16 * ROWS * RES * EMBED, transcendentals=0)
KEY_SHAPES = ((2 * ROWS * FULL, KEYS // 2), (2 * ROWS * FULL, KEYS // 4))
WIDE = pltpu.CompilerParams(vmem_limit_bytes=16 * 1024 * 1024)
VMEM = pl.BlockSpec(memory_space=pltpu.VMEM)
SMEM = pl.BlockSpec(memory_space=pltpu.SMEM)
ANY = pl.BlockSpec(memory_space=pl.ANY)
HBM = pl.BlockSpec(memory_space=pltpu.HBM)


def chunk_pieces(z):
    base = z * CHUNK
    if z % 2 == 0:
        return (base, FULL), (base + FULL, HALF)
    return (base + HALF, FULL), (base, HALF)


def dot(a, b, ca, cb):
    return lax.dot_general(a, b, (((ca,), (cb,)), ((), ())), preferred_element_type=f32)


def shared_head(z):
    return z // 2 * (2 * CHUNK) + FULL


def chunk_rows(z):
    odd = lax.rem(z, 2)
    base = z * CHUNK
    return pl.multiple_of(base + odd * HALF, HALF), pl.multiple_of(base + (1 - odd) * FULL, HALF)


def fetches(sources, buffers, sems):
    copies = [pltpu.make_async_copy(a, b, sems.at[i]) for i, (a, b) in enumerate(zip(sources, buffers))]
    for copy in copies:
        copy.start()
    return copies


def in_hbm(*arrays):
    return [pltpu.with_memory_space_constraint(a, pltpu.HBM) for a in arrays]


def key_kernel(me_ref, x_hbm, w_hbm, n_ref, *rest):
    outs, (x_ref, w_ref, t_ref, sems) = rest[:Z], rest[Z:]
    copy_x, copy_w = fetches((x_hbm, w_hbm), (x_ref, w_ref), sems)
    copy_x.wait()
    x = x_ref[...].astype(f32)
    centred = x - jnp.mean(x, axis=-1, keepdims=True)
    var = jnp.mean(centred * centred, axis=-1, keepdims=True)
    normed = (centred * lax.rsqrt(var + 1e-05)).astype(bf16)
    for h in range(2):
        n_ref[h] = normed[:, h * SUB : (h + 1) * SUB, :]
    copy_w.wait()
    t_ref[...] = dot(w_ref[...], n_ref[...].reshape(ROWS * RES, EMBED), 0, 1).astype(bf16)
    for s, out in enumerate(outs):
        z = lax.rem(me_ref[2] + s, Z)
        first, odd = shared_head(z), lax.rem(z, 2)
        lanes = pl.ds(pl.multiple_of(odd * TOKENS, TOKENS), TOKENS)
        out[0:FULL, :] = t_ref[pl.ds(chunk_rows(z)[0], FULL), :]
        for d in range(2):
            rows = pl.ds(pl.multiple_of(first + d * HALF, HALF), HALF)
            out[FULL:CHUNK, d * TOKENS : (d + 1) * TOKENS] = t_ref[rows, lanes]


def key_chunks(me, x, w):
    n, *k = pl.pallas_call(
        key_kernel,
        out_shape=(jax.ShapeDtypeStruct((2, ROWS, SUB, EMBED), bf16),)
        + (jax.ShapeDtypeStruct((CHUNK, ROWS * RES), bf16),) * Z,
        in_specs=[SMEM, ANY, ANY],
        out_specs=(VMEM,) * (1 + Z),
        scratch_shapes=[
            pltpu.VMEM((ROWS, RES, EMBED), bf16),
            pltpu.VMEM((EMBED, EMBED), bf16),
            pltpu.VMEM((EMBED, ROWS * RES), bf16),
            pltpu.SemaphoreType.DMA((2,)),
        ],
        compiler_params=PARAMS,
    )(me, *in_hbm(x, w))
    return n, k


def query_kernel(n_ref, w_ref, q_ref):
    for c in range(2):
        t = dot(w_ref[...], n_ref[c].reshape(TOKENS, EMBED), 0, 1).astype(bf16)
        for z in range(Z):
            a, b = chunk_pieces(z)[0][0], shared_head(z)
            q_ref[2 * z + c, 0:FULL, :] = t[a : a + FULL]
            q_ref[2 * z + c, FULL:, :] = t[b : b + FULL]


def query_chunks(n, w):
    return pl.pallas_call(
        query_kernel,
        out_shape=jax.ShapeDtypeStruct((2 * Z, 2 * FULL, TOKENS), bf16),
        in_specs=[VMEM] * 2,
        out_specs=VMEM,
        compiler_params=PARAMS,
        cost_estimate=PROJECTION,
    )(n, w)


def value_kernel(me_ref, n_ref, w_ref, *rest):
    outs, t_ref = rest[:Z], rest[Z]
    t_ref[...] = dot(w_ref[...], n_ref[...].reshape(ROWS * RES, EMBED), 0, 1).astype(bf16)
    for s, out in enumerate(outs):
        full, half = chunk_rows(lax.rem(me_ref[2] + s, Z))
        out[0:FULL, :] = t_ref[pl.ds(full, FULL), :]
        out[FULL:CHUNK, :] = t_ref[pl.ds(half, HALF), :]


def value_chunks(me, n, w):
    return pl.pallas_call(
        value_kernel,
        out_shape=(jax.ShapeDtypeStruct((CHUNK, ROWS * RES), bf16),) * Z,
        in_specs=[SMEM, VMEM, VMEM],
        out_specs=(VMEM,) * Z,
        scratch_shapes=[pltpu.VMEM((EMBED, ROWS * RES), bf16)],
        compiler_params=PARAMS,
        cost_estimate=PROJECTION,
    )(me, n, w)


def lay_keys(me, own, other, kf, kh):
    where = [lax.rem(me - z + Z, Z) for z in range(Z)]
    for cr, ref in enumerate((own, other)):
        for r in range(ROWS):
            n = (cr * ROWS + r) * FULL
            whole = [ref[z, 0:FULL, h * TOKENS + r * SUB : h * TOKENS + (r + 1) * SUB] for z in where for h in range(2)]
            kf[n : n + FULL, :] = jnp.concatenate(whole, axis=1)
            for d in range(2):
                first = d * TOKENS + r * SUB
                shared = [ref[z, FULL:CHUNK, first : first + SUB] for z in where]
                kh[n + d * HALF : n + (d + 1) * HALF, :] = jnp.concatenate(shared, axis=1)


def keys_kernel(me_ref, own, other, kf, kh):
    lay_keys(me_ref[2], own, other, kf, kh)


def keys_laid(me, own, other):
    return pl.pallas_call(
        keys_kernel,
        out_shape=tuple(jax.ShapeDtypeStruct(s, bf16) for s in KEY_SHAPES),
        in_specs=[SMEM, VMEM, VMEM],
        out_specs=(VMEM,) * 2,
        compiler_params=PARAMS,
        cost_estimate=LAYOUT,
    )(me, own, other)


def score_kernel(me_ref, q_hbm, kf_hbm, kh_hbm, own_hbm, other_hbm, out, qf, qh, kf1, kh1, *rest):
    own, other, q_ref, kf0, kh0, sems = rest
    copies = fetches((own_hbm, other_hbm, q_hbm, kf_hbm, kh_hbm), rest[:5], sems)
    for copy in copies[:2]:
        copy.wait()
    lay_keys(me_ref[2], own, other, kf1, kh1)
    for copy in copies[2:]:
        copy.wait()
    for cr in range(2):
        c = jnp.bitwise_xor(me_ref[1], cr)
        queries = [q_ref[2 * p + c] for p in range(PEERS)]
        for r in range(ROWS):
            n = (cr * ROWS + r) * FULL
            t = jnp.concatenate([b[:, r * SUB : (r + 1) * SUB] for b in queries], axis=1)
            qf[n : n + FULL, :] = t[:FULL]
            qh[n : n + FULL, :] = t[FULL:]
    first = 0
    for a, b in ((qf, kf0), (qf, kf1), (qh, kh0), (qh, kh1)):
        t = dot(a[...], b[...], 0, 0)
        for p in range(PEERS):
            out[p, :, first : first + t.shape[1]] = t[p * SUB : (p + 1) * SUB]
        first += t.shape[1]


def score(me, q, laid, own, other):
    rows = 2 * ROWS * FULL
    return pl.pallas_call(
        score_kernel,
        out_shape=jax.ShapeDtypeStruct((PEERS, SUB, LOGITS), f32),
        in_specs=[SMEM] + [ANY] * 5,
        out_specs=VMEM,
        scratch_shapes=[pltpu.VMEM((rows, QUERIES), bf16)] * 2
        + [pltpu.VMEM(s, bf16) for s in KEY_SHAPES]
        + [pltpu.VMEM(a.shape, bf16) for a in (own, other, q, *laid)]
        + [pltpu.SemaphoreType.DMA((5,))],
        compiler_params=PARAMS,
    )(me, *in_hbm(q), *laid, *in_hbm(own), other)


def total_kernel(parts, full, half):
    t = parts[0]
    for p in range(1, PEERS):
        t = t + parts[p]
    full[...] = t[:, :KEYS]
    half[...] = t[:, KEYS:]


def total(parts):
    return pl.pallas_call(
        total_kernel,
        out_shape=tuple(jax.ShapeDtypeStruct((SUB, n), f32) for n in (KEYS, KEYS // 2)),
        in_specs=[VMEM],
        out_specs=(VMEM,) * 2,
        compiler_params=PARAMS,
    )(parts)


def softmax_kernel(factor, full, half, other, out):
    for i, logits in enumerate((full[...], jnp.concatenate([half[...], other[...]], axis=1))):
        logits = logits * factor
        powered = jnp.exp(logits - jnp.max(logits, axis=-1, keepdims=True))
        probs = (powered / jnp.sum(powered, axis=-1, keepdims=True)).astype(bf16)
        for p in range(PEERS):
            out[p, i] = probs


def softmax(factor, full, half, other):
    return pl.pallas_call(
        functools.partial(softmax_kernel, factor),
        out_shape=jax.ShapeDtypeStruct((PEERS, 2, SUB, KEYS), bf16),
        in_specs=[VMEM] * 3,
        out_specs=VMEM,
        compiler_params=PARAMS,
    )(full, half, other)


def values_kernel(me_ref, *refs):
    (vf, vh), (v00, v01, v10, v11), sems = refs[4:6], refs[6:10], refs[10]
    for copy in fetches(refs[:4], refs[6:10], sems):
        copy.wait()
    z = me_ref[2]
    odd = lax.rem(z, 2)
    where = [lax.rem(z - source + Z, Z) for source in range(Z)]
    for cr, refs in enumerate(((v00, v01), (v10, v11))):
        halves = [
            ref[i, FULL:CHUNK, pl.ds(pl.multiple_of(h * TOKENS, TOKENS), TOKENS)]
            for h in (odd, 1 - odd)
            for ref in refs
            for i in where
        ]
        whole = [ref[i, 0:FULL, h * TOKENS : (h + 1) * TOKENS] for ref in refs for i in where for h in range(2)]
        for r in range(ROWS):
            n = cr * ROWS + r
            lanes = slice(r * SUB, (r + 1) * SUB)
            vf[n * FULL : (n + 1) * FULL, :] = jnp.concatenate([b[:, lanes] for b in whole], axis=1)
            vh[n * HALF : (n + 1) * HALF, :] = jnp.concatenate([b[:, lanes] for b in halves], axis=1)


def values_laid(me, vs):
    return pl.pallas_call(
        values_kernel,
        out_shape=tuple(jax.ShapeDtypeStruct((2 * ROWS * n, KEYS), bf16) for n in (FULL, HALF)),
        in_specs=[SMEM] + [ANY] * 4,
        out_specs=(VMEM,) * 2,
        scratch_shapes=[pltpu.VMEM(v.shape, bf16) for v in vs] + [pltpu.SemaphoreType.DMA((4,))],
        compiler_params=PARAMS,
        cost_estimate=LAYOUT,
    )(me, *in_hbm(*vs[:2]), *vs[2:])


def mix_kernel(me_ref, vf, vh, p_ref, o_ref):
    core = me_ref[1]
    for i, (v, first, n) in enumerate(((vf, 0, FULL), (vh, FULL, HALF))):
        probs = p_ref[:, i].reshape(QUERIES, KEYS)
        for cr in range(2):
            c = jnp.bitwise_xor(core, cr)
            mixed = dot(v[cr * ROWS * n : (cr + 1) * ROWS * n, :], probs, 1, 1).astype(bf16)
            for s in range(PEERS):
                o_ref[2 * s + c, first : first + n, :] = jnp.concatenate(
                    [mixed[r * n : (r + 1) * n, s * SUB : (s + 1) * SUB] for r in range(ROWS)], axis=1
                )


def mix(me, laid, probs):
    return pl.pallas_call(
        mix_kernel,
        out_shape=jax.ShapeDtypeStruct((2 * Z, CHUNK, ROWS * SUB), bf16),
        in_specs=[SMEM] + [VMEM] * 3,
        out_specs=VMEM,
        compiler_params=PARAMS,
    )(me, *laid, probs)


def final_kernel(m_ref, w_ref, o_ref, t_ref):
    for c in range(2):
        for z in range(Z):
            (a, na), (b, nb) = chunk_pieces(z)
            t_ref[a : a + na, :] = m_ref[2 * z + c, 0:FULL, :]
            t_ref[b : b + nb, :] = m_ref[2 * z + c, FULL:CHUNK, :]
        attended = dot(t_ref[...], w_ref[...], 0, 0).astype(bf16)
        o_ref[:, c * SUB : (c + 1) * SUB, :] = attended.reshape(ROWS, SUB, EMBED)


def final(m, w):
    return pl.pallas_call(
        final_kernel,
        out_shape=jax.ShapeDtypeStruct((ROWS, RES, EMBED), bf16),
        in_specs=[VMEM] * 2,
        out_specs=VMEM,
        scratch_shapes=[pltpu.VMEM((EMBED, ROWS * SUB), bf16)],
        compiler_params=PARAMS,
    )(m, w)


def flip(x, axes, n, s):
    return lax.ppermute(x, axes, [(i, i ^ s) for i in range(n)])


def gather4(own):
    far = flip(own, "xl", 2, 1)
    return own, far, flip(own, "c", 2, 1), flip(far, "c", 2, 1)


def shift(x, s):
    return lax.ppermute(x, "z", [(i, (i + s) % Z) for i in range(Z)])


def local(x, wq, wk, wv, wf):
    me = jnp.stack([lax.axis_index(("y", "xh")), lax.axis_index("c"), lax.axis_index("z")])
    me = me.astype(jnp.int32)
    n, k = key_chunks(me, x, wk)
    for s in (1, 7, 2, 6, 3, 5, 4):
        k[s] = shift(k[s], s)
    early = (1, 7, 2, 6, 3, 5)
    q, *got = lax.optimization_barrier((query_chunks(n, wq), *(k[s] for s in early)))
    for s, a in zip(early, got):
        k[s] = a
    q = lax.all_to_all(q, ("z", "c"), 0, 0, tiled=True)
    v = list(value_chunks(me, n, wv))
    k = jnp.stack(k)
    near, shared = keys_laid(me, k, flip(k, "c", 2, 1))
    for s in (1, 7):
        v[s] = shift(v[s], s)
    k_far, v[1], v[7], shared = lax.optimization_barrier((flip(k, "xl", 2, 1), v[1], v[7], shared))
    scores = score(me, q, (near, shared), k_far, flip(k_far, "c", 2, 1))
    *v, scores = lax.optimization_barrier((*v, scores))
    parts = lax.all_to_all(scores, ("y", "xh"), 0, 0, tiled=True)
    for s in (4, 3, 5, 2, 6):
        v[s] = shift(v[s], s)
    full, half = total(parts)
    rows = ROWS * 2 * PEERS
    probs = softmax(1.0 / math.sqrt(DH * rows), full, half, flip(half, "z", Z, 1))
    probs = lax.all_to_all(probs, ("y", "xh"), 0, 0, tiled=True)
    laid = values_laid(me, gather4(jnp.stack(v)))
    mixed = lax.all_to_all(mix(me, laid, probs), ("z", "c"), 0, 0, tiled=True)
    return final(mixed, wf)


def solution(mesh):
    fine = Mesh(mesh.devices.reshape(4, 2, 2, 8, 2), ("y", "xh", "c", "z", "xl"))
    spec = P(("y", "xh", "c"), ("z", "xl"), None)
    return jax.shard_map(
        local,
        mesh=fine,
        in_specs=(spec, P(), P(), P(), P()),
        out_specs=spec,
        check_vma=False,
    )
```

```python
import functools
import math

import jax
import jax.numpy as jnp
from jax import lax
from jax.experimental import pallas as pl
from jax.experimental.pallas import tpu as pltpu
from jax.sharding import Mesh, PartitionSpec as P

H = 12
DH = 64
EMBED = 768
ROWS = 8
RES = 64
Z = 8
CHUNK = EMBED // Z
FULL = DH
HALF = CHUNK - DH
PEERS = 8
SUB = RES // 2
TOKENS = ROWS * SUB
QUERIES = Z * SUB
KEYS = 2 * Z * RES
LOGITS = KEYS + KEYS // 2

f32 = jnp.float32
bf16 = jnp.bfloat16
PARAMS = pltpu.CompilerParams(vmem_limit_bytes=16 * 1024 * 1024)
PROJECTION = pl.CostEstimate(
    flops=2 * ROWS * RES * EMBED * EMBED, bytes_accessed=2 * EMBED * (EMBED + 2 * ROWS * RES), transcendentals=0
)
LAYOUT = pl.CostEstimate(flops=0, bytes_accessed=16 * ROWS * RES * EMBED, transcendentals=0)
KEY_SHAPES = ((2 * ROWS * FULL, KEYS // 2), (2 * ROWS * FULL, KEYS // 4))
WIDE = pltpu.CompilerParams(vmem_limit_bytes=16 * 1024 * 1024)
VMEM = pl.BlockSpec(memory_space=pltpu.VMEM)
SMEM = pl.BlockSpec(memory_space=pltpu.SMEM)
ANY = pl.BlockSpec(memory_space=pl.ANY)
HBM = pl.BlockSpec(memory_space=pltpu.HBM)


def chunk_pieces(z):
    base = z * CHUNK
    if z % 2 == 0:
        return (base, FULL), (base + FULL, HALF)
    return (base + HALF, FULL), (base, HALF)


def dot(a, b, ca, cb):
    return lax.dot_general(a, b, (((ca,), (cb,)), ((), ())), preferred_element_type=f32)


def shared_head(z):
    return z // 2 * (2 * CHUNK) + FULL


def chunk_rows(z):
    odd = lax.rem(z, 2)
    base = z * CHUNK
    return pl.multiple_of(base + odd * HALF, HALF), pl.multiple_of(base + (1 - odd) * FULL, HALF)


def fetches(sources, buffers, sems):
    copies = [pltpu.make_async_copy(a, b, sems.at[i]) for i, (a, b) in enumerate(zip(sources, buffers))]
    for copy in copies:
        copy.start()
    return copies


def in_hbm(*arrays):
    return [pltpu.with_memory_space_constraint(a, pltpu.HBM) for a in arrays]


def key_kernel(me_ref, x_hbm, w_hbm, n_ref, *rest):
    outs, (x_ref, w_ref, t_ref, sems) = rest[:Z], rest[Z:]
    copy_x, copy_w = fetches((x_hbm, w_hbm), (x_ref, w_ref), sems)
    copy_x.wait()
    x = x_ref[...].astype(f32)
    centred = x - jnp.mean(x, axis=-1, keepdims=True)
    var = jnp.mean(centred * centred, axis=-1, keepdims=True)
    normed = (centred * lax.rsqrt(var + 1e-05)).astype(bf16)
    for h in range(2):
        n_ref[h] = normed[:, h * SUB : (h + 1) * SUB, :]
    copy_w.wait()
    t_ref[...] = dot(w_ref[...], n_ref[...].reshape(ROWS * RES, EMBED), 0, 1).astype(bf16)
    for s, out in enumerate(outs):
        z = lax.rem(me_ref[2] + s, Z)
        first, odd = shared_head(z), lax.rem(z, 2)
        lanes = pl.ds(pl.multiple_of(odd * TOKENS, TOKENS), TOKENS)
        out[0:FULL, :] = t_ref[pl.ds(chunk_rows(z)[0], FULL), :]
        for d in range(2):
            rows = pl.ds(pl.multiple_of(first + d * HALF, HALF), HALF)
            out[FULL:CHUNK, d * TOKENS : (d + 1) * TOKENS] = t_ref[rows, lanes]


def key_chunks(me, x, w):
    n, *k = pl.pallas_call(
        key_kernel,
        out_shape=(jax.ShapeDtypeStruct((2, ROWS, SUB, EMBED), bf16),)
        + (jax.ShapeDtypeStruct((CHUNK, ROWS * RES), bf16),) * Z,
        in_specs=[SMEM, ANY, ANY],
        out_specs=(VMEM,) * (1 + Z),
        scratch_shapes=[
            pltpu.VMEM((ROWS, RES, EMBED), bf16),
            pltpu.VMEM((EMBED, EMBED), bf16),
            pltpu.VMEM((EMBED, ROWS * RES), bf16),
            pltpu.SemaphoreType.DMA((2,)),
        ],
        compiler_params=PARAMS,
    )(me, *in_hbm(x, w))
    return n, k


def query_kernel(n_ref, w_ref, q_ref):
    for c in range(2):
        t = dot(w_ref[...], n_ref[c].reshape(TOKENS, EMBED), 0, 1).astype(bf16)
        for z in range(Z):
            a, b = chunk_pieces(z)[0][0], shared_head(z)
            q_ref[2 * z + c, 0:FULL, :] = t[a : a + FULL]
            q_ref[2 * z + c, FULL:, :] = t[b : b + FULL]


def query_chunks(n, w):
    return pl.pallas_call(
        query_kernel,
        out_shape=jax.ShapeDtypeStruct((2 * Z, 2 * FULL, TOKENS), bf16),
        in_specs=[VMEM] * 2,
        out_specs=VMEM,
        compiler_params=PARAMS,
        cost_estimate=PROJECTION,
    )(n, w)


def value_kernel(me_ref, n_ref, w_ref, *rest):
    outs, t_ref = rest[:Z], rest[Z]
    t_ref[...] = dot(w_ref[...], n_ref[...].reshape(ROWS * RES, EMBED), 0, 1).astype(bf16)
    for s, out in enumerate(outs):
        full, half = chunk_rows(lax.rem(me_ref[2] + s, Z))
        out[0:FULL, :] = t_ref[pl.ds(full, FULL), :]
        out[FULL:CHUNK, :] = t_ref[pl.ds(half, HALF), :]


def value_chunks(me, n, w):
    return pl.pallas_call(
        value_kernel,
        out_shape=(jax.ShapeDtypeStruct((CHUNK, ROWS * RES), bf16),) * Z,
        in_specs=[SMEM, VMEM, VMEM],
        out_specs=(VMEM,) * Z,
        scratch_shapes=[pltpu.VMEM((EMBED, ROWS * RES), bf16)],
        compiler_params=PARAMS,
        cost_estimate=PROJECTION,
    )(me, n, w)


def lay_keys(me, own, other, kf, kh):
    where = [lax.rem(me - z + Z, Z) for z in range(Z)]
    for cr, ref in enumerate((own, other)):
        for r in range(ROWS):
            n = (cr * ROWS + r) * FULL
            whole = [ref[z, 0:FULL, h * TOKENS + r * SUB : h * TOKENS + (r + 1) * SUB] for z in where for h in range(2)]
            kf[n : n + FULL, :] = jnp.concatenate(whole, axis=1)
            for d in range(2):
                first = d * TOKENS + r * SUB
                shared = [ref[z, FULL:CHUNK, first : first + SUB] for z in where]
                kh[n + d * HALF : n + (d + 1) * HALF, :] = jnp.concatenate(shared, axis=1)


def keys_kernel(me_ref, own, other, kf, kh):
    lay_keys(me_ref[2], own, other, kf, kh)


def keys_laid(me, own, other):
    return pl.pallas_call(
        keys_kernel,
        out_shape=tuple(jax.ShapeDtypeStruct(s, bf16) for s in KEY_SHAPES),
        in_specs=[SMEM, VMEM, VMEM],
        out_specs=(VMEM,) * 2,
        compiler_params=PARAMS,
        cost_estimate=LAYOUT,
    )(me, own, other)


def score_kernel(me_ref, q_hbm, kf_hbm, kh_hbm, own_hbm, other_hbm, out, qf, qh, kf1, kh1, *rest):
    own, other, q_ref, kf0, kh0, sems = rest
    copies = fetches((own_hbm, other_hbm, q_hbm, kf_hbm, kh_hbm), rest[:5], sems)
    for copy in copies[:2]:
        copy.wait()
    lay_keys(me_ref[2], own, other, kf1, kh1)
    for copy in copies[2:]:
        copy.wait()
    for cr in range(2):
        c = jnp.bitwise_xor(me_ref[1], cr)
        queries = [q_ref[2 * p + c] for p in range(PEERS)]
        for r in range(ROWS):
            n = (cr * ROWS + r) * FULL
            t = jnp.concatenate([b[:, r * SUB : (r + 1) * SUB] for b in queries], axis=1)
            qf[n : n + FULL, :] = t[:FULL]
            qh[n : n + FULL, :] = t[FULL:]
    first = 0
    for a, b in ((qf, kf0), (qf, kf1), (qh, kh0), (qh, kh1)):
        t = dot(a[...], b[...], 0, 0)
        for p in range(PEERS):
            out[p, :, first : first + t.shape[1]] = t[p * SUB : (p + 1) * SUB]
        first += t.shape[1]


def score(me, q, laid, own, other):
    rows = 2 * ROWS * FULL
    return pl.pallas_call(
        score_kernel,
        out_shape=jax.ShapeDtypeStruct((PEERS, SUB, LOGITS), f32),
        in_specs=[SMEM] + [ANY] * 5,
        out_specs=VMEM,
        scratch_shapes=[pltpu.VMEM((rows, QUERIES), bf16)] * 2
        + [pltpu.VMEM(s, bf16) for s in KEY_SHAPES]
        + [pltpu.VMEM(a.shape, bf16) for a in (own, other, q, *laid)]
        + [pltpu.SemaphoreType.DMA((5,))],
        compiler_params=PARAMS,
    )(me, *in_hbm(q), *laid, *in_hbm(own), other)


def total_kernel(parts, full, half):
    t = parts[0]
    for p in range(1, PEERS):
        t = t + parts[p]
    full[...] = t[:, :KEYS]
    half[...] = t[:, KEYS:]


def total(parts):
    return pl.pallas_call(
        total_kernel,
        out_shape=tuple(jax.ShapeDtypeStruct((SUB, n), f32) for n in (KEYS, KEYS // 2)),
        in_specs=[VMEM],
        out_specs=(VMEM,) * 2,
        compiler_params=PARAMS,
    )(parts)


def softmax_kernel(factor, full, half, other, out):
    for i, logits in enumerate((full[...], jnp.concatenate([half[...], other[...]], axis=1))):
        logits = logits * factor
        powered = jnp.exp(logits - jnp.max(logits, axis=-1, keepdims=True))
        probs = (powered / jnp.sum(powered, axis=-1, keepdims=True)).astype(bf16)
        for p in range(PEERS):
            out[p, i] = probs


def softmax(factor, full, half, other):
    return pl.pallas_call(
        functools.partial(softmax_kernel, factor),
        out_shape=jax.ShapeDtypeStruct((PEERS, 2, SUB, KEYS), bf16),
        in_specs=[VMEM] * 3,
        out_specs=VMEM,
        compiler_params=PARAMS,
    )(full, half, other)


def values_kernel(me_ref, *refs):
    (vf, vh), (v00, v01, v10, v11), sems = refs[4:6], refs[6:10], refs[10]
    for copy in fetches(refs[:4], refs[6:10], sems):
        copy.wait()
    z = me_ref[2]
    odd = lax.rem(z, 2)
    where = [lax.rem(z - source + Z, Z) for source in range(Z)]
    for cr, refs in enumerate(((v00, v01), (v10, v11))):
        halves = [
            ref[i, FULL:CHUNK, pl.ds(pl.multiple_of(h * TOKENS, TOKENS), TOKENS)]
            for h in (odd, 1 - odd)
            for ref in refs
            for i in where
        ]
        whole = [ref[i, 0:FULL, h * TOKENS : (h + 1) * TOKENS] for ref in refs for i in where for h in range(2)]
        for r in range(ROWS):
            n = cr * ROWS + r
            lanes = slice(r * SUB, (r + 1) * SUB)
            vf[n * FULL : (n + 1) * FULL, :] = jnp.concatenate([b[:, lanes] for b in whole], axis=1)
            vh[n * HALF : (n + 1) * HALF, :] = jnp.concatenate([b[:, lanes] for b in halves], axis=1)


def values_laid(me, vs):
    return pl.pallas_call(
        values_kernel,
        out_shape=tuple(jax.ShapeDtypeStruct((2 * ROWS * n, KEYS), bf16) for n in (FULL, HALF)),
        in_specs=[SMEM] + [ANY] * 4,
        out_specs=(VMEM,) * 2,
        scratch_shapes=[pltpu.VMEM(v.shape, bf16) for v in vs] + [pltpu.SemaphoreType.DMA((4,))],
        compiler_params=PARAMS,
        cost_estimate=LAYOUT,
    )(me, *in_hbm(*vs[:2]), *vs[2:])


def mix_kernel(me_ref, vf, vh, p_ref, o_ref):
    core = me_ref[1]
    for i, (v, first, n) in enumerate(((vf, 0, FULL), (vh, FULL, HALF))):
        probs = p_ref[:, i].reshape(QUERIES, KEYS)
        for cr in range(2):
            c = jnp.bitwise_xor(core, cr)
            mixed = dot(v[cr * ROWS * n : (cr + 1) * ROWS * n, :], probs, 1, 1).astype(bf16)
            for s in range(PEERS):
                o_ref[2 * s + c, first : first + n, :] = jnp.concatenate(
                    [mixed[r * n : (r + 1) * n, s * SUB : (s + 1) * SUB] for r in range(ROWS)], axis=1
                )


def mix(me, laid, probs):
    return pl.pallas_call(
        mix_kernel,
        out_shape=jax.ShapeDtypeStruct((2 * Z, CHUNK, ROWS * SUB), bf16),
        in_specs=[SMEM] + [VMEM] * 3,
        out_specs=VMEM,
        compiler_params=PARAMS,
    )(me, *laid, probs)


def final_kernel(m_ref, w_ref, o_ref, t_ref):
    for c in range(2):
        for z in range(Z):
            (a, na), (b, nb) = chunk_pieces(z)
            t_ref[a : a + na, :] = m_ref[2 * z + c, 0:FULL, :]
            t_ref[b : b + nb, :] = m_ref[2 * z + c, FULL:CHUNK, :]
        attended = dot(t_ref[...], w_ref[...], 0, 0).astype(bf16)
        o_ref[:, c * SUB : (c + 1) * SUB, :] = attended.reshape(ROWS, SUB, EMBED)


def final(m, w):
    return pl.pallas_call(
        final_kernel,
        out_shape=jax.ShapeDtypeStruct((ROWS, RES, EMBED), bf16),
        in_specs=[VMEM] * 2,
        out_specs=VMEM,
        scratch_shapes=[pltpu.VMEM((EMBED, ROWS * SUB), bf16)],
        compiler_params=PARAMS,
    )(m, w)


def flip(x, axes, n, s):
    return lax.ppermute(x, axes, [(i, i ^ s) for i in range(n)])


def gather4(own):
    far = flip(own, "xl", 2, 1)
    return own, far, flip(own, "c", 2, 1), flip(far, "c", 2, 1)


def shift(x, s):
    return lax.ppermute(x, "z", [(i, (i + s) % Z) for i in range(Z)])


def local(x, wq, wk, wv, wf):
    me = jnp.stack([lax.axis_index(("y", "xh")), lax.axis_index("c"), lax.axis_index("z")])
    me = me.astype(jnp.int32)
    n, k = key_chunks(me, x, wk)
    for s in (1, 7, 2, 6, 3, 5, 4):
        k[s] = shift(k[s], s)
    early = (1, 7, 2, 6, 3)
    q, *got = lax.optimization_barrier((query_chunks(n, wq), *(k[s] for s in early)))
    for s, a in zip(early, got):
        k[s] = a
    q = lax.all_to_all(q, ("z", "c"), 0, 0, tiled=True)
    v = list(value_chunks(me, n, wv))
    k = jnp.stack(k)
    near, shared = keys_laid(me, k, flip(k, "c", 2, 1))
    k_far, v[4], shared = lax.optimization_barrier((flip(k, "xl", 2, 1), v[4], shared))
    for s in (3, 5):
        v[s] = shift(v[s], s)
    scores = score(me, q, (near, shared), k_far, flip(k_far, "c", 2, 1))
    *v, scores = lax.optimization_barrier((*v, scores))
    parts = lax.all_to_all(scores, ("y", "xh"), 0, 0, tiled=True)
    for s in (4, 2, 6, 1, 7):
        v[s] = shift(v[s], s)
    full, half = total(parts)
    rows = ROWS * 2 * PEERS
    probs = softmax(1.0 / math.sqrt(DH * rows), full, half, flip(half, "z", Z, 1))
    probs = lax.all_to_all(probs, ("y", "xh"), 0, 0, tiled=True)
    laid = values_laid(me, gather4(jnp.stack(v)))
    mixed = lax.all_to_all(mix(me, laid, probs), ("z", "c"), 0, 0, tiled=True)
    return final(mixed, wf)


def solution(mesh):
    fine = Mesh(mesh.devices.reshape(4, 2, 2, 8, 2), ("y", "xh", "c", "z", "xl"))
    spec = P(("y", "xh", "c"), ("z", "xl"), None)
    return jax.shard_map(
        local,
        mesh=fine,
        in_specs=(spec, P(), P(), P(), P()),
        out_specs=spec,
        check_vma=False,
    )
```

```python
import functools
import math

import jax
import jax.numpy as jnp
from jax import lax
from jax.experimental import pallas as pl
from jax.experimental.pallas import tpu as pltpu
from jax.sharding import Mesh, PartitionSpec as P

H = 12
DH = 64
EMBED = 768
ROWS = 8
RES = 64
Z = 8
CHUNK = EMBED // Z
FULL = DH
HALF = CHUNK - DH
PEERS = 8
SUB = RES // 2
TOKENS = ROWS * SUB
QUERIES = Z * SUB
KEYS = 2 * Z * RES
LOGITS = KEYS + KEYS // 2

f32 = jnp.float32
bf16 = jnp.bfloat16
PARAMS = pltpu.CompilerParams(vmem_limit_bytes=16 * 1024 * 1024)
PROJECTION = pl.CostEstimate(
    flops=2 * ROWS * RES * EMBED * EMBED, bytes_accessed=2 * EMBED * (EMBED + 2 * ROWS * RES), transcendentals=0
)
LAYOUT = pl.CostEstimate(flops=0, bytes_accessed=16 * ROWS * RES * EMBED, transcendentals=0)
KEY_SHAPES = ((2 * ROWS * FULL, KEYS // 2), (2 * ROWS * FULL, KEYS // 4))
WIDE = pltpu.CompilerParams(vmem_limit_bytes=16 * 1024 * 1024)
VMEM = pl.BlockSpec(memory_space=pltpu.VMEM)
SMEM = pl.BlockSpec(memory_space=pltpu.SMEM)
ANY = pl.BlockSpec(memory_space=pl.ANY)
HBM = pl.BlockSpec(memory_space=pltpu.HBM)


def chunk_pieces(z):
    base = z * CHUNK
    if z % 2 == 0:
        return (base, FULL), (base + FULL, HALF)
    return (base + HALF, FULL), (base, HALF)


def dot(a, b, ca, cb):
    return lax.dot_general(a, b, (((ca,), (cb,)), ((), ())), preferred_element_type=f32)


def shared_head(z):
    return z // 2 * (2 * CHUNK) + FULL


def chunk_rows(z):
    odd = lax.rem(z, 2)
    base = z * CHUNK
    return pl.multiple_of(base + odd * HALF, HALF), pl.multiple_of(base + (1 - odd) * FULL, HALF)


def fetches(sources, buffers, sems):
    copies = [pltpu.make_async_copy(a, b, sems.at[i]) for i, (a, b) in enumerate(zip(sources, buffers))]
    for copy in copies:
        copy.start()
    return copies


def in_hbm(*arrays):
    return [pltpu.with_memory_space_constraint(a, pltpu.HBM) for a in arrays]


def key_kernel(me_ref, x_hbm, w_hbm, n_ref, *rest):
    outs, (x_ref, w_ref, t_ref, sems) = rest[:Z], rest[Z:]
    copy_x, copy_w = fetches((x_hbm, w_hbm), (x_ref, w_ref), sems)
    copy_x.wait()
    x = x_ref[...].astype(f32)
    centred = x - jnp.mean(x, axis=-1, keepdims=True)
    var = jnp.mean(centred * centred, axis=-1, keepdims=True)
    normed = (centred * lax.rsqrt(var + 1e-05)).astype(bf16)
    for h in range(2):
        n_ref[h] = normed[:, h * SUB : (h + 1) * SUB, :]
    copy_w.wait()
    t_ref[...] = dot(w_ref[...], n_ref[...].reshape(ROWS * RES, EMBED), 0, 1).astype(bf16)
    for s, out in enumerate(outs):
        z = lax.rem(me_ref[2] + s, Z)
        first, odd = shared_head(z), lax.rem(z, 2)
        lanes = pl.ds(pl.multiple_of(odd * TOKENS, TOKENS), TOKENS)
        out[0:FULL, :] = t_ref[pl.ds(chunk_rows(z)[0], FULL), :]
        for d in range(2):
            rows = pl.ds(pl.multiple_of(first + d * HALF, HALF), HALF)
            out[FULL:CHUNK, d * TOKENS : (d + 1) * TOKENS] = t_ref[rows, lanes]


def key_chunks(me, x, w):
    n, *k = pl.pallas_call(
        key_kernel,
        out_shape=(jax.ShapeDtypeStruct((2, ROWS, SUB, EMBED), bf16),)
        + (jax.ShapeDtypeStruct((CHUNK, ROWS * RES), bf16),) * Z,
        in_specs=[SMEM, ANY, ANY],
        out_specs=(VMEM,) * (1 + Z),
        scratch_shapes=[
            pltpu.VMEM((ROWS, RES, EMBED), bf16),
            pltpu.VMEM((EMBED, EMBED), bf16),
            pltpu.VMEM((EMBED, ROWS * RES), bf16),
            pltpu.SemaphoreType.DMA((2,)),
        ],
        compiler_params=PARAMS,
    )(me, *in_hbm(x, w))
    return n, k


def query_kernel(n_ref, w_ref, q_ref):
    for c in range(2):
        t = dot(w_ref[...], n_ref[c].reshape(TOKENS, EMBED), 0, 1).astype(bf16)
        for z in range(Z):
            a, b = chunk_pieces(z)[0][0], shared_head(z)
            q_ref[2 * z + c, 0:FULL, :] = t[a : a + FULL]
            q_ref[2 * z + c, FULL:, :] = t[b : b + FULL]


def query_chunks(n, w):
    return pl.pallas_call(
        query_kernel,
        out_shape=jax.ShapeDtypeStruct((2 * Z, 2 * FULL, TOKENS), bf16),
        in_specs=[VMEM] * 2,
        out_specs=VMEM,
        compiler_params=PARAMS,
        cost_estimate=PROJECTION,
    )(n, w)


def value_kernel(me_ref, n_ref, w_ref, *rest):
    outs, t_ref = rest[:Z], rest[Z]
    t_ref[...] = dot(w_ref[...], n_ref[...].reshape(ROWS * RES, EMBED), 0, 1).astype(bf16)
    for s, out in enumerate(outs):
        full, half = chunk_rows(lax.rem(me_ref[2] + s, Z))
        out[0:FULL, :] = t_ref[pl.ds(full, FULL), :]
        out[FULL:CHUNK, :] = t_ref[pl.ds(half, HALF), :]


def value_chunks(me, n, w):
    return pl.pallas_call(
        value_kernel,
        out_shape=(jax.ShapeDtypeStruct((CHUNK, ROWS * RES), bf16),) * Z,
        in_specs=[SMEM, VMEM, VMEM],
        out_specs=(VMEM,) * Z,
        scratch_shapes=[pltpu.VMEM((EMBED, ROWS * RES), bf16)],
        compiler_params=PARAMS,
        cost_estimate=PROJECTION,
    )(me, n, w)


def lay_keys(me, own, other, kf, kh):
    where = [lax.rem(me - z + Z, Z) for z in range(Z)]
    for cr, ref in enumerate((own, other)):
        for r in range(ROWS):
            n = (cr * ROWS + r) * FULL
            whole = [ref[z, 0:FULL, h * TOKENS + r * SUB : h * TOKENS + (r + 1) * SUB] for z in where for h in range(2)]
            kf[n : n + FULL, :] = jnp.concatenate(whole, axis=1)
            for d in range(2):
                first = d * TOKENS + r * SUB
                shared = [ref[z, FULL:CHUNK, first : first + SUB] for z in where]
                kh[n + d * HALF : n + (d + 1) * HALF, :] = jnp.concatenate(shared, axis=1)


def keys_kernel(me_ref, own, other, kf, kh):
    lay_keys(me_ref[2], own, other, kf, kh)


def keys_laid(me, own, other):
    return pl.pallas_call(
        keys_kernel,
        out_shape=tuple(jax.ShapeDtypeStruct(s, bf16) for s in KEY_SHAPES),
        in_specs=[SMEM, VMEM, VMEM],
        out_specs=(VMEM,) * 2,
        compiler_params=PARAMS,
        cost_estimate=LAYOUT,
    )(me, own, other)


def score_kernel(me_ref, q_hbm, kf_hbm, kh_hbm, own_hbm, other_hbm, out, qf, qh, kf1, kh1, *rest):
    own, other, q_ref, kf0, kh0, sems = rest
    copies = fetches((own_hbm, other_hbm, q_hbm, kf_hbm, kh_hbm), rest[:5], sems)
    for copy in copies[:2]:
        copy.wait()
    lay_keys(me_ref[2], own, other, kf1, kh1)
    for copy in copies[2:]:
        copy.wait()
    for cr in range(2):
        c = jnp.bitwise_xor(me_ref[1], cr)
        queries = [q_ref[2 * p + c] for p in range(PEERS)]
        for r in range(ROWS):
            n = (cr * ROWS + r) * FULL
            t = jnp.concatenate([b[:, r * SUB : (r + 1) * SUB] for b in queries], axis=1)
            qf[n : n + FULL, :] = t[:FULL]
            qh[n : n + FULL, :] = t[FULL:]
    first = 0
    for a, b in ((qf, kf0), (qf, kf1), (qh, kh0), (qh, kh1)):
        t = dot(a[...], b[...], 0, 0)
        for p in range(PEERS):
            out[p, :, first : first + t.shape[1]] = t[p * SUB : (p + 1) * SUB]
        first += t.shape[1]


def score(me, q, laid, own, other):
    rows = 2 * ROWS * FULL
    return pl.pallas_call(
        score_kernel,
        out_shape=jax.ShapeDtypeStruct((PEERS, SUB, LOGITS), f32),
        in_specs=[SMEM] + [ANY] * 5,
        out_specs=VMEM,
        scratch_shapes=[pltpu.VMEM((rows, QUERIES), bf16)] * 2
        + [pltpu.VMEM(s, bf16) for s in KEY_SHAPES]
        + [pltpu.VMEM(a.shape, bf16) for a in (own, other, q, *laid)]
        + [pltpu.SemaphoreType.DMA((5,))],
        compiler_params=PARAMS,
    )(me, *in_hbm(q), *laid, *in_hbm(own), other)


def total_kernel(parts, full, half):
    t = parts[0]
    for p in range(1, PEERS):
        t = t + parts[p]
    full[...] = t[:, :KEYS]
    half[...] = t[:, KEYS:]


def total(parts):
    return pl.pallas_call(
        total_kernel,
        out_shape=tuple(jax.ShapeDtypeStruct((SUB, n), f32) for n in (KEYS, KEYS // 2)),
        in_specs=[VMEM],
        out_specs=(VMEM,) * 2,
        compiler_params=PARAMS,
    )(parts)


def softmax_kernel(factor, full, half, other, out):
    for i, logits in enumerate((full[...], jnp.concatenate([half[...], other[...]], axis=1))):
        logits = logits * factor
        powered = jnp.exp(logits - jnp.max(logits, axis=-1, keepdims=True))
        probs = (powered / jnp.sum(powered, axis=-1, keepdims=True)).astype(bf16)
        for p in range(PEERS):
            out[p, i] = probs


def softmax(factor, full, half, other):
    return pl.pallas_call(
        functools.partial(softmax_kernel, factor),
        out_shape=jax.ShapeDtypeStruct((PEERS, 2, SUB, KEYS), bf16),
        in_specs=[VMEM] * 3,
        out_specs=VMEM,
        compiler_params=PARAMS,
    )(full, half, other)


def values_kernel(me_ref, *refs):
    (vf, vh), (v00, v01, v10, v11), sems = refs[4:6], refs[6:10], refs[10]
    for copy in fetches(refs[:4], refs[6:10], sems):
        copy.wait()
    z = me_ref[2]
    odd = lax.rem(z, 2)
    where = [lax.rem(z - source + Z, Z) for source in range(Z)]
    for cr, refs in enumerate(((v00, v01), (v10, v11))):
        halves = [
            ref[i, FULL:CHUNK, pl.ds(pl.multiple_of(h * TOKENS, TOKENS), TOKENS)]
            for h in (odd, 1 - odd)
            for ref in refs
            for i in where
        ]
        whole = [ref[i, 0:FULL, h * TOKENS : (h + 1) * TOKENS] for ref in refs for i in where for h in range(2)]
        for r in range(ROWS):
            n = cr * ROWS + r
            lanes = slice(r * SUB, (r + 1) * SUB)
            vf[n * FULL : (n + 1) * FULL, :] = jnp.concatenate([b[:, lanes] for b in whole], axis=1)
            vh[n * HALF : (n + 1) * HALF, :] = jnp.concatenate([b[:, lanes] for b in halves], axis=1)


def values_laid(me, vs):
    return pl.pallas_call(
        values_kernel,
        out_shape=(
            jax.ShapeDtypeStruct((2 * ROWS * FULL, KEYS), bf16),
            pltpu.HBM((2 * ROWS * HALF, KEYS), bf16),
        ),
        in_specs=[SMEM] + [ANY] * 4,
        out_specs=(VMEM,) * 2,
        scratch_shapes=[pltpu.VMEM(v.shape, bf16) for v in vs] + [pltpu.SemaphoreType.DMA((4,))],
        compiler_params=PARAMS,
        cost_estimate=LAYOUT,
    )(me, *in_hbm(*vs[:2]), *vs[2:])


def mix_kernel(me_ref, vf, vh_hbm, p_ref, o_ref, vh, sems):
    core = me_ref[1]
    copy = fetches((vh_hbm,), (vh,), sems)[0]
    for i, (v, first, n) in enumerate(((vf, 0, FULL), (vh, FULL, HALF))):
        if i == 1:
            copy.wait()
        probs = p_ref[:, i].reshape(QUERIES, KEYS)
        for cr in range(2):
            c = jnp.bitwise_xor(core, cr)
            mixed = dot(v[cr * ROWS * n : (cr + 1) * ROWS * n, :], probs, 1, 1).astype(bf16)
            for s in range(PEERS):
                o_ref[2 * s + c, first : first + n, :] = jnp.concatenate(
                    [mixed[r * n : (r + 1) * n, s * SUB : (s + 1) * SUB] for r in range(ROWS)], axis=1
                )


def mix(me, laid, probs):
    whole, shared = laid
    return pl.pallas_call(
        mix_kernel,
        out_shape=jax.ShapeDtypeStruct((2 * Z, CHUNK, ROWS * SUB), bf16),
        in_specs=[SMEM, VMEM, ANY, VMEM],
        out_specs=VMEM,
        scratch_shapes=[pltpu.VMEM(shared.shape, bf16), pltpu.SemaphoreType.DMA((1,))],
        compiler_params=PARAMS,
    )(me, whole, *in_hbm(shared), probs)


def final_kernel(m_ref, w_ref, o_ref, t_ref):
    for c in range(2):
        for z in range(Z):
            (a, na), (b, nb) = chunk_pieces(z)
            t_ref[a : a + na, :] = m_ref[2 * z + c, 0:FULL, :]
            t_ref[b : b + nb, :] = m_ref[2 * z + c, FULL:CHUNK, :]
        attended = dot(t_ref[...], w_ref[...], 0, 0).astype(bf16)
        o_ref[:, c * SUB : (c + 1) * SUB, :] = attended.reshape(ROWS, SUB, EMBED)


def final(m, w):
    return pl.pallas_call(
        final_kernel,
        out_shape=jax.ShapeDtypeStruct((ROWS, RES, EMBED), bf16),
        in_specs=[VMEM] * 2,
        out_specs=VMEM,
        scratch_shapes=[pltpu.VMEM((EMBED, ROWS * SUB), bf16)],
        compiler_params=PARAMS,
    )(m, w)


def flip(x, axes, n, s):
    return lax.ppermute(x, axes, [(i, i ^ s) for i in range(n)])


def gather4(own):
    far = flip(own, "xl", 2, 1)
    return own, far, flip(own, "c", 2, 1), flip(far, "c", 2, 1)


def shift(x, s):
    return lax.ppermute(x, "z", [(i, (i + s) % Z) for i in range(Z)])


def local(x, wq, wk, wv, wf):
    me = jnp.stack([lax.axis_index(("y", "xh")), lax.axis_index("c"), lax.axis_index("z")])
    me = me.astype(jnp.int32)
    n, k = key_chunks(me, x, wk)
    for s in (1, 7, 2, 6, 3, 5, 4):
        k[s] = shift(k[s], s)
    early = (1, 7, 2, 6, 3)
    q, *got = lax.optimization_barrier((query_chunks(n, wq), *(k[s] for s in early)))
    for s, a in zip(early, got):
        k[s] = a
    q = lax.all_to_all(q, ("z", "c"), 0, 0, tiled=True)
    v = list(value_chunks(me, n, wv))
    k = jnp.stack(k)
    near, shared = keys_laid(me, k, flip(k, "c", 2, 1))
    k_far, v[4], shared = lax.optimization_barrier((flip(k, "xl", 2, 1), v[4], shared))
    for s in (2, 6):
        v[s] = shift(v[s], s)
    scores = score(me, q, (near, shared), k_far, flip(k_far, "c", 2, 1))
    *v, scores = lax.optimization_barrier((*v, scores))
    parts = lax.all_to_all(scores, ("y", "xh"), 0, 0, tiled=True)
    for s in (4, 3, 5, 1, 7):
        v[s] = shift(v[s], s)
    full, half = total(parts)
    rows = ROWS * 2 * PEERS
    probs = softmax(1.0 / math.sqrt(DH * rows), full, half, flip(half, "z", Z, 1))
    probs = lax.all_to_all(probs, ("y", "xh"), 0, 0, tiled=True)
    laid = values_laid(me, gather4(jnp.stack(v)))
    mixed = lax.all_to_all(mix(me, laid, probs), ("z", "c"), 0, 0, tiled=True)
    return final(mixed, wf)


def solution(mesh):
    fine = Mesh(mesh.devices.reshape(4, 2, 2, 8, 2), ("y", "xh", "c", "z", "xl"))
    spec = P(("y", "xh", "c"), ("z", "xl"), None)
    return jax.shard_map(
        local,
        mesh=fine,
        in_specs=(spec, P(), P(), P(), P()),
        out_specs=spec,
        check_vma=False,
    )
```

```python
import functools
import math

import jax
import jax.numpy as jnp
from jax import lax
from jax.experimental import pallas as pl
from jax.experimental.pallas import tpu as pltpu
from jax.sharding import Mesh, PartitionSpec as P

H = 12
DH = 64
EMBED = 768
ROWS = 8
RES = 64
Z = 8
CHUNK = EMBED // Z
FULL = DH
HALF = CHUNK - DH
PEERS = 8
SUB = RES // 2
TOKENS = ROWS * SUB
QUERIES = Z * SUB
KEYS = 2 * Z * RES
LOGITS = KEYS + KEYS // 2

f32 = jnp.float32
bf16 = jnp.bfloat16
PARAMS = pltpu.CompilerParams(vmem_limit_bytes=16 * 1024 * 1024)
PROJECTION = pl.CostEstimate(
    flops=2 * ROWS * RES * EMBED * EMBED, bytes_accessed=2 * EMBED * (EMBED + 2 * ROWS * RES), transcendentals=0
)
LAYOUT = pl.CostEstimate(flops=0, bytes_accessed=16 * ROWS * RES * EMBED, transcendentals=0)
KEY_SHAPES = ((2 * ROWS * FULL, KEYS // 2), (2 * ROWS * FULL, KEYS // 4))
WIDE = pltpu.CompilerParams(vmem_limit_bytes=16 * 1024 * 1024)
VMEM = pl.BlockSpec(memory_space=pltpu.VMEM)
SMEM = pl.BlockSpec(memory_space=pltpu.SMEM)
ANY = pl.BlockSpec(memory_space=pl.ANY)
HBM = pl.BlockSpec(memory_space=pltpu.HBM)


def chunk_pieces(z):
    base = z * CHUNK
    if z % 2 == 0:
        return (base, FULL), (base + FULL, HALF)
    return (base + HALF, FULL), (base, HALF)


def dot(a, b, ca, cb):
    return lax.dot_general(a, b, (((ca,), (cb,)), ((), ())), preferred_element_type=f32)


def shared_head(z):
    return z // 2 * (2 * CHUNK) + FULL


def chunk_rows(z):
    odd = lax.rem(z, 2)
    base = z * CHUNK
    return pl.multiple_of(base + odd * HALF, HALF), pl.multiple_of(base + (1 - odd) * FULL, HALF)


def fetches(sources, buffers, sems):
    copies = [pltpu.make_async_copy(a, b, sems.at[i]) for i, (a, b) in enumerate(zip(sources, buffers))]
    for copy in copies:
        copy.start()
    return copies


def in_hbm(*arrays):
    return [pltpu.with_memory_space_constraint(a, pltpu.HBM) for a in arrays]


def key_kernel(me_ref, x_hbm, w_hbm, n_ref, *rest):
    outs, (x_ref, w_ref, t_ref, sems) = rest[:Z], rest[Z:]
    copy_x, copy_w = fetches((x_hbm, w_hbm), (x_ref, w_ref), sems)
    copy_x.wait()
    x = x_ref[...].astype(f32)
    centred = x - jnp.mean(x, axis=-1, keepdims=True)
    var = jnp.mean(centred * centred, axis=-1, keepdims=True)
    normed = (centred * lax.rsqrt(var + 1e-05)).astype(bf16)
    for h in range(2):
        n_ref[h] = normed[:, h * SUB : (h + 1) * SUB, :]
    copy_w.wait()
    t_ref[...] = dot(w_ref[...], n_ref[...].reshape(ROWS * RES, EMBED), 0, 1).astype(bf16)
    for s, out in enumerate(outs):
        z = lax.rem(me_ref[2] + s, Z)
        first, odd = shared_head(z), lax.rem(z, 2)
        lanes = pl.ds(pl.multiple_of(odd * TOKENS, TOKENS), TOKENS)
        out[0:FULL, :] = t_ref[pl.ds(chunk_rows(z)[0], FULL), :]
        for d in range(2):
            rows = pl.ds(pl.multiple_of(first + d * HALF, HALF), HALF)
            out[FULL:CHUNK, d * TOKENS : (d + 1) * TOKENS] = t_ref[rows, lanes]


def key_chunks(me, x, w):
    n, *k = pl.pallas_call(
        key_kernel,
        out_shape=(jax.ShapeDtypeStruct((2, ROWS, SUB, EMBED), bf16),)
        + (jax.ShapeDtypeStruct((CHUNK, ROWS * RES), bf16),) * Z,
        in_specs=[SMEM, ANY, ANY],
        out_specs=(VMEM,) * (1 + Z),
        scratch_shapes=[
            pltpu.VMEM((ROWS, RES, EMBED), bf16),
            pltpu.VMEM((EMBED, EMBED), bf16),
            pltpu.VMEM((EMBED, ROWS * RES), bf16),
            pltpu.SemaphoreType.DMA((2,)),
        ],
        compiler_params=PARAMS,
    )(me, *in_hbm(x, w))
    return n, k


def query_kernel(n_ref, w_ref, q_ref):
    for c in range(2):
        t = dot(w_ref[...], n_ref[c].reshape(TOKENS, EMBED), 0, 1).astype(bf16)
        for z in range(Z):
            a, b = chunk_pieces(z)[0][0], shared_head(z)
            q_ref[2 * z + c, 0:FULL, :] = t[a : a + FULL]
            q_ref[2 * z + c, FULL:, :] = t[b : b + FULL]


def query_chunks(n, w):
    return pl.pallas_call(
        query_kernel,
        out_shape=jax.ShapeDtypeStruct((2 * Z, 2 * FULL, TOKENS), bf16),
        in_specs=[VMEM] * 2,
        out_specs=VMEM,
        compiler_params=PARAMS,
        cost_estimate=PROJECTION,
    )(n, w)


def value_kernel(me_ref, n_ref, w_ref, *rest):
    outs, t_ref = rest[:Z], rest[Z]
    t_ref[...] = dot(w_ref[...], n_ref[...].reshape(ROWS * RES, EMBED), 0, 1).astype(bf16)
    for s, out in enumerate(outs):
        full, half = chunk_rows(lax.rem(me_ref[2] + s, Z))
        out[0:FULL, :] = t_ref[pl.ds(full, FULL), :]
        out[FULL:CHUNK, :] = t_ref[pl.ds(half, HALF), :]


def value_chunks(me, n, w):
    return pl.pallas_call(
        value_kernel,
        out_shape=(jax.ShapeDtypeStruct((CHUNK, ROWS * RES), bf16),) * Z,
        in_specs=[SMEM, VMEM, VMEM],
        out_specs=(VMEM,) * Z,
        scratch_shapes=[pltpu.VMEM((EMBED, ROWS * RES), bf16)],
        compiler_params=PARAMS,
        cost_estimate=PROJECTION,
    )(me, n, w)


def lay_keys(me, own, other, kf, kh):
    where = [lax.rem(me - z + Z, Z) for z in range(Z)]
    for cr, ref in enumerate((own, other)):
        for r in range(ROWS):
            n = (cr * ROWS + r) * FULL
            whole = [ref[z, 0:FULL, h * TOKENS + r * SUB : h * TOKENS + (r + 1) * SUB] for z in where for h in range(2)]
            kf[n : n + FULL, :] = jnp.concatenate(whole, axis=1)
            for d in range(2):
                first = d * TOKENS + r * SUB
                shared = [ref[z, FULL:CHUNK, first : first + SUB] for z in where]
                kh[n + d * HALF : n + (d + 1) * HALF, :] = jnp.concatenate(shared, axis=1)


def keys_kernel(me_ref, own, other, kf, kh):
    lay_keys(me_ref[2], own, other, kf, kh)


def keys_laid(me, own, other):
    return pl.pallas_call(
        keys_kernel,
        out_shape=tuple(jax.ShapeDtypeStruct(s, bf16) for s in KEY_SHAPES),
        in_specs=[SMEM, VMEM, VMEM],
        out_specs=(VMEM,) * 2,
        compiler_params=PARAMS,
        cost_estimate=LAYOUT,
    )(me, own, other)


def score_kernel(me_ref, q_hbm, kf_hbm, kh_hbm, own_hbm, other_hbm, out, qf, qh, kf1, kh1, *rest):
    own, other, q_ref, kf0, kh0, sems = rest
    copies = fetches((own_hbm, other_hbm, q_hbm, kf_hbm, kh_hbm), rest[:5], sems)
    for copy in copies[:2]:
        copy.wait()
    lay_keys(me_ref[2], own, other, kf1, kh1)
    for copy in copies[2:]:
        copy.wait()
    for cr in range(2):
        c = jnp.bitwise_xor(me_ref[1], cr)
        queries = [q_ref[2 * p + c] for p in range(PEERS)]
        for r in range(ROWS):
            n = (cr * ROWS + r) * FULL
            t = jnp.concatenate([b[:, r * SUB : (r + 1) * SUB] for b in queries], axis=1)
            qf[n : n + FULL, :] = t[:FULL]
            qh[n : n + FULL, :] = t[FULL:]
    first = 0
    for a, b in ((qf, kf0), (qf, kf1), (qh, kh0), (qh, kh1)):
        t = dot(a[...], b[...], 0, 0)
        for p in range(PEERS):
            out[p, :, first : first + t.shape[1]] = t[p * SUB : (p + 1) * SUB]
        first += t.shape[1]


def score(me, q, laid, own, other):
    rows = 2 * ROWS * FULL
    return pl.pallas_call(
        score_kernel,
        out_shape=jax.ShapeDtypeStruct((PEERS, SUB, LOGITS), f32),
        in_specs=[SMEM] + [ANY] * 5,
        out_specs=VMEM,
        scratch_shapes=[pltpu.VMEM((rows, QUERIES), bf16)] * 2
        + [pltpu.VMEM(s, bf16) for s in KEY_SHAPES]
        + [pltpu.VMEM(a.shape, bf16) for a in (own, other, q, *laid)]
        + [pltpu.SemaphoreType.DMA((5,))],
        compiler_params=PARAMS,
    )(me, *in_hbm(q), *laid, *in_hbm(own), other)


def total_kernel(parts, full, half):
    t = parts[0]
    for p in range(1, PEERS):
        t = t + parts[p]
    full[...] = t[:, :KEYS]
    half[...] = t[:, KEYS:]


def total(parts):
    return pl.pallas_call(
        total_kernel,
        out_shape=tuple(jax.ShapeDtypeStruct((SUB, n), f32) for n in (KEYS, KEYS // 2)),
        in_specs=[VMEM],
        out_specs=(VMEM,) * 2,
        compiler_params=PARAMS,
    )(parts)


def softmax_kernel(factor, full, half, other, out):
    for i, logits in enumerate((full[...], jnp.concatenate([half[...], other[...]], axis=1))):
        logits = logits * factor
        powered = jnp.exp(logits - jnp.max(logits, axis=-1, keepdims=True))
        probs = (powered / jnp.sum(powered, axis=-1, keepdims=True)).astype(bf16)
        for p in range(PEERS):
            out[p, i] = probs


def softmax(factor, full, half, other):
    return pl.pallas_call(
        functools.partial(softmax_kernel, factor),
        out_shape=jax.ShapeDtypeStruct((PEERS, 2, SUB, KEYS), bf16),
        in_specs=[VMEM] * 3,
        out_specs=VMEM,
        compiler_params=PARAMS,
    )(full, half, other)


def values_kernel(me_ref, *refs):
    (vf, vh), (v00, v01, v10, v11), sems = refs[4:6], refs[6:10], refs[10]
    for copy in fetches(refs[:4], refs[6:10], sems):
        copy.wait()
    z = me_ref[2]
    odd = lax.rem(z, 2)
    where = [lax.rem(z - source + Z, Z) for source in range(Z)]
    for cr, refs in enumerate(((v00, v01), (v10, v11))):
        halves = [
            ref[i, FULL:CHUNK, pl.ds(pl.multiple_of(h * TOKENS, TOKENS), TOKENS)]
            for h in (odd, 1 - odd)
            for ref in refs
            for i in where
        ]
        whole = [ref[i, 0:FULL, h * TOKENS : (h + 1) * TOKENS] for ref in refs for i in where for h in range(2)]
        for r in range(ROWS):
            n = cr * ROWS + r
            lanes = slice(r * SUB, (r + 1) * SUB)
            vf[n * FULL : (n + 1) * FULL, :] = jnp.concatenate([b[:, lanes] for b in whole], axis=1)
            vh[n * HALF : (n + 1) * HALF, :] = jnp.concatenate([b[:, lanes] for b in halves], axis=1)


def values_laid(me, vs):
    return pl.pallas_call(
        values_kernel,
        out_shape=(
            jax.ShapeDtypeStruct((2 * ROWS * FULL, KEYS), bf16),
            pltpu.HBM((2 * ROWS * HALF, KEYS), bf16),
        ),
        in_specs=[SMEM] + [ANY] * 4,
        out_specs=(VMEM,) * 2,
        scratch_shapes=[pltpu.VMEM(v.shape, bf16) for v in vs] + [pltpu.SemaphoreType.DMA((4,))],
        compiler_params=PARAMS,
        cost_estimate=LAYOUT,
    )(me, *in_hbm(*vs[:2]), *vs[2:])


def mix_kernel(me_ref, vf, vh_hbm, p_ref, o_ref, vh, sems):
    core = me_ref[1]
    copy = fetches((vh_hbm,), (vh,), sems)[0]
    for i, (v, first, n) in enumerate(((vf, 0, FULL), (vh, FULL, HALF))):
        if i == 1:
            copy.wait()
        probs = p_ref[:, i].reshape(QUERIES, KEYS)
        for cr in range(2):
            c = jnp.bitwise_xor(core, cr)
            mixed = dot(v[cr * ROWS * n : (cr + 1) * ROWS * n, :], probs, 1, 1).astype(bf16)
            for s in range(PEERS):
                o_ref[2 * s + c, first : first + n, :] = jnp.concatenate(
                    [mixed[r * n : (r + 1) * n, s * SUB : (s + 1) * SUB] for r in range(ROWS)], axis=1
                )


def mix(me, laid, probs):
    whole, shared = laid
    return pl.pallas_call(
        mix_kernel,
        out_shape=jax.ShapeDtypeStruct((2 * Z, CHUNK, ROWS * SUB), bf16),
        in_specs=[SMEM, VMEM, ANY, VMEM],
        out_specs=VMEM,
        scratch_shapes=[pltpu.VMEM(shared.shape, bf16), pltpu.SemaphoreType.DMA((1,))],
        compiler_params=PARAMS,
    )(me, whole, *in_hbm(shared), probs)


def final_kernel(m_ref, w_ref, o_ref, t_ref):
    for c in range(2):
        for z in range(Z):
            (a, na), (b, nb) = chunk_pieces(z)
            t_ref[a : a + na, :] = m_ref[2 * z + c, 0:FULL, :]
            t_ref[b : b + nb, :] = m_ref[2 * z + c, FULL:CHUNK, :]
        attended = dot(t_ref[...], w_ref[...], 0, 0).astype(bf16)
        o_ref[:, c * SUB : (c + 1) * SUB, :] = attended.reshape(ROWS, SUB, EMBED)


def final(m, w):
    return pl.pallas_call(
        final_kernel,
        out_shape=jax.ShapeDtypeStruct((ROWS, RES, EMBED), bf16),
        in_specs=[VMEM] * 2,
        out_specs=VMEM,
        scratch_shapes=[pltpu.VMEM((EMBED, ROWS * SUB), bf16)],
        compiler_params=PARAMS,
    )(m, w)


def flip(x, axes, n, s):
    return lax.ppermute(x, axes, [(i, i ^ s) for i in range(n)])


def gather4(own):
    far = flip(own, "xl", 2, 1)
    return own, far, flip(own, "c", 2, 1), flip(far, "c", 2, 1)


def shift(x, s):
    return lax.ppermute(x, "z", [(i, (i + s) % Z) for i in range(Z)])


def local(x, wq, wk, wv, wf):
    me = jnp.stack([lax.axis_index(("y", "xh")), lax.axis_index("c"), lax.axis_index("z")])
    me = me.astype(jnp.int32)
    n, k = key_chunks(me, x, wk)
    for s in (4, 3, 5, 2, 6, 1, 7):
        k[s] = shift(k[s], s)
    early = (4, 3, 5, 2)
    q, *got = lax.optimization_barrier((query_chunks(n, wq), *(k[s] for s in early)))
    for s, a in zip(early, got):
        k[s] = a
    q = lax.all_to_all(q, ("z", "c"), 0, 0, tiled=True)
    v = list(value_chunks(me, n, wv))
    k = jnp.stack(k)
    near, shared = keys_laid(me, k, flip(k, "c", 2, 1))
    k_far, v[4], shared = lax.optimization_barrier((flip(k, "xl", 2, 1), v[4], shared))
    for s in (2, 6):
        v[s] = shift(v[s], s)
    scores = score(me, q, (near, shared), k_far, flip(k_far, "c", 2, 1))
    *v, scores = lax.optimization_barrier((*v, scores))
    parts = lax.all_to_all(scores, ("y", "xh"), 0, 0, tiled=True)
    for s in (4, 3, 5, 1, 7):
        v[s] = shift(v[s], s)
    full, half = total(parts)
    rows = ROWS * 2 * PEERS
    probs = softmax(1.0 / math.sqrt(DH * rows), full, half, flip(half, "z", Z, 1))
    probs = lax.all_to_all(probs, ("y", "xh"), 0, 0, tiled=True)
    laid = values_laid(me, gather4(jnp.stack(v)))
    mixed = lax.all_to_all(mix(me, laid, probs), ("z", "c"), 0, 0, tiled=True)
    return final(mixed, wf)


def solution(mesh):
    fine = Mesh(mesh.devices.reshape(4, 2, 2, 8, 2), ("y", "xh", "c", "z", "xl"))
    spec = P(("y", "xh", "c"), ("z", "xl"), None)
    return jax.shard_map(
        local,
        mesh=fine,
        in_specs=(spec, P(), P(), P(), P()),
        out_specs=spec,
        check_vma=False,
    )
```

```python
import functools
import math

import jax
import jax.numpy as jnp
from jax import lax
from jax.experimental import pallas as pl
from jax.experimental.pallas import tpu as pltpu
from jax.sharding import Mesh, PartitionSpec as P

H = 12
DH = 64
EMBED = 768
ROWS = 8
RES = 64
Z = 8
CHUNK = EMBED // Z
FULL = DH
HALF = CHUNK - DH
PEERS = 8
SUB = RES // 2
TOKENS = ROWS * SUB
QUERIES = Z * SUB
KEYS = 2 * Z * RES
LOGITS = KEYS + KEYS // 2

f32 = jnp.float32
bf16 = jnp.bfloat16
PARAMS = pltpu.CompilerParams(vmem_limit_bytes=16 * 1024 * 1024)
PROJECTION = pl.CostEstimate(
    flops=2 * ROWS * RES * EMBED * EMBED, bytes_accessed=2 * EMBED * (EMBED + 2 * ROWS * RES), transcendentals=0
)
LAYOUT = pl.CostEstimate(flops=0, bytes_accessed=16 * ROWS * RES * EMBED, transcendentals=0)
KEY_SHAPES = ((2 * ROWS * FULL, KEYS // 2), (2 * ROWS * FULL, KEYS // 4))
WIDE = pltpu.CompilerParams(vmem_limit_bytes=16 * 1024 * 1024)
VMEM = pl.BlockSpec(memory_space=pltpu.VMEM)
SMEM = pl.BlockSpec(memory_space=pltpu.SMEM)
ANY = pl.BlockSpec(memory_space=pl.ANY)
HBM = pl.BlockSpec(memory_space=pltpu.HBM)


def chunk_pieces(z):
    base = z * CHUNK
    if z % 2 == 0:
        return (base, FULL), (base + FULL, HALF)
    return (base + HALF, FULL), (base, HALF)


def dot(a, b, ca, cb):
    return lax.dot_general(a, b, (((ca,), (cb,)), ((), ())), preferred_element_type=f32)


def shared_head(z):
    return z // 2 * (2 * CHUNK) + FULL


def chunk_rows(z):
    odd = lax.rem(z, 2)
    base = z * CHUNK
    return pl.multiple_of(base + odd * HALF, HALF), pl.multiple_of(base + (1 - odd) * FULL, HALF)


def fetches(sources, buffers, sems):
    copies = [pltpu.make_async_copy(a, b, sems.at[i]) for i, (a, b) in enumerate(zip(sources, buffers))]
    for copy in copies:
        copy.start()
    return copies


def in_hbm(*arrays):
    return [pltpu.with_memory_space_constraint(a, pltpu.HBM) for a in arrays]


def key_kernel(me_ref, x_hbm, w_hbm, n_ref, *rest):
    outs, (x_ref, w_ref, t_ref, sems) = rest[:Z], rest[Z:]
    rows = [slice(r, r + 2) for r in range(0, ROWS, 2)]
    columns = [slice(c, c + EMBED // 4) for c in range(0, EMBED, EMBED // 4)]
    copies = fetches(
        [x_hbm.at[r] for r in rows] + [w_hbm.at[c] for c in columns],
        [x_ref.at[r] for r in rows] + [w_ref.at[c] for c in columns],
        sems,
    )
    for r, copy in zip(rows, copies):
        copy.wait()
        x = x_ref[r].astype(f32)
        centred = x - jnp.mean(x, axis=-1, keepdims=True)
        var = jnp.mean(centred * centred, axis=-1, keepdims=True)
        normed = (centred * lax.rsqrt(var + 1e-05)).astype(bf16)
        for h in range(2):
            n_ref[h, r] = normed[:, h * SUB : (h + 1) * SUB, :]
    for copy in copies[len(rows) :]:
        copy.wait()
    t_ref[...] = dot(w_ref[...], n_ref[...].reshape(ROWS * RES, EMBED), 0, 1).astype(bf16)
    for s, out in enumerate(outs):
        z = lax.rem(me_ref[2] + s, Z)
        first, odd = shared_head(z), lax.rem(z, 2)
        lanes = pl.ds(pl.multiple_of(odd * TOKENS, TOKENS), TOKENS)
        out[0:FULL, :] = t_ref[pl.ds(chunk_rows(z)[0], FULL), :]
        for d in range(2):
            rows = pl.ds(pl.multiple_of(first + d * HALF, HALF), HALF)
            out[FULL:CHUNK, d * TOKENS : (d + 1) * TOKENS] = t_ref[rows, lanes]


def key_chunks(me, x, w):
    n, *k = pl.pallas_call(
        key_kernel,
        out_shape=(jax.ShapeDtypeStruct((2, ROWS, SUB, EMBED), bf16),)
        + (jax.ShapeDtypeStruct((CHUNK, ROWS * RES), bf16),) * Z,
        in_specs=[SMEM, ANY, ANY],
        out_specs=(VMEM,) * (1 + Z),
        scratch_shapes=[
            pltpu.VMEM((ROWS, RES, EMBED), bf16),
            pltpu.VMEM((EMBED, EMBED), bf16),
            pltpu.VMEM((EMBED, ROWS * RES), bf16),
            pltpu.SemaphoreType.DMA((8,)),
        ],
        compiler_params=PARAMS,
    )(me, *in_hbm(x, w))
    return n, k


def query_kernel(n_ref, w_ref, q_ref):
    for c in range(2):
        t = dot(w_ref[...], n_ref[c].reshape(TOKENS, EMBED), 0, 1).astype(bf16)
        for z in range(Z):
            a, b = chunk_pieces(z)[0][0], shared_head(z)
            q_ref[2 * z + c, 0:FULL, :] = t[a : a + FULL]
            q_ref[2 * z + c, FULL:, :] = t[b : b + FULL]


def query_chunks(n, w):
    return pl.pallas_call(
        query_kernel,
        out_shape=jax.ShapeDtypeStruct((2 * Z, 2 * FULL, TOKENS), bf16),
        in_specs=[VMEM] * 2,
        out_specs=VMEM,
        compiler_params=PARAMS,
        cost_estimate=PROJECTION,
    )(n, w)


def value_kernel(me_ref, n_ref, w_ref, *rest):
    outs, t_ref = rest[:Z], rest[Z]
    t_ref[...] = dot(w_ref[...], n_ref[...].reshape(ROWS * RES, EMBED), 0, 1).astype(bf16)
    for s, out in enumerate(outs):
        full, half = chunk_rows(lax.rem(me_ref[2] + s, Z))
        out[0:FULL, :] = t_ref[pl.ds(full, FULL), :]
        out[FULL:CHUNK, :] = t_ref[pl.ds(half, HALF), :]


def value_chunks(me, n, w):
    return pl.pallas_call(
        value_kernel,
        out_shape=(jax.ShapeDtypeStruct((CHUNK, ROWS * RES), bf16),) * Z,
        in_specs=[SMEM, VMEM, VMEM],
        out_specs=(VMEM,) * Z,
        scratch_shapes=[pltpu.VMEM((EMBED, ROWS * RES), bf16)],
        compiler_params=PARAMS,
        cost_estimate=PROJECTION,
    )(me, n, w)


def lay_keys(me, own, other, kf, kh):
    where = [lax.rem(me - z + Z, Z) for z in range(Z)]
    for cr, ref in enumerate((own, other)):
        for r in range(ROWS):
            n = (cr * ROWS + r) * FULL
            whole = [ref[z, 0:FULL, h * TOKENS + r * SUB : h * TOKENS + (r + 1) * SUB] for z in where for h in range(2)]
            kf[n : n + FULL, :] = jnp.concatenate(whole, axis=1)
            for d in range(2):
                first = d * TOKENS + r * SUB
                shared = [ref[z, FULL:CHUNK, first : first + SUB] for z in where]
                kh[n + d * HALF : n + (d + 1) * HALF, :] = jnp.concatenate(shared, axis=1)


def keys_kernel(me_ref, own, other, kf, kh):
    lay_keys(me_ref[2], own, other, kf, kh)


def keys_laid(me, own, other):
    return pl.pallas_call(
        keys_kernel,
        out_shape=tuple(jax.ShapeDtypeStruct(s, bf16) for s in KEY_SHAPES),
        in_specs=[SMEM, VMEM, VMEM],
        out_specs=(VMEM,) * 2,
        compiler_params=PARAMS,
        cost_estimate=LAYOUT,
    )(me, own, other)


def score_kernel(me_ref, q_hbm, kf_hbm, kh_hbm, own_hbm, other_hbm, out, qf, qh, kf1, kh1, *rest):
    own, other, q_ref, kf0, kh0, sems = rest
    copies = fetches((own_hbm, other_hbm, q_hbm, kf_hbm, kh_hbm), rest[:5], sems)
    for copy in copies[:2]:
        copy.wait()
    lay_keys(me_ref[2], own, other, kf1, kh1)
    for copy in copies[2:]:
        copy.wait()
    for cr in range(2):
        c = jnp.bitwise_xor(me_ref[1], cr)
        queries = [q_ref[2 * p + c] for p in range(PEERS)]
        for r in range(ROWS):
            n = (cr * ROWS + r) * FULL
            t = jnp.concatenate([b[:, r * SUB : (r + 1) * SUB] for b in queries], axis=1)
            qf[n : n + FULL, :] = t[:FULL]
            qh[n : n + FULL, :] = t[FULL:]
    first = 0
    for a, b in ((qf, kf0), (qf, kf1), (qh, kh0), (qh, kh1)):
        t = dot(a[...], b[...], 0, 0)
        for p in range(PEERS):
            out[p, :, first : first + t.shape[1]] = t[p * SUB : (p + 1) * SUB]
        first += t.shape[1]


def score(me, q, laid, own, other):
    rows = 2 * ROWS * FULL
    return pl.pallas_call(
        score_kernel,
        out_shape=jax.ShapeDtypeStruct((PEERS, SUB, LOGITS), f32),
        in_specs=[SMEM] + [ANY] * 5,
        out_specs=VMEM,
        scratch_shapes=[pltpu.VMEM((rows, QUERIES), bf16)] * 2
        + [pltpu.VMEM(s, bf16) for s in KEY_SHAPES]
        + [pltpu.VMEM(a.shape, bf16) for a in (own, other, q, *laid)]
        + [pltpu.SemaphoreType.DMA((5,))],
        compiler_params=PARAMS,
    )(me, *in_hbm(q), *laid, *in_hbm(own), other)


def total_kernel(parts, full, half):
    t = parts[0]
    for p in range(1, PEERS):
        t = t + parts[p]
    full[...] = t[:, :KEYS]
    half[...] = t[:, KEYS:]


def total(parts):
    return pl.pallas_call(
        total_kernel,
        out_shape=tuple(jax.ShapeDtypeStruct((SUB, n), f32) for n in (KEYS, KEYS // 2)),
        in_specs=[VMEM],
        out_specs=(VMEM,) * 2,
        compiler_params=PARAMS,
    )(parts)


def softmax_kernel(factor, full, half, other, out):
    for i, logits in enumerate((full[...], jnp.concatenate([half[...], other[...]], axis=1))):
        logits = logits * factor
        powered = jnp.exp(logits - jnp.max(logits, axis=-1, keepdims=True))
        probs = (powered / jnp.sum(powered, axis=-1, keepdims=True)).astype(bf16)
        for p in range(PEERS):
            out[p, i] = probs


def softmax(factor, full, half, other):
    return pl.pallas_call(
        functools.partial(softmax_kernel, factor),
        out_shape=jax.ShapeDtypeStruct((PEERS, 2, SUB, KEYS), bf16),
        in_specs=[VMEM] * 3,
        out_specs=VMEM,
        compiler_params=PARAMS,
    )(full, half, other)


def values_kernel(me_ref, *refs):
    (vf, vh), (v00, v01, v10, v11), sems = refs[4:6], refs[6:10], refs[10]
    for copy in fetches(refs[:4], refs[6:10], sems):
        copy.wait()
    z = me_ref[2]
    odd = lax.rem(z, 2)
    where = [lax.rem(z - source + Z, Z) for source in range(Z)]
    for cr, refs in enumerate(((v00, v01), (v10, v11))):
        halves = [
            ref[i, FULL:CHUNK, pl.ds(pl.multiple_of(h * TOKENS, TOKENS), TOKENS)]
            for h in (odd, 1 - odd)
            for ref in refs
            for i in where
        ]
        whole = [ref[i, 0:FULL, h * TOKENS : (h + 1) * TOKENS] for ref in refs for i in where for h in range(2)]
        for r in range(ROWS):
            n = cr * ROWS + r
            lanes = slice(r * SUB, (r + 1) * SUB)
            vf[n * FULL : (n + 1) * FULL, :] = jnp.concatenate([b[:, lanes] for b in whole], axis=1)
            vh[n * HALF : (n + 1) * HALF, :] = jnp.concatenate([b[:, lanes] for b in halves], axis=1)


def values_laid(me, vs):
    return pl.pallas_call(
        values_kernel,
        out_shape=(
            jax.ShapeDtypeStruct((2 * ROWS * FULL, KEYS), bf16),
            pltpu.HBM((2 * ROWS * HALF, KEYS), bf16),
        ),
        in_specs=[SMEM] + [ANY] * 4,
        out_specs=(VMEM,) * 2,
        scratch_shapes=[pltpu.VMEM(v.shape, bf16) for v in vs] + [pltpu.SemaphoreType.DMA((4,))],
        compiler_params=PARAMS,
        cost_estimate=LAYOUT,
    )(me, *in_hbm(*vs[:2]), *vs[2:])


def mix_kernel(me_ref, vf, vh_hbm, p_ref, o_ref, vh, sems):
    core = me_ref[1]
    copy = fetches((vh_hbm,), (vh,), sems)[0]
    for i, (v, first, n) in enumerate(((vf, 0, FULL), (vh, FULL, HALF))):
        if i == 1:
            copy.wait()
        probs = p_ref[:, i].reshape(QUERIES, KEYS)
        for cr in range(2):
            c = jnp.bitwise_xor(core, cr)
            mixed = dot(v[cr * ROWS * n : (cr + 1) * ROWS * n, :], probs, 1, 1).astype(bf16)
            for s in range(PEERS):
                o_ref[2 * s + c, first : first + n, :] = jnp.concatenate(
                    [mixed[r * n : (r + 1) * n, s * SUB : (s + 1) * SUB] for r in range(ROWS)], axis=1
                )


def mix(me, laid, probs):
    whole, shared = laid
    return pl.pallas_call(
        mix_kernel,
        out_shape=jax.ShapeDtypeStruct((2 * Z, CHUNK, ROWS * SUB), bf16),
        in_specs=[SMEM, VMEM, ANY, VMEM],
        out_specs=VMEM,
        scratch_shapes=[pltpu.VMEM(shared.shape, bf16), pltpu.SemaphoreType.DMA((1,))],
        compiler_params=PARAMS,
    )(me, whole, *in_hbm(shared), probs)


def final_kernel(m_ref, w_ref, o_ref, t_ref):
    for c in range(2):
        for z in range(Z):
            (a, na), (b, nb) = chunk_pieces(z)
            t_ref[a : a + na, :] = m_ref[2 * z + c, 0:FULL, :]
            t_ref[b : b + nb, :] = m_ref[2 * z + c, FULL:CHUNK, :]
        attended = dot(t_ref[...], w_ref[...], 0, 0).astype(bf16)
        o_ref[:, c * SUB : (c + 1) * SUB, :] = attended.reshape(ROWS, SUB, EMBED)


def final(m, w):
    return pl.pallas_call(
        final_kernel,
        out_shape=jax.ShapeDtypeStruct((ROWS, RES, EMBED), bf16),
        in_specs=[VMEM] * 2,
        out_specs=VMEM,
        scratch_shapes=[pltpu.VMEM((EMBED, ROWS * SUB), bf16)],
        compiler_params=PARAMS,
    )(m, w)


def flip(x, axes, n, s):
    return lax.ppermute(x, axes, [(i, i ^ s) for i in range(n)])


def gather4(own):
    far = flip(own, "xl", 2, 1)
    return own, far, flip(own, "c", 2, 1), flip(far, "c", 2, 1)


def shift(x, s):
    return lax.ppermute(x, "z", [(i, (i + s) % Z) for i in range(Z)])


def local(x, wq, wk, wv, wf):
    me = jnp.stack([lax.axis_index(("y", "xh")), lax.axis_index("c"), lax.axis_index("z")])
    me = me.astype(jnp.int32)
    n, k = key_chunks(me, x, wk)
    for s in (1, 7, 2, 6, 3, 5, 4):
        k[s] = shift(k[s], s)
    early = (1, 7, 2, 6, 3)
    q, *got = lax.optimization_barrier((query_chunks(n, wq), *(k[s] for s in early)))
    for s, a in zip(early, got):
        k[s] = a
    q = lax.all_to_all(q, ("z", "c"), 0, 0, tiled=True)
    v = list(value_chunks(me, n, wv))
    k = jnp.stack(k)
    near, shared = keys_laid(me, k, flip(k, "c", 2, 1))
    k_far, v[4], shared = lax.optimization_barrier((flip(k, "xl", 2, 1), v[4], shared))
    for s in (2, 6):
        v[s] = shift(v[s], s)
    scores = score(me, q, (near, shared), k_far, flip(k_far, "c", 2, 1))
    *v, scores = lax.optimization_barrier((*v, scores))
    parts = lax.all_to_all(scores, ("y", "xh"), 0, 0, tiled=True)
    for s in (4, 3, 5, 1, 7):
        v[s] = shift(v[s], s)
    full, half = total(parts)
    rows = ROWS * 2 * PEERS
    probs = softmax(1.0 / math.sqrt(DH * rows), full, half, flip(half, "z", Z, 1))
    probs = lax.all_to_all(probs, ("y", "xh"), 0, 0, tiled=True)
    laid = values_laid(me, gather4(jnp.stack(v)))
    mixed = lax.all_to_all(mix(me, laid, probs), ("z", "c"), 0, 0, tiled=True)
    return final(mixed, wf)


def solution(mesh):
    fine = Mesh(mesh.devices.reshape(4, 2, 2, 8, 2), ("y", "xh", "c", "z", "xl"))
    spec = P(("y", "xh", "c"), ("z", "xl"), None)
    return jax.shard_map(
        local,
        mesh=fine,
        in_specs=(spec, P(), P(), P(), P()),
        out_specs=spec,
        check_vma=False,
    )
```

```python
import functools
import math

import jax
import jax.numpy as jnp
from jax import lax
from jax.experimental import pallas as pl
from jax.experimental.pallas import tpu as pltpu
from jax.sharding import Mesh, PartitionSpec as P

H = 12
DH = 64
EMBED = 768
ROWS = 8
RES = 64
Z = 8
CHUNK = EMBED // Z
FULL = DH
HALF = CHUNK - DH
PEERS = 8
SUB = RES // 2
TOKENS = ROWS * SUB
QUERIES = Z * SUB
KEYS = 2 * Z * RES
LOGITS = KEYS + KEYS // 2

f32 = jnp.float32
bf16 = jnp.bfloat16
PARAMS = pltpu.CompilerParams(vmem_limit_bytes=16 * 1024 * 1024)
PROJECTION = pl.CostEstimate(
    flops=2 * ROWS * RES * EMBED * EMBED, bytes_accessed=2 * EMBED * (EMBED + 2 * ROWS * RES), transcendentals=0
)
LAYOUT = pl.CostEstimate(flops=0, bytes_accessed=16 * ROWS * RES * EMBED, transcendentals=0)
KEY_SHAPES = ((2 * ROWS * FULL, KEYS // 2), (2 * ROWS * FULL, KEYS // 4))
WIDE = pltpu.CompilerParams(vmem_limit_bytes=16 * 1024 * 1024)
VMEM = pl.BlockSpec(memory_space=pltpu.VMEM)
SMEM = pl.BlockSpec(memory_space=pltpu.SMEM)
ANY = pl.BlockSpec(memory_space=pl.ANY)
HBM = pl.BlockSpec(memory_space=pltpu.HBM)


def chunk_pieces(z):
    base = z * CHUNK
    if z % 2 == 0:
        return (base, FULL), (base + FULL, HALF)
    return (base + HALF, FULL), (base, HALF)


def dot(a, b, ca, cb):
    return lax.dot_general(a, b, (((ca,), (cb,)), ((), ())), preferred_element_type=f32)


def shared_head(z):
    return z // 2 * (2 * CHUNK) + FULL


def chunk_rows(z):
    odd = lax.rem(z, 2)
    base = z * CHUNK
    return pl.multiple_of(base + odd * HALF, HALF), pl.multiple_of(base + (1 - odd) * FULL, HALF)


def fetches(sources, buffers, sems):
    copies = [pltpu.make_async_copy(a, b, sems.at[i]) for i, (a, b) in enumerate(zip(sources, buffers))]
    for copy in copies:
        copy.start()
    return copies


def in_hbm(*arrays):
    return [pltpu.with_memory_space_constraint(a, pltpu.HBM) for a in arrays]


def key_kernel(me_ref, x_hbm, w_hbm, n_ref, *rest):
    outs, (x_ref, w_ref, t_ref, sems) = rest[:Z], rest[Z:]
    copy_x, copy_w = fetches((x_hbm, w_hbm), (x_ref, w_ref), sems)
    copy_x.wait()
    x = x_ref[...].astype(f32)
    centred = x - jnp.mean(x, axis=-1, keepdims=True)
    var = jnp.mean(centred * centred, axis=-1, keepdims=True)
    normed = (centred * lax.rsqrt(var + 1e-05)).astype(bf16)
    for h in range(2):
        n_ref[h] = normed[:, h * SUB : (h + 1) * SUB, :]
    copy_w.wait()
    t_ref[...] = dot(w_ref[...], n_ref[...].reshape(ROWS * RES, EMBED), 0, 1).astype(bf16)
    for s, out in enumerate(outs):
        z = lax.rem(me_ref[2] + s, Z)
        first, odd = shared_head(z), lax.rem(z, 2)
        lanes = pl.ds(pl.multiple_of(odd * TOKENS, TOKENS), TOKENS)
        out[0:FULL, :] = t_ref[pl.ds(chunk_rows(z)[0], FULL), :]
        for d in range(2):
            rows = pl.ds(pl.multiple_of(first + d * HALF, HALF), HALF)
            out[FULL:CHUNK, d * TOKENS : (d + 1) * TOKENS] = t_ref[rows, lanes]


def key_chunks(me, x, w):
    n, *k = pl.pallas_call(
        key_kernel,
        out_shape=(jax.ShapeDtypeStruct((2, ROWS, SUB, EMBED), bf16),)
        + (jax.ShapeDtypeStruct((CHUNK, ROWS * RES), bf16),) * Z,
        in_specs=[SMEM, ANY, ANY],
        out_specs=(VMEM,) * (1 + Z),
        scratch_shapes=[
            pltpu.VMEM((ROWS, RES, EMBED), bf16),
            pltpu.VMEM((EMBED, EMBED), bf16),
            pltpu.VMEM((EMBED, ROWS * RES), bf16),
            pltpu.SemaphoreType.DMA((2,)),
        ],
        compiler_params=PARAMS,
    )(me, *in_hbm(x, w))
    return n, k


def query_kernel(n_ref, w_ref, q_ref):
    for c in range(2):
        t = dot(w_ref[...], n_ref[c].reshape(TOKENS, EMBED), 0, 1).astype(bf16)
        for z in range(Z):
            a, b = chunk_pieces(z)[0][0], shared_head(z)
            q_ref[2 * z + c, 0:FULL, :] = t[a : a + FULL]
            q_ref[2 * z + c, FULL:, :] = t[b : b + FULL]


def query_chunks(n, w):
    return pl.pallas_call(
        query_kernel,
        out_shape=jax.ShapeDtypeStruct((2 * Z, 2 * FULL, TOKENS), bf16),
        in_specs=[VMEM] * 2,
        out_specs=VMEM,
        compiler_params=PARAMS,
        cost_estimate=PROJECTION,
    )(n, w)


def value_kernel(me_ref, n_ref, w_ref, *rest):
    outs, t_ref = rest[:Z], rest[Z]
    t_ref[...] = dot(w_ref[...], n_ref[...].reshape(ROWS * RES, EMBED), 0, 1).astype(bf16)
    for s, out in enumerate(outs):
        full, half = chunk_rows(lax.rem(me_ref[2] + s, Z))
        out[0:FULL, :] = t_ref[pl.ds(full, FULL), :]
        out[FULL:CHUNK, :] = t_ref[pl.ds(half, HALF), :]


def value_chunks(me, n, w):
    return pl.pallas_call(
        value_kernel,
        out_shape=(jax.ShapeDtypeStruct((CHUNK, ROWS * RES), bf16),) * Z,
        in_specs=[SMEM, VMEM, VMEM],
        out_specs=(VMEM,) * Z,
        scratch_shapes=[pltpu.VMEM((EMBED, ROWS * RES), bf16)],
        compiler_params=PARAMS,
        cost_estimate=PROJECTION,
    )(me, n, w)


def lay_keys(me, own, other, kf, kh):
    where = [lax.rem(me - z + Z, Z) for z in range(Z)]
    for cr, ref in enumerate((own, other)):
        for r in range(ROWS):
            n = (cr * ROWS + r) * FULL
            whole = [ref[z, 0:FULL, h * TOKENS + r * SUB : h * TOKENS + (r + 1) * SUB] for z in where for h in range(2)]
            kf[n : n + FULL, :] = jnp.concatenate(whole, axis=1)
            for d in range(2):
                first = d * TOKENS + r * SUB
                shared = [ref[z, FULL:CHUNK, first : first + SUB] for z in where]
                kh[n + d * HALF : n + (d + 1) * HALF, :] = jnp.concatenate(shared, axis=1)


def keys_kernel(me_ref, own, other, kf, kh):
    lay_keys(me_ref[2], own, other, kf, kh)


def keys_laid(me, own, other):
    return pl.pallas_call(
        keys_kernel,
        out_shape=tuple(jax.ShapeDtypeStruct(s, bf16) for s in KEY_SHAPES),
        in_specs=[SMEM, VMEM, VMEM],
        out_specs=(VMEM,) * 2,
        compiler_params=PARAMS,
        cost_estimate=LAYOUT,
    )(me, own, other)


def score_kernel(me_ref, q_hbm, kf_hbm, kh_hbm, own_hbm, other_hbm, out, qf, qh, kf1, kh1, *rest):
    own, other, q_ref, kf0, kh0, sems = rest
    copies = fetches((own_hbm, other_hbm, q_hbm, kf_hbm, kh_hbm), rest[:5], sems)
    for copy in copies[:2]:
        copy.wait()
    lay_keys(me_ref[2], own, other, kf1, kh1)
    for copy in copies[2:]:
        copy.wait()
    for cr in range(2):
        c = jnp.bitwise_xor(me_ref[1], cr)
        queries = [q_ref[2 * p + c] for p in range(PEERS)]
        for r in range(ROWS):
            n = (cr * ROWS + r) * FULL
            t = jnp.concatenate([b[:, r * SUB : (r + 1) * SUB] for b in queries], axis=1)
            qf[n : n + FULL, :] = t[:FULL]
            qh[n : n + FULL, :] = t[FULL:]
    first = 0
    for a, b in ((qf, kf0), (qf, kf1), (qh, kh0), (qh, kh1)):
        t = dot(a[...], b[...], 0, 0)
        for p in range(PEERS):
            out[p, :, first : first + t.shape[1]] = t[p * SUB : (p + 1) * SUB]
        first += t.shape[1]


def score(me, q, laid, own, other):
    rows = 2 * ROWS * FULL
    return pl.pallas_call(
        score_kernel,
        out_shape=jax.ShapeDtypeStruct((PEERS, SUB, LOGITS), f32),
        in_specs=[SMEM] + [ANY] * 5,
        out_specs=VMEM,
        scratch_shapes=[pltpu.VMEM((rows, QUERIES), bf16)] * 2
        + [pltpu.VMEM(s, bf16) for s in KEY_SHAPES]
        + [pltpu.VMEM(a.shape, bf16) for a in (own, other, q, *laid)]
        + [pltpu.SemaphoreType.DMA((5,))],
        compiler_params=PARAMS,
    )(me, *in_hbm(q), *laid, *in_hbm(own), other)


def total_kernel(parts, full, half):
    t = parts[0]
    for p in range(1, PEERS):
        t = t + parts[p]
    full[...] = t[:, :KEYS]
    half[...] = t[:, KEYS:]


def total(parts):
    return pl.pallas_call(
        total_kernel,
        out_shape=tuple(jax.ShapeDtypeStruct((SUB, n), f32) for n in (KEYS, KEYS // 2)),
        in_specs=[VMEM],
        out_specs=(VMEM,) * 2,
        compiler_params=PARAMS,
    )(parts)


def softmax_kernel(factor, full, half, other, out):
    for i, logits in enumerate((full[...], jnp.concatenate([half[...], other[...]], axis=1))):
        logits = logits * factor
        powered = jnp.exp(logits - jnp.max(logits, axis=-1, keepdims=True))
        probs = (powered / jnp.sum(powered, axis=-1, keepdims=True)).astype(bf16)
        for p in range(PEERS):
            out[p, i] = probs


def softmax(factor, full, half, other):
    return pl.pallas_call(
        functools.partial(softmax_kernel, factor),
        out_shape=jax.ShapeDtypeStruct((PEERS, 2, SUB, KEYS), bf16),
        in_specs=[VMEM] * 3,
        out_specs=VMEM,
        compiler_params=PARAMS,
    )(full, half, other)


def values_kernel(me_ref, *refs):
    (vf, vh), (v00, v01, v10, v11), sems = refs[4:6], refs[6:10], refs[10]
    for copy in fetches(refs[:4], refs[6:10], sems):
        copy.wait()
    z = me_ref[2]
    odd = lax.rem(z, 2)
    where = [lax.rem(z - source + Z, Z) for source in range(Z)]
    for cr, refs in enumerate(((v00, v01), (v10, v11))):
        halves = [
            ref[i, FULL:CHUNK, pl.ds(pl.multiple_of(h * TOKENS, TOKENS), TOKENS)]
            for h in (odd, 1 - odd)
            for ref in refs
            for i in where
        ]
        whole = [ref[i, 0:FULL, h * TOKENS : (h + 1) * TOKENS] for ref in refs for i in where for h in range(2)]
        for r in range(ROWS):
            n = cr * ROWS + r
            lanes = slice(r * SUB, (r + 1) * SUB)
            vf[n * FULL : (n + 1) * FULL, :] = jnp.concatenate([b[:, lanes] for b in whole], axis=1)
            vh[n * HALF : (n + 1) * HALF, :] = jnp.concatenate([b[:, lanes] for b in halves], axis=1)


def values_laid(me, vs):
    return pl.pallas_call(
        values_kernel,
        out_shape=(
            jax.ShapeDtypeStruct((2 * ROWS * FULL, KEYS), bf16),
            pltpu.HBM((2 * ROWS * HALF, KEYS), bf16),
        ),
        in_specs=[SMEM] + [ANY] * 4,
        out_specs=(VMEM,) * 2,
        scratch_shapes=[pltpu.VMEM(v.shape, bf16) for v in vs] + [pltpu.SemaphoreType.DMA((4,))],
        compiler_params=PARAMS,
        cost_estimate=LAYOUT,
    )(me, *in_hbm(*vs[:2]), *vs[2:])


def mix_kernel(me_ref, vf, vh_hbm, p_ref, o_ref, vh, sems):
    core = me_ref[1]
    copy = fetches((vh_hbm,), (vh,), sems)[0]
    for i, (v, first, n) in enumerate(((vf, 0, FULL), (vh, FULL, HALF))):
        if i == 1:
            copy.wait()
        probs = p_ref[:, i].reshape(QUERIES, KEYS)
        for cr in range(2):
            c = jnp.bitwise_xor(core, cr)
            mixed = dot(v[cr * ROWS * n : (cr + 1) * ROWS * n, :], probs, 1, 1).astype(bf16)
            for s in range(PEERS):
                o_ref[2 * s + c, first : first + n, :] = jnp.concatenate(
                    [mixed[r * n : (r + 1) * n, s * SUB : (s + 1) * SUB] for r in range(ROWS)], axis=1
                )


def mix(me, laid, probs):
    whole, shared = laid
    return pl.pallas_call(
        mix_kernel,
        out_shape=jax.ShapeDtypeStruct((2 * Z, CHUNK, ROWS * SUB), bf16),
        in_specs=[SMEM, VMEM, ANY, VMEM],
        out_specs=VMEM,
        scratch_shapes=[pltpu.VMEM(shared.shape, bf16), pltpu.SemaphoreType.DMA((1,))],
        compiler_params=PARAMS,
    )(me, whole, *in_hbm(shared), probs)


def final_kernel(m_ref, w_ref, o_ref, t_ref):
    for c in range(2):
        for z in range(Z):
            (a, na), (b, nb) = chunk_pieces(z)
            t_ref[a : a + na, :] = m_ref[2 * z + c, 0:FULL, :]
            t_ref[b : b + nb, :] = m_ref[2 * z + c, FULL:CHUNK, :]
        attended = dot(t_ref[...], w_ref[...], 0, 0).astype(bf16)
        o_ref[:, c * SUB : (c + 1) * SUB, :] = attended.reshape(ROWS, SUB, EMBED)


def final(m, w):
    return pl.pallas_call(
        final_kernel,
        out_shape=jax.ShapeDtypeStruct((ROWS, RES, EMBED), bf16),
        in_specs=[VMEM] * 2,
        out_specs=VMEM,
        scratch_shapes=[pltpu.VMEM((EMBED, ROWS * SUB), bf16)],
        compiler_params=PARAMS,
    )(m, w)


def flip(x, axes, n, s):
    return lax.ppermute(x, axes, [(i, i ^ s) for i in range(n)])


def gather4(own):
    far = flip(own, "xl", 2, 1)
    return own, far, flip(own, "c", 2, 1), flip(far, "c", 2, 1)


def shift(x, s):
    return lax.ppermute(x, "z", [(i, (i + s) % Z) for i in range(Z)])


def local(x, wq, wk, wv, wf):
    me = jnp.stack([lax.axis_index(("y", "xh")), lax.axis_index("c"), lax.axis_index("z")])
    me = me.astype(jnp.int32)
    n, k = key_chunks(me, x, wk)
    for s in (1, 7, 2, 6, 3, 5, 4):
        k[s] = shift(k[s], s)
    early = (1, 7, 2, 6, 3)
    q, *got = lax.optimization_barrier((query_chunks(n, wq), *(k[s] for s in early)))
    for s, a in zip(early, got):
        k[s] = a
    q = lax.all_to_all(q, ("z", "c"), 0, 0, tiled=True)
    v = list(value_chunks(me, n, wv))
    k = jnp.stack(k)
    near, shared = keys_laid(me, k, flip(k, "c", 2, 1))
    k_far, v[7], shared = lax.optimization_barrier((flip(k, "xl", 2, 1), v[7], shared))
    for s in (4,):
        v[s] = shift(v[s], s)
    scores = score(me, q, (near, shared), k_far, flip(k_far, "c", 2, 1))
    *v, scores = lax.optimization_barrier((*v, scores))
    parts = lax.all_to_all(scores, ("y", "xh"), 0, 0, tiled=True)
    for s in (3, 5, 2, 6, 1, 7):
        v[s] = shift(v[s], s)
    full, half = total(parts)
    rows = ROWS * 2 * PEERS
    probs = softmax(1.0 / math.sqrt(DH * rows), full, half, flip(half, "z", Z, 1))
    probs = lax.all_to_all(probs, ("y", "xh"), 0, 0, tiled=True)
    laid = values_laid(me, gather4(jnp.stack(v)))
    mixed = lax.all_to_all(mix(me, laid, probs), ("z", "c"), 0, 0, tiled=True)
    return final(mixed, wf)


def solution(mesh):
    fine = Mesh(mesh.devices.reshape(4, 2, 2, 8, 2), ("y", "xh", "c", "z", "xl"))
    spec = P(("y", "xh", "c"), ("z", "xl"), None)
    return jax.shard_map(
        local,
        mesh=fine,
        in_specs=(spec, P(), P(), P(), P()),
        out_specs=spec,
        check_vma=False,
    )
```

```python
import functools
import math

import jax
import jax.numpy as jnp
from jax import lax
from jax.experimental import pallas as pl
from jax.experimental.pallas import tpu as pltpu
from jax.sharding import Mesh, PartitionSpec as P

H = 12
DH = 64
EMBED = 768
ROWS = 8
RES = 64
Z = 8
CHUNK = EMBED // Z
FULL = DH
HALF = CHUNK - DH
PEERS = 8
SUB = RES // 2
TOKENS = ROWS * SUB
QUERIES = Z * SUB
KEYS = 2 * Z * RES
LOGITS = KEYS + KEYS // 2

f32 = jnp.float32
bf16 = jnp.bfloat16
PARAMS = pltpu.CompilerParams(vmem_limit_bytes=16 * 1024 * 1024)
PROJECTION = pl.CostEstimate(
    flops=2 * ROWS * RES * EMBED * EMBED, bytes_accessed=2 * EMBED * (EMBED + 2 * ROWS * RES), transcendentals=0
)
LAYOUT = pl.CostEstimate(flops=0, bytes_accessed=16 * ROWS * RES * EMBED, transcendentals=0)
KEY_SHAPES = ((2 * ROWS * FULL, KEYS // 2), (2 * ROWS * FULL, KEYS // 4))
WIDE = pltpu.CompilerParams(vmem_limit_bytes=16 * 1024 * 1024)
VMEM = pl.BlockSpec(memory_space=pltpu.VMEM)
SMEM = pl.BlockSpec(memory_space=pltpu.SMEM)
ANY = pl.BlockSpec(memory_space=pl.ANY)
HBM = pl.BlockSpec(memory_space=pltpu.HBM)


def chunk_pieces(z):
    base = z * CHUNK
    if z % 2 == 0:
        return (base, FULL), (base + FULL, HALF)
    return (base + HALF, FULL), (base, HALF)


def dot(a, b, ca, cb):
    return lax.dot_general(a, b, (((ca,), (cb,)), ((), ())), preferred_element_type=f32)


def shared_head(z):
    return z // 2 * (2 * CHUNK) + FULL


def chunk_rows(z):
    odd = lax.rem(z, 2)
    base = z * CHUNK
    return pl.multiple_of(base + odd * HALF, HALF), pl.multiple_of(base + (1 - odd) * FULL, HALF)


def fetches(sources, buffers, sems):
    copies = [pltpu.make_async_copy(a, b, sems.at[i]) for i, (a, b) in enumerate(zip(sources, buffers))]
    for copy in copies:
        copy.start()
    return copies


def in_hbm(*arrays):
    return [pltpu.with_memory_space_constraint(a, pltpu.HBM) for a in arrays]


def key_kernel(me_ref, x_hbm, w_hbm, n_ref, *rest):
    outs, (x_ref, w_ref, t_ref, sems) = rest[:Z], rest[Z:]
    copy_x, copy_w = fetches((x_hbm, w_hbm), (x_ref, w_ref), sems)
    copy_x.wait()
    x = x_ref[...].astype(f32)
    centred = x - jnp.mean(x, axis=-1, keepdims=True)
    var = jnp.mean(centred * centred, axis=-1, keepdims=True)
    normed = (centred * lax.rsqrt(var + 1e-05)).astype(bf16)
    for h in range(2):
        n_ref[h] = normed[:, h * SUB : (h + 1) * SUB, :]
    copy_w.wait()
    t_ref[...] = dot(w_ref[...], n_ref[...].reshape(ROWS * RES, EMBED), 0, 1).astype(bf16)
    for s, out in enumerate(outs):
        z = lax.rem(me_ref[2] + s, Z)
        first, odd = shared_head(z), lax.rem(z, 2)
        lanes = pl.ds(pl.multiple_of(odd * TOKENS, TOKENS), TOKENS)
        out[0:FULL, :] = t_ref[pl.ds(chunk_rows(z)[0], FULL), :]
        for d in range(2):
            rows = pl.ds(pl.multiple_of(first + d * HALF, HALF), HALF)
            out[FULL:CHUNK, d * TOKENS : (d + 1) * TOKENS] = t_ref[rows, lanes]


def key_chunks(me, x, w):
    n, *k = pl.pallas_call(
        key_kernel,
        out_shape=(jax.ShapeDtypeStruct((2, ROWS, SUB, EMBED), bf16),)
        + (jax.ShapeDtypeStruct((CHUNK, ROWS * RES), bf16),) * Z,
        in_specs=[SMEM, ANY, ANY],
        out_specs=(VMEM,) * (1 + Z),
        scratch_shapes=[
            pltpu.VMEM((ROWS, RES, EMBED), bf16),
            pltpu.VMEM((EMBED, EMBED), bf16),
            pltpu.VMEM((EMBED, ROWS * RES), bf16),
            pltpu.SemaphoreType.DMA((2,)),
        ],
        compiler_params=PARAMS,
    )(me, *in_hbm(x, w))
    return n, k


def query_kernel(n_ref, w_ref, q_ref):
    for c in range(2):
        t = dot(w_ref[...], n_ref[c].reshape(TOKENS, EMBED), 0, 1).astype(bf16)
        for z in range(Z):
            a, b = chunk_pieces(z)[0][0], shared_head(z)
            q_ref[2 * z + c, 0:FULL, :] = t[a : a + FULL]
            q_ref[2 * z + c, FULL:, :] = t[b : b + FULL]


def query_chunks(n, w):
    return pl.pallas_call(
        query_kernel,
        out_shape=jax.ShapeDtypeStruct((2 * Z, 2 * FULL, TOKENS), bf16),
        in_specs=[VMEM] * 2,
        out_specs=VMEM,
        compiler_params=PARAMS,
        cost_estimate=PROJECTION,
    )(n, w)


def value_kernel(me_ref, n_ref, w_ref, *rest):
    outs, t_ref = rest[:Z], rest[Z]
    t_ref[...] = dot(w_ref[...], n_ref[...].reshape(ROWS * RES, EMBED), 0, 1).astype(bf16)
    for s, out in enumerate(outs):
        full, half = chunk_rows(lax.rem(me_ref[2] + s, Z))
        out[0:FULL, :] = t_ref[pl.ds(full, FULL), :]
        out[FULL:CHUNK, :] = t_ref[pl.ds(half, HALF), :]


def value_chunks(me, n, w):
    return pl.pallas_call(
        value_kernel,
        out_shape=(jax.ShapeDtypeStruct((CHUNK, ROWS * RES), bf16),) * Z,
        in_specs=[SMEM, VMEM, VMEM],
        out_specs=(VMEM,) * Z,
        scratch_shapes=[pltpu.VMEM((EMBED, ROWS * RES), bf16)],
        compiler_params=PARAMS,
        cost_estimate=PROJECTION,
    )(me, n, w)


def lay_keys(me, own, other, kf, kh):
    where = [lax.rem(me - z + Z, Z) for z in range(Z)]
    for cr, ref in enumerate((own, other)):
        for r in range(ROWS):
            n = (cr * ROWS + r) * FULL
            whole = [ref[z, 0:FULL, h * TOKENS + r * SUB : h * TOKENS + (r + 1) * SUB] for z in where for h in range(2)]
            kf[n : n + FULL, :] = jnp.concatenate(whole, axis=1)
            for d in range(2):
                first = d * TOKENS + r * SUB
                shared = [ref[z, FULL:CHUNK, first : first + SUB] for z in where]
                kh[n + d * HALF : n + (d + 1) * HALF, :] = jnp.concatenate(shared, axis=1)


def keys_kernel(me_ref, own, other, kf, kh):
    lay_keys(me_ref[2], own, other, kf, kh)


def keys_laid(me, own, other):
    return pl.pallas_call(
        keys_kernel,
        out_shape=tuple(jax.ShapeDtypeStruct(s, bf16) for s in KEY_SHAPES),
        in_specs=[SMEM, VMEM, VMEM],
        out_specs=(VMEM,) * 2,
        compiler_params=PARAMS,
        cost_estimate=LAYOUT,
    )(me, own, other)


def score_kernel(me_ref, q_hbm, kf_hbm, kh_hbm, own_hbm, other_hbm, out, qf, qh, kf1, kh1, *rest):
    own, other, q_ref, kf0, kh0, sems = rest
    copies = fetches((own_hbm, other_hbm, q_hbm, kf_hbm, kh_hbm), rest[:5], sems)
    for copy in copies[:2]:
        copy.wait()
    lay_keys(me_ref[2], own, other, kf1, kh1)
    for copy in copies[2:]:
        copy.wait()
    for cr in range(2):
        c = jnp.bitwise_xor(me_ref[1], cr)
        queries = [q_ref[2 * p + c] for p in range(PEERS)]
        for r in range(ROWS):
            n = (cr * ROWS + r) * FULL
            t = jnp.concatenate([b[:, r * SUB : (r + 1) * SUB] for b in queries], axis=1)
            qf[n : n + FULL, :] = t[:FULL]
            qh[n : n + FULL, :] = t[FULL:]
    first = 0
    for a, b in ((qf, kf0), (qf, kf1), (qh, kh0), (qh, kh1)):
        t = dot(a[...], b[...], 0, 0)
        for p in range(PEERS):
            out[p, :, first : first + t.shape[1]] = t[p * SUB : (p + 1) * SUB]
        first += t.shape[1]


def score(me, q, laid, own, other):
    rows = 2 * ROWS * FULL
    return pl.pallas_call(
        score_kernel,
        out_shape=jax.ShapeDtypeStruct((PEERS, SUB, LOGITS), f32),
        in_specs=[SMEM] + [ANY] * 5,
        out_specs=VMEM,
        scratch_shapes=[pltpu.VMEM((rows, QUERIES), bf16)] * 2
        + [pltpu.VMEM(s, bf16) for s in KEY_SHAPES]
        + [pltpu.VMEM(a.shape, bf16) for a in (own, other, q, *laid)]
        + [pltpu.SemaphoreType.DMA((5,))],
        compiler_params=PARAMS,
    )(me, *in_hbm(q), *laid, *in_hbm(own), other)


def total_kernel(parts, full, half):
    t = parts[0]
    for p in range(1, PEERS):
        t = t + parts[p]
    full[...] = t[:, :KEYS]
    half[...] = t[:, KEYS:]


def total(parts):
    return pl.pallas_call(
        total_kernel,
        out_shape=tuple(jax.ShapeDtypeStruct((SUB, n), f32) for n in (KEYS, KEYS // 2)),
        in_specs=[VMEM],
        out_specs=(VMEM,) * 2,
        compiler_params=PARAMS,
    )(parts)


def softmax_kernel(factor, full, half, other, out):
    for i, logits in enumerate((full[...], jnp.concatenate([half[...], other[...]], axis=1))):
        logits = logits * factor
        powered = jnp.exp(logits - jnp.max(logits, axis=-1, keepdims=True))
        probs = (powered / jnp.sum(powered, axis=-1, keepdims=True)).astype(bf16)
        for p in range(PEERS):
            out[p, i] = probs


def softmax(factor, full, half, other):
    return pl.pallas_call(
        functools.partial(softmax_kernel, factor),
        out_shape=jax.ShapeDtypeStruct((PEERS, 2, SUB, KEYS), bf16),
        in_specs=[VMEM] * 3,
        out_specs=VMEM,
        compiler_params=PARAMS,
    )(full, half, other)


def values_kernel(me_ref, *refs):
    (vf, vh), (v00, v01, v10, v11), sems = refs[4:6], refs[6:10], refs[10]
    for copy in fetches(refs[:4], refs[6:10], sems):
        copy.wait()
    z = me_ref[2]
    odd = lax.rem(z, 2)
    where = [lax.rem(z - source + Z, Z) for source in range(Z)]
    for cr, refs in enumerate(((v00, v01), (v10, v11))):
        halves = [
            ref[i, FULL:CHUNK, pl.ds(pl.multiple_of(h * TOKENS, TOKENS), TOKENS)]
            for h in (odd, 1 - odd)
            for ref in refs
            for i in where
        ]
        whole = [ref[i, 0:FULL, h * TOKENS : (h + 1) * TOKENS] for ref in refs for i in where for h in range(2)]
        for r in range(ROWS):
            n = cr * ROWS + r
            lanes = slice(r * SUB, (r + 1) * SUB)
            vf[n * FULL : (n + 1) * FULL, :] = jnp.concatenate([b[:, lanes] for b in whole], axis=1)
            vh[n * HALF : (n + 1) * HALF, :] = jnp.concatenate([b[:, lanes] for b in halves], axis=1)


def values_laid(me, vs):
    return pl.pallas_call(
        values_kernel,
        out_shape=(
            jax.ShapeDtypeStruct((2 * ROWS * FULL, KEYS), bf16),
            pltpu.HBM((2 * ROWS * HALF, KEYS), bf16),
        ),
        in_specs=[SMEM] + [ANY] * 4,
        out_specs=(VMEM,) * 2,
        scratch_shapes=[pltpu.VMEM(v.shape, bf16) for v in vs] + [pltpu.SemaphoreType.DMA((4,))],
        compiler_params=PARAMS,
        cost_estimate=LAYOUT,
    )(me, *in_hbm(*vs[:2]), *vs[2:])


def mix_kernel(me_ref, vf, vh_hbm, p_ref, o_ref, vh, sems):
    core = me_ref[1]
    copy = fetches((vh_hbm,), (vh,), sems)[0]
    for i, (v, first, n) in enumerate(((vf, 0, FULL), (vh, FULL, HALF))):
        if i == 1:
            copy.wait()
        probs = p_ref[:, i].reshape(QUERIES, KEYS)
        for cr in range(2):
            c = jnp.bitwise_xor(core, cr)
            mixed = dot(v[cr * ROWS * n : (cr + 1) * ROWS * n, :], probs, 1, 1).astype(bf16)
            for s in range(PEERS):
                o_ref[2 * s + c, first : first + n, :] = jnp.concatenate(
                    [mixed[r * n : (r + 1) * n, s * SUB : (s + 1) * SUB] for r in range(ROWS)], axis=1
                )


def mix(me, laid, probs):
    whole, shared = laid
    return pl.pallas_call(
        mix_kernel,
        out_shape=jax.ShapeDtypeStruct((2 * Z, CHUNK, ROWS * SUB), bf16),
        in_specs=[SMEM, VMEM, ANY, VMEM],
        out_specs=VMEM,
        scratch_shapes=[pltpu.VMEM(shared.shape, bf16), pltpu.SemaphoreType.DMA((1,))],
        compiler_params=PARAMS,
    )(me, whole, *in_hbm(shared), probs)


def final_kernel(m_ref, w_ref, o_ref, t_ref):
    for c in range(2):
        for z in range(Z):
            (a, na), (b, nb) = chunk_pieces(z)
            t_ref[a : a + na, :] = m_ref[2 * z + c, 0:FULL, :]
            t_ref[b : b + nb, :] = m_ref[2 * z + c, FULL:CHUNK, :]
        attended = dot(t_ref[...], w_ref[...], 0, 0).astype(bf16)
        o_ref[:, c * SUB : (c + 1) * SUB, :] = attended.reshape(ROWS, SUB, EMBED)


def final(m, w):
    return pl.pallas_call(
        final_kernel,
        out_shape=jax.ShapeDtypeStruct((ROWS, RES, EMBED), bf16),
        in_specs=[VMEM] * 2,
        out_specs=VMEM,
        scratch_shapes=[pltpu.VMEM((EMBED, ROWS * SUB), bf16)],
        compiler_params=PARAMS,
    )(m, w)


def flip(x, axes, n, s):
    return lax.ppermute(x, axes, [(i, i ^ s) for i in range(n)])


def gather4(own):
    far = flip(own, "xl", 2, 1)
    return own, far, flip(own, "c", 2, 1), flip(far, "c", 2, 1)


def shift(x, s):
    return lax.ppermute(x, "z", [(i, (i + s) % Z) for i in range(Z)])


def local(x, wq, wk, wv, wf):
    me = jnp.stack([lax.axis_index(("y", "xh")), lax.axis_index("c"), lax.axis_index("z")])
    me = me.astype(jnp.int32)
    n, k = key_chunks(me, x, wk)
    for s in (1, 7, 2, 6, 3, 5, 4):
        k[s] = shift(k[s], s)
    early = (1, 7, 2, 6, 3)
    q, *got = lax.optimization_barrier((query_chunks(n, wq), *(k[s] for s in early)))
    for s, a in zip(early, got):
        k[s] = a
    q = lax.all_to_all(q, ("z", "c"), 0, 0, tiled=True)
    v = list(value_chunks(me, n, wv))
    k = jnp.stack(k)
    near, shared = keys_laid(me, k, flip(k, "c", 2, 1))
    k_far, v[4], shared = lax.optimization_barrier((flip(k, "xl", 2, 1), v[4], shared))
    for s in (2, 6, 1):
        v[s] = shift(v[s], s)
    scores = score(me, q, (near, shared), k_far, flip(k_far, "c", 2, 1))
    *v, scores = lax.optimization_barrier((*v, scores))
    parts = lax.all_to_all(scores, ("y", "xh"), 0, 0, tiled=True)
    for s in (4, 3, 5, 7):
        v[s] = shift(v[s], s)
    full, half = total(parts)
    rows = ROWS * 2 * PEERS
    probs = softmax(1.0 / math.sqrt(DH * rows), full, half, flip(half, "z", Z, 1))
    probs = lax.all_to_all(probs, ("y", "xh"), 0, 0, tiled=True)
    laid = values_laid(me, gather4(jnp.stack(v)))
    mixed = lax.all_to_all(mix(me, laid, probs), ("z", "c"), 0, 0, tiled=True)
    return final(mixed, wf)


def solution(mesh):
    fine = Mesh(mesh.devices.reshape(4, 2, 2, 8, 2), ("y", "xh", "c", "z", "xl"))
    spec = P(("y", "xh", "c"), ("z", "xl"), None)
    return jax.shard_map(
        local,
        mesh=fine,
        in_specs=(spec, P(), P(), P(), P()),
        out_specs=spec,
        check_vma=False,
    )
```
